128 devices in a mesh: sec: 32 (over z, x, y_hi), tp: 4 (over y_lo, core).
Axes of the slice: x: 4, y: 4 (y_hi: 2, y_lo: 2; y = y_hi * 2 + y_lo), z: 4, core: 2. Of those that a mesh axis runs over, the one named last changes fastest.
Arguments:
- patches: bfloat16 [32768, 1280], P('sec'), may hold values from -48 to 48
- image_ids: int32 [32, 256], P('sec'), may hold values from 0 to 3, never falling along the last dimension, each value on 1 to 128 neighbouring positions
- qkv_weight: bfloat16 [3, 1280, 1280], P(None, None, 'tp'), may hold values from -0.15625 to 0.15625
- out_weight: bfloat16 [1280, 1280], P('tp'), may hold values from -0.15625 to 0.15625
- merge_gain: float32 [1280], replicated, may hold values from 0.5 to 1.5
- merge_weight: bfloat16 [5120, 8192], P('sec', 'tp'), may hold values from -0.078125 to 0.078125
- text_rows: bfloat16 [16384, 8192], P('sec', 'tp'), may hold values from -21 to 21
- image_refs: int32 [16384], P('sec'), may hold values from -1 to 8191, as said below
- llm_gain: float32 [8192], P('tp'), may hold values from 0.5 to 1.5
Outputs:
- prompt_states: bfloat16 [16384, 8192], P('sec', 'tp')
The draws below stay inside these ranges and needn't reach their ends.
Inputs may be any that keep to these rules, and one draw needn't show every extreme that they name: `image_ids`: each image's rows form one run within its device's row of ids. `image_refs`: -1 marks a text row; any other value names one of the 8192 image rows, those of device s starting at s * 256. Each image row is named at most once. The 512 prompt rows of one device name at most 16 image rows of one device, and exactly 16 for some pairs of devices.
All inputs are finite; a program needn't handle non-finite values.
Results may differ from the reference program's by a relative error of at most 0.012.
Values may be sent and summed in bfloat16 or wider, within the bound.
No kernel may reach another device: no remote copies, remote signals or barrier semaphores. Data moves between devices by JAX's collectives and lax.ppermute only.
A program may use at most 128 MiB of HBM per device.

```python
import math
import jax
import jax.numpy as jnp
import numpy as np
from jax import lax

D_VIT = 1280
HEADS_VIT = 16
HEAD_DIM = 80
D_LLM = 8192
MERGE = 4
IMG_DEV = 4
P_DEV = 1024
M_DEV = 256
S_DEV = 512
FAN = 16
CAP = 16
N_SEC = 32


def draw_patches(key, part):
    key = jax.random.fold_in(key, 3)
    first_key = jax.random.fold_in(key, 0)
    total_rows = N_SEC * P_DEV
    values = jnp.clip(jax.random.normal(first_key, (total_rows, D_VIT), jnp.float32), -6.0, 6.0)
    return values.astype(jnp.bfloat16)


def draw_text_rows(key, part):
    key = jax.random.fold_in(key, 5)
    first_key, second_key = jax.random.split(key, 2)
    total_rows = N_SEC * S_DEV
    column_scale = jnp.exp(jax.random.uniform(first_key, (D_LLM,), jnp.float32, math.log(0.3), math.log(3.0)))
    values = jnp.clip(jax.random.normal(second_key, (total_rows, D_LLM), jnp.float32), -6.0, 6.0) * column_scale[None, :]
    return values.astype(jnp.bfloat16)


def permute_slots(slot_key):
    return jax.random.permutation(slot_key, S_DEV)


def place_values(ordering, entries):
    return jnp.zeros((S_DEV,), jnp.int32).at[ordering].set(entries)


def draw_image_refs(key, part):
    key = jax.random.fold_in(key, 7)
    first_key, second_key, third_key = jax.random.split(key, 3)
    favour = jax.random.permutation(first_key, N_SEC)
    jitter = jax.random.randint(second_key, (N_SEC, N_SEC), 0, 2 * N_SEC)
    ranking = (jitter + 2 * favour[None, :]) * N_SEC + jnp.arange(N_SEC)[None, :]
    chosen = lax.top_k(ranking, FAN)[1]
    target_hits = chosen[:, :, None] == jnp.arange(N_SEC)[None, None, :]
    block_index = jnp.sum(target_hits.astype(jnp.int32) * jnp.arange(FAN)[None, :, None], axis=1)
    incoming = jnp.any(target_hits, axis=1).astype(jnp.int32).T
    before = jnp.cumsum(incoming, axis=1) - incoming
    slot_ids = jnp.arange(S_DEV)
    pair_index = slot_ids // CAP
    within = slot_ids % CAP
    matches = (incoming[:, None, :] == 1) & (before[:, None, :] == pair_index[None, :, None])
    first_rows = jnp.arange(N_SEC)[None, :] * M_DEV + block_index.T * CAP
    entries = jnp.sum(matches.astype(jnp.int32) * first_rows[:, None, :], axis=2) + within[None, :]
    entries = jnp.where(jnp.any(matches, axis=2), entries, -1).astype(jnp.int32)
    orderings = jax.vmap(permute_slots)(jax.random.split(third_key, N_SEC))
    placed = jax.vmap(place_values)(orderings, entries)
    return placed.reshape(N_SEC * S_DEV).astype(jnp.int32)


def shard_levels(stream_key, shape, shards, least, high):
    gain = 1.0
    for dim, shards_of in shards:
        steps = jax.random.uniform(jax.random.fold_in(jax.random.fold_in(stream_key, 6), dim), (shards_of,), jnp.float32, least / len(shards), high / len(shards))
        gain = gain * jnp.repeat(jnp.exp(steps), shape[dim] // shards_of).reshape((-1,) + (1,) * (len(shape) - 1 - dim))
    return gain


def length_profile(count, total, most, slope):
    portions = [(1 << 20) // math.isqrt(grade ** slope) + 1 for grade in range(2, count + 1)]
    surplus, given = total - most - (count - 1), [1] * (count - 1)
    while surplus > 0:
        free = [i for i in range(count - 1) if given[i] < most]
        pool, budget = sum([portions[i] for i in free]), surplus
        for i in free:
            more = min(most - given[i], max(1, budget * portions[i] // pool), surplus)
            given[i] = given[i] + more
            surplus = surplus - more
    return np.array([most] + given)


def ragged_sizes(rng, number_of, total, limit, slope):
    if number_of == 2:
        one = jax.random.randint(rng, (), max(1, total - limit), min(limit, total - 1) + 1)
        return jnp.stack([one, total - one])
    sizes = jnp.asarray(length_profile(number_of, total, limit, slope), jnp.int32)
    pairs = (number_of - 1) // 2
    donor, sink = sizes[1:1 + 2 * pairs:2], sizes[2:2 + 2 * pairs:2]
    margin = jnp.minimum(donor - 1, limit - sink)
    passed = jax.random.randint(jax.random.fold_in(rng, 1), (pairs,), 0, 1 << 20) % (margin + 1)
    sizes = sizes.at[1:1 + 2 * pairs:2].set(donor - passed).at[2:2 + 2 * pairs:2].set(sink + passed)
    return sizes[jax.random.permutation(jax.random.fold_in(rng, 2), number_of)]


def noise(key, dims, width, most, cuts=(), held_as=jnp.bfloat16):
    factor_of = shard_levels(key, dims, cuts, -0.22, 0.18) if cuts else 1.0
    drawn = jax.random.normal(key, dims, jnp.float32) * width * factor_of
    return jnp.minimum(jnp.maximum(drawn, -most), most).astype(held_as)


def setup_inputs(seed: int = 0) -> dict:
    seeds = jax.random.split(jax.random.key(seed), 10)
    return {
        "patches": draw_patches(jax.random.fold_in(seeds[9], 71), 0),
        "image_ids": jax.vmap(lambda own: jnp.searchsorted(jnp.cumsum(ragged_sizes(own, IMG_DEV, M_DEV, M_DEV // 2, 2)), jnp.arange(M_DEV), side="right"))(jax.random.split(seeds[1], N_SEC)).reshape((N_SEC, M_DEV)).astype(jnp.int32),
        "qkv_weight": noise(seeds[2], (3, D_VIT, D_VIT), D_VIT ** -0.5, 0.15625, ((2, 4),)),
        "out_weight": noise(seeds[3], (D_VIT, D_VIT), D_VIT ** -0.5, 0.15625, ((0, 4),)),
        "merge_gain": jnp.clip(1.0 + 0.1 * jax.random.normal(seeds[4], (D_VIT,), jnp.float32), 0.5, 1.5),
        "merge_weight": noise(seeds[5], (MERGE * D_VIT, D_LLM), (MERGE * D_VIT) ** -0.5, 0.078125, ((0, 32), (1, 4))),
        "text_rows": draw_text_rows(jax.random.fold_in(seeds[9], 71), 0),
        "image_refs": draw_image_refs(jax.random.fold_in(seeds[9], 71), 0),
        "llm_gain": jnp.clip(1.0 + 0.1 * jax.random.normal(seeds[8], (D_LLM,), jnp.float32), 0.5, 1.5),
    }


EPSILON = 1e-06

def encode_device(patch_block, id_block, qkv_weight, out_weight, merge_gain, merge_weight):
    row_count = patch_block.shape[0]
    projected = jnp.einsum('pd,cde->cpe', patch_block.astype(jnp.float32), qkv_weight.astype(jnp.float32)).astype(jnp.bfloat16)
    queries = projected[0].reshape(row_count, HEADS_VIT, HEAD_DIM)
    key_heads = projected[1].reshape(row_count, HEADS_VIT, HEAD_DIM)
    value_heads = projected[2].reshape(row_count, HEADS_VIT, HEAD_DIM)
    patch_ids = jnp.repeat(id_block, MERGE)
    same_image = patch_ids[:, None] == patch_ids[None, :]

    def one_head(head_index):
        query_part = lax.dynamic_index_in_dim(queries, head_index, 1, keepdims=False)
        key_part = lax.dynamic_index_in_dim(key_heads, head_index, 1, keepdims=False)
        value_part = lax.dynamic_index_in_dim(value_heads, head_index, 1, keepdims=False)
        scores = jnp.dot(query_part, key_part.T, preferred_element_type=jnp.float32) * HEAD_DIM ** (-0.5)
        scores = jnp.where(same_image, scores, -1e+30)
        highest = lax.optimization_barrier(jnp.max(scores, axis=1, keepdims=True))
        weights = jnp.exp(scores - highest)
        attention = (weights / lax.optimization_barrier(jnp.sum(weights, axis=1, keepdims=True))).astype(jnp.bfloat16)
        return jnp.dot(attention, value_part, preferred_element_type=jnp.float32).astype(jnp.bfloat16)
    contexts = lax.map(one_head, jnp.arange(HEADS_VIT, dtype=jnp.int32))
    context = jnp.transpose(contexts, (1, 0, 2)).reshape(row_count, HEADS_VIT * HEAD_DIM)
    attended = patch_block.astype(jnp.float32) + jnp.dot(context, out_weight, preferred_element_type=jnp.float32)
    moment = lax.optimization_barrier(jnp.mean(attended * attended, axis=1, keepdims=True))
    normed = (attended * lax.rsqrt(moment + EPSILON) * merge_gain).astype(jnp.bfloat16)
    merged = normed.reshape(row_count // MERGE, MERGE * normed.shape[1])
    return jnp.dot(merged, merge_weight, preferred_element_type=jnp.float32).astype(jnp.bfloat16)

def reference(patches, image_ids, qkv_weight, out_weight, merge_gain, merge_weight, text_rows, image_refs, llm_gain):

    def encode_one(inputs):
        return encode_device(inputs[0], inputs[1], qkv_weight, out_weight, merge_gain, merge_weight)
    images = lax.map(encode_one, (patches.reshape(N_SEC, P_DEV, D_VIT), image_ids))
    images = images.reshape(N_SEC * M_DEV, D_LLM)
    usable = image_refs >= 0
    picked = jnp.take(images, jnp.maximum(image_refs, 0).astype(jnp.int32), axis=0)
    prompt = jnp.where(usable[:, None], picked, text_rows)
    widened = prompt.astype(jnp.float32)
    moment = lax.optimization_barrier(jnp.mean(widened * widened, axis=1, keepdims=True))
    return (widened * lax.rsqrt(moment + EPSILON) * llm_gain).astype(jnp.bfloat16)
```

```python
import jax
import jax.numpy as jnp
from jax import lax
from jax.sharding import Mesh, PartitionSpec as P

HEAD_DIM = 80
MERGE = 4
EPSILON = 1e-06
SEC = ("z", "x", "yh")
TP = ("yl", "c")
BF = jnp.bfloat16
F32 = jnp.float32


def vision_context(patches, image_ids, qkv_weight):
    row_count = patches.shape[0]
    projected = jnp.einsum(
        "pd,cde->cpe", patches, qkv_weight, preferred_element_type=F32
    ).astype(BF)
    local_heads = projected.shape[2] // HEAD_DIM
    queries = projected[0].reshape(row_count, local_heads, HEAD_DIM)
    key_heads = projected[1].reshape(row_count, local_heads, HEAD_DIM)
    value_heads = projected[2].reshape(row_count, local_heads, HEAD_DIM)
    patch_ids = jnp.repeat(image_ids.reshape(-1), MERGE)
    block_rows = min(512, row_count)

    def one_block(block_index):
        first_row = block_index * block_rows
        query_part = lax.dynamic_slice_in_dim(queries, first_row, block_rows, 0)
        id_part = lax.dynamic_slice_in_dim(patch_ids, first_row, block_rows, 0)
        scores = jnp.einsum(
            "qhd,khd->hqk", query_part, key_heads, preferred_element_type=F32
        ) * HEAD_DIM ** (-0.5)
        same_image = id_part[:, None] == patch_ids[None, :]
        scores = jnp.where(same_image[None, :, :], scores, -1e30)
        highest = jnp.max(scores, axis=2, keepdims=True)
        weights = jnp.exp(scores - highest)
        attention = (weights / jnp.sum(weights, axis=2, keepdims=True)).astype(BF)
        context = jnp.einsum("hqk,khd->qhd", attention, value_heads, preferred_element_type=F32)
        return context.astype(BF).reshape(block_rows, local_heads * HEAD_DIM)

    contexts = lax.map(one_block, jnp.arange(row_count // block_rows))
    return contexts.reshape(row_count, local_heads * HEAD_DIM)


def swap_tp(block, k):
    return lax.ppermute(block, TP, [(i, i ^ k) for i in range(4)])


def shift_y(block, d):
    return lax.ppermute(block, ("yh", "yl"), [(i, (i + d) % 4) for i in range(4)])


def swap_core(block):
    return lax.ppermute(block, "c", [(0, 1), (1, 0)])


def on_device(
    patches,
    image_ids,
    qkv_weight,
    out_weight,
    merge_gain,
    merge_weight,
    text_rows,
    image_refs,
    llm_gain,
):
    yh = lax.axis_index("yh")
    tp = lax.axis_index(TP)
    y = lax.axis_index(("yh", "yl"))
    core = lax.axis_index("c")

    half = merge_weight.shape[1] // 2
    own = lax.dynamic_slice_in_dim(merge_weight, yh * half, half, 1)
    other = lax.dynamic_slice_in_dim(merge_weight, (1 - yh) * half, half, 1)
    arrived = lax.ppermute(other, "yh", [(0, 1), (1, 0)])
    both = jnp.concatenate(
        [jnp.where(yh == 0, own, arrived), jnp.where(yh == 0, arrived, own)], axis=0
    )
    weight = lax.all_gather(both, ("z", "x"), axis=0, tiled=True)

    out_blocks = [out_weight] + [swap_tp(out_weight, k) for k in (1, 2, 3)]

    prompt_rows = image_refs.shape[0]
    usable = image_refs >= 0
    source = jnp.where(usable, image_refs // 256, -1)
    hits = (source[:, None] == jnp.arange(32)[None, :]).astype(BF)
    before = (jnp.arange(prompt_rows)[:, None] > jnp.arange(prompt_rows)[None, :]).astype(BF)
    earlier = jnp.dot(before, hits, preferred_element_type=F32)
    arrival = jnp.sum(earlier * hits.astype(F32), axis=1).astype(jnp.int32)
    slot = jnp.where(usable, source * 16 + arrival, -1)
    pick = (slot[:, None] == jnp.arange(512)[None, :]).astype(BF)
    names = jnp.where(usable, image_refs % 256 + 1, 0).astype(BF)
    table = jnp.dot(names[None, :], pick, preferred_element_type=F32).astype(jnp.int32)
    table = jnp.broadcast_to(table.reshape(16, 1, 32), (16, 2, 32)).reshape(32, 32)
    table = lax.all_to_all(table, SEC, split_axis=0, concat_axis=0, tiled=True)

    context = vision_context(patches, image_ids, qkv_weight)
    rows = context.shape[0] // 4
    parts = [
        lax.dynamic_slice_in_dim(context, (tp ^ k) * rows, rows, 0) for k in range(4)
    ]
    parts = [parts[0]] + [swap_tp(parts[k], k) for k in (1, 2, 3)]
    terms = sum(
        jnp.dot(part, block, preferred_element_type=F32)
        for part, block in zip(parts, out_blocks)
    )
    own_patches = lax.dynamic_slice_in_dim(patches, tp * rows, rows, 0)
    attended = own_patches.astype(F32) + terms
    moment = jnp.mean(attended * attended, axis=1, keepdims=True)
    normed = (attended * lax.rsqrt(moment + EPSILON) * merge_gain).astype(BF)
    merged = normed.reshape(rows // MERGE, MERGE * normed.shape[1])

    n = merged.shape[0]
    far = jnp.concatenate([shift_y(merged[: n // 2], 2), shift_y(merged[n // 2 :], -2)], axis=0)
    ring = [merged, shift_y(merged, 1), shift_y(merged, -1), far]
    blocks = []
    ids = []
    for d, block in zip((0, 1, -1, 2), ring):
        blocks += [block, swap_core(block)]
        origin = (y - d + 4) % 4
        ids += [origin * 128 + core * 64, origin * 128 + (1 - core) * 64]
    ring_rows = jnp.concatenate(blocks, axis=0)
    row_ids = (jnp.stack(ids)[:, None] + jnp.arange(n)[None, :]).reshape(-1)

    image_rows = jnp.dot(ring_rows, weight, preferred_element_type=F32).astype(BF)
    wanted = table.reshape(32, 2, 16) - 1
    wanted = jnp.where(wanted >= 0, wanted + jnp.arange(2)[None, :, None] * 256, -1).reshape(-1)
    send = (wanted[:, None] == row_ids[None, :]).astype(BF)
    outgoing = jnp.dot(send, image_rows, preferred_element_type=F32).astype(BF)
    received = lax.all_to_all(outgoing, SEC, split_axis=0, concat_axis=0, tiled=True)
    received = received.reshape(16, 2, 32, half)
    picked = jnp.concatenate(
        [
            jnp.dot(pick, received[:, h].reshape(512, half), preferred_element_type=F32).astype(BF)
            for h in range(2)
        ],
        axis=1,
    )
    prompt = jnp.where(usable[:, None], picked, text_rows)
    widened = prompt.astype(F32)
    squares = lax.psum(jnp.sum(widened * widened, axis=1), TP)
    total_width = widened.shape[1] * 4
    inverse = lax.rsqrt(squares / total_width + EPSILON)
    return (widened * inverse[:, None] * llm_gain[None, :]).astype(BF)


def solution(mesh):
    torus = Mesh(mesh.devices.reshape(4, 4, 2, 2, 2), ("z", "x", "yh", "yl", "c"))
    return jax.shard_map(
        on_device,
        mesh=torus,
        in_specs=(
            P(SEC, None),
            P(SEC, None),
            P(None, None, TP),
            P(TP, None),
            P(),
            P(SEC, TP),
            P(SEC, TP),
            P(SEC),
            P(TP),
        ),
        out_specs=P(SEC, TP),
        check_vma=False,
    )
```

```python
import jax
import jax.numpy as jnp
from jax import lax
from jax.experimental import pallas as pl
from jax.experimental.pallas import tpu as pltpu
from jax.sharding import Mesh, PartitionSpec as P

HEAD_DIM = 80
MERGE = 4
EPSILON = 1e-06
LOG2E = 1.4426950408889634
SEC = ("z", "x", "yh")
TP = ("yl", "c")
BF = jnp.bfloat16
F32 = jnp.float32


def attention_kernel(row_ids, column_ids, projected, context, keys, values):
    heads = keys.shape[0]
    row_count = projected.shape[1]
    one = jnp.ones((row_count, 128 - HEAD_DIM), BF)
    for head in range(heads):
        columns = slice(head * HEAD_DIM, (head + 1) * HEAD_DIM)
        keys[head] = projected[1, :, columns]
        values[head] = jnp.concatenate([projected[2, :, columns], one], axis=1)
    scale = HEAD_DIM ** (-0.5) * LOG2E
    block = min(256, row_count)

    def one_block(index, carry):
        rows = pl.ds(pl.multiple_of(index * block, block), block)
        same_image = row_ids[rows, :] == column_ids[...]
        outs = []
        for head in range(heads):
            query = projected[0, rows, head * HEAD_DIM : (head + 1) * HEAD_DIM]
            scores = lax.dot_general(
                query, keys[head], (((1,), (1,)), ((), ())), preferred_element_type=F32
            )
            scores = jnp.where(same_image, scores, -1e30)
            highest = jnp.max(scores, axis=1, keepdims=True)
            weights = jnp.exp2((scores - highest) * scale).astype(BF)
            summed = jnp.dot(weights, values[head], preferred_element_type=F32)
            outs.append(summed[:, :HEAD_DIM] / summed[:, HEAD_DIM : HEAD_DIM + 1])
        context[rows, :] = jnp.concatenate(outs, axis=1).astype(BF)
        return carry

    lax.fori_loop(0, row_count // block, one_block, 0)


def vision_context(projected, image_ids):
    row_count, width = projected.shape[1:]
    heads = width // HEAD_DIM
    patch_ids = jnp.repeat(image_ids.reshape(-1), MERGE)
    return pl.pallas_call(
        attention_kernel,
        out_shape=jax.ShapeDtypeStruct((row_count, width), BF),
        in_specs=[pl.BlockSpec(memory_space=pltpu.VMEM)] * 3,
        out_specs=pl.BlockSpec(memory_space=pltpu.VMEM),
        scratch_shapes=[
            pltpu.VMEM((heads, row_count, HEAD_DIM), BF),
            pltpu.VMEM((heads, row_count, 128), BF),
        ],
        compiler_params=pltpu.CompilerParams(vmem_limit_bytes=40 * 2**20),
        cost_estimate=pl.CostEstimate(
            flops=4 * heads * row_count * row_count * 256,
            bytes_accessed=8 * row_count * width,
            transcendentals=heads * row_count * row_count,
        ),
        name="vision_attention",
    )(patch_ids[:, None], patch_ids[None, :], projected)


def merge_kernel(*refs):
    blocks, (weight, send, outgoing, rows) = refs[:8], refs[8:]
    n = blocks[0].shape[0]

    @pl.when(pl.program_id(0) == 0)
    def _():
        for k in range(8):
            rows[k * n : (k + 1) * n, :] = blocks[k][...]

    image = jnp.dot(rows[...], weight[...], preferred_element_type=F32).astype(BF)
    outgoing[...] = jnp.dot(send[...], image, preferred_element_type=F32).astype(BF)


def merge_and_select(blocks, weight, send, tile=256):
    depth, columns = weight.shape
    n = blocks[0].shape[0]
    slots = send.shape[0]
    whole = lambda shape: pl.BlockSpec(shape, lambda i: (0, 0), pipeline_mode=pl.Buffered(1))
    return pl.pallas_call(
        merge_kernel,
        grid=(columns // tile,),
        out_shape=jax.ShapeDtypeStruct((slots, columns), BF),
        in_specs=[whole((n, depth))] * 8
        + [pl.BlockSpec((depth, tile), lambda i: (0, i)), whole(send.shape)],
        out_specs=pl.BlockSpec((slots, tile), lambda i: (0, i)),
        scratch_shapes=[pltpu.VMEM((8 * n, depth), BF)],
        compiler_params=pltpu.CompilerParams(vmem_limit_bytes=48 * 2**20),
        cost_estimate=pl.CostEstimate(
            flops=2 * 8 * n * (depth + slots) * columns,
            bytes_accessed=2 * (8 * n * depth + depth * columns + slots * columns),
            transcendentals=0,
        ),
        name="merge_rows",
    )(*blocks, weight, send)


def swap_tp(block, k):
    return lax.ppermute(block, TP, [(i, i ^ k) for i in range(4)])


def shift_y(block, d):
    return lax.ppermute(block, ("yh", "yl"), [(i, (i + d) % 4) for i in range(4)])


def swap_core(block):
    return lax.ppermute(block, "c", [(0, 1), (1, 0)])


def on_device(
    patches,
    image_ids,
    qkv_weight,
    out_weight,
    merge_gain,
    merge_weight,
    text_rows,
    image_refs,
    llm_gain,
):
    yh = lax.axis_index("yh")
    tp = lax.axis_index(TP)
    y = lax.axis_index(("yh", "yl"))
    core = lax.axis_index("c")

    half = merge_weight.shape[1] // 2
    own = lax.dynamic_slice_in_dim(merge_weight, yh * half, half, 1)
    other = lax.dynamic_slice_in_dim(merge_weight, (1 - yh) * half, half, 1)
    arrived = lax.ppermute(other, "yh", [(0, 1), (1, 0)])
    projected = jnp.einsum("pd,cde->cpe", patches, qkv_weight, preferred_element_type=F32)
    projected = projected.astype(BF)
    arrived, projected = lax.optimization_barrier((arrived, projected))
    both = jnp.concatenate(
        [jnp.where(yh == 0, own, arrived), jnp.where(yh == 0, arrived, own)], axis=0
    )

    out_blocks = [out_weight] + [swap_tp(out_weight, k) for k in (1, 2, 3)]

    prompt_rows = image_refs.shape[0]
    usable = image_refs >= 0
    source = jnp.where(usable, image_refs // 256, -1)
    hits = (source[:, None] == jnp.arange(32)[None, :]).astype(BF)
    before = (jnp.arange(prompt_rows)[:, None] > jnp.arange(prompt_rows)[None, :]).astype(BF)
    earlier = jnp.dot(before, hits, preferred_element_type=F32)
    arrival = jnp.sum(earlier * hits.astype(F32), axis=1).astype(jnp.int32)
    slot = jnp.where(usable, source * 16 + arrival, -1)
    pick = (slot[:, None] == jnp.arange(512)[None, :]).astype(BF)
    names = jnp.where(usable, image_refs % 256 + 1, 0).astype(BF)
    table = jnp.dot(names[None, :], pick, preferred_element_type=F32).astype(jnp.int32)
    table = jnp.broadcast_to(table.reshape(16, 1, 32), (16, 2, 32)).reshape(32, 32)
    table, both, projected = lax.optimization_barrier((table, both, projected))
    weight = lax.all_gather(both, ("z", "x"), axis=0, tiled=True)
    table = lax.all_to_all(table, SEC, split_axis=0, concat_axis=0, tiled=True)

    context = vision_context(projected, image_ids)
    context, table, *out_blocks = lax.optimization_barrier((context, table, *out_blocks))
    rows = context.shape[0] // 4
    parts = [
        lax.dynamic_slice_in_dim(context, (tp ^ k) * rows, rows, 0) for k in range(4)
    ]
    parts = [parts[0]] + [swap_tp(parts[k], k) for k in (1, 2, 3)]
    terms = sum(
        jnp.dot(part, block, preferred_element_type=F32)
        for part, block in zip(parts, out_blocks)
    )
    own_patches = lax.dynamic_slice_in_dim(patches, tp * rows, rows, 0)
    attended = own_patches.astype(F32) + terms
    moment = jnp.mean(attended * attended, axis=1, keepdims=True)
    normed = (attended * lax.rsqrt(moment + EPSILON) * merge_gain).astype(BF)
    merged = normed.reshape(rows // MERGE, MERGE * normed.shape[1])

    n = merged.shape[0]
    far = jnp.concatenate([shift_y(merged[: n // 2], 2), shift_y(merged[n // 2 :], -2)], axis=0)
    ring = [merged, shift_y(merged, 1), shift_y(merged, -1), far]
    blocks = []
    ids = []
    for d, block in zip((0, 1, -1, 2), ring):
        blocks += [block, swap_core(block)]
        origin = (y - d + 4) % 4
        ids += [origin * 128 + core * 64, origin * 128 + (1 - core) * 64]
    row_ids = (jnp.stack(ids)[:, None] + jnp.arange(n)[None, :]).reshape(-1)

    wanted = table.reshape(32, 2, 16) - 1
    wanted = jnp.where(wanted >= 0, wanted + jnp.arange(2)[None, :, None] * 256, -1).reshape(-1)
    send = (wanted[:, None] == row_ids[None, :]).astype(BF)
    outgoing = merge_and_select(blocks, weight, send)
    received = lax.all_to_all(outgoing, SEC, split_axis=0, concat_axis=0, tiled=True)
    received = received.reshape(16, 2, 32, half)
    picked = jnp.concatenate(
        [
            jnp.dot(pick, received[:, h].reshape(512, half), preferred_element_type=F32).astype(BF)
            for h in range(2)
        ],
        axis=1,
    )
    prompt = jnp.where(usable[:, None], picked, text_rows)
    widened = prompt.astype(F32)
    squares = lax.psum(jnp.sum(widened * widened, axis=1), TP)
    total_width = widened.shape[1] * 4
    inverse = lax.rsqrt(squares / total_width + EPSILON)
    return (widened * inverse[:, None] * llm_gain[None, :]).astype(BF)


def solution(mesh):
    torus = Mesh(mesh.devices.reshape(4, 4, 2, 2, 2), ("z", "x", "yh", "yl", "c"))
    return jax.shard_map(
        on_device,
        mesh=torus,
        in_specs=(
            P(SEC, None),
            P(SEC, None),
            P(None, None, TP),
            P(TP, None),
            P(),
            P(SEC, TP),
            P(SEC, TP),
            P(SEC),
            P(TP),
        ),
        out_specs=P(SEC, TP),
        check_vma=False,
    )
```

```python
import jax
import jax.numpy as jnp
from jax import lax
from jax.experimental import pallas as pl
from jax.experimental.pallas import tpu as pltpu
from jax.sharding import Mesh, PartitionSpec as P

HEAD_DIM = 80
MERGE = 4
EPSILON = 1e-06
LOG2E = 1.4426950408889634
SEC = ("z", "x", "yh")
TP = ("yl", "c")
BF = jnp.bfloat16
F32 = jnp.float32


def attention_kernel(row_ids, column_ids, projected, context, keys, values):
    heads = keys.shape[0]
    row_count = projected.shape[1]
    one = jnp.ones((row_count, 128 - HEAD_DIM), BF)
    for head in range(heads):
        columns = slice(head * HEAD_DIM, (head + 1) * HEAD_DIM)
        keys[head] = projected[1, :, columns]
        values[head] = jnp.concatenate([projected[2, :, columns], one], axis=1)
    scale = HEAD_DIM ** (-0.5) * LOG2E
    block = min(256, row_count)

    def one_block(index, carry):
        rows = pl.ds(pl.multiple_of(index * block, block), block)
        same_image = row_ids[rows, :] == column_ids[...]
        outs = []
        for head in range(heads):
            query = projected[0, rows, head * HEAD_DIM : (head + 1) * HEAD_DIM]
            scores = lax.dot_general(
                query, keys[head], (((1,), (1,)), ((), ())), preferred_element_type=F32
            )
            scores = jnp.where(same_image, scores, -1e30)
            highest = jnp.max(scores, axis=1, keepdims=True)
            weights = jnp.exp2((scores - highest) * scale).astype(BF)
            summed = jnp.dot(weights, values[head], preferred_element_type=F32)
            outs.append(summed[:, :HEAD_DIM] / summed[:, HEAD_DIM : HEAD_DIM + 1])
        context[rows, :] = jnp.concatenate(outs, axis=1).astype(BF)
        return carry

    lax.fori_loop(0, row_count // block, one_block, 0)


def vision_context(projected, image_ids):
    row_count, width = projected.shape[1:]
    heads = width // HEAD_DIM
    patch_ids = jnp.repeat(image_ids.reshape(-1), MERGE)
    return pl.pallas_call(
        attention_kernel,
        out_shape=jax.ShapeDtypeStruct((row_count, width), BF),
        in_specs=[pl.BlockSpec(memory_space=pltpu.VMEM)] * 3,
        out_specs=pl.BlockSpec(memory_space=pltpu.VMEM),
        scratch_shapes=[
            pltpu.VMEM((heads, row_count, HEAD_DIM), BF),
            pltpu.VMEM((heads, row_count, 128), BF),
        ],
        compiler_params=pltpu.CompilerParams(vmem_limit_bytes=40 * 2**20),
        cost_estimate=pl.CostEstimate(
            flops=4 * heads * row_count * row_count * 256,
            bytes_accessed=8 * row_count * width,
            transcendentals=heads * row_count * row_count,
        ),
        name="vision_attention",
    )(patch_ids[:, None], patch_ids[None, :], projected)


def project_kernel(patches, weight, projected):
    projected[0] = jnp.dot(patches[...], weight[0], preferred_element_type=F32).astype(BF)


def project(patches, weight):
    rows, depth = patches.shape
    count, _, width = weight.shape
    return pl.pallas_call(
        project_kernel,
        grid=(count,),
        out_shape=jax.ShapeDtypeStruct((count, rows, width), BF),
        in_specs=[
            pl.BlockSpec((rows, depth), lambda i: (0, 0), pipeline_mode=pl.Buffered(1)),
            pl.BlockSpec((1, depth, width), lambda i: (i, 0, 0)),
        ],
        out_specs=pl.BlockSpec((1, rows, width), lambda i: (i, 0, 0)),
        compiler_params=pltpu.CompilerParams(vmem_limit_bytes=32 * 2**20),
        cost_estimate=pl.CostEstimate(
            flops=2 * rows * depth * width * count,
            bytes_accessed=2 * (rows * depth + count * width * (depth + rows)),
            transcendentals=0,
        ),
        name="project_qkv",
    )(patches, weight)


def norm_kernel(*refs):
    tp, parts, outs, (patches, gain, merged, top, bottom, normed) = (
        refs[0], refs[1:5], refs[5:9], refs[9:],
    )
    attended = patches[...].astype(F32)
    for part, weight in zip(parts, outs):
        attended += jnp.dot(part[...], weight[...], preferred_element_type=F32)
    moment = jnp.mean(attended * attended, axis=1, keepdims=True)
    scaled = attended * lax.rsqrt(moment + EPSILON) * gain[...]
    count, width = merged.shape[0], scaled.shape[1]
    for q in range(width // 128):
        normed[q] = scaled[:, q * 128 : (q + 1) * 128]
    for j in range(MERGE):
        for q in range(width // 128):
            piece = normed[q, pl.ds(j, count, stride=MERGE), :].astype(BF)
            columns = slice(j * width + q * 128, j * width + (q + 1) * 128)
            merged[:, columns] = piece
            top[:, columns] = piece[: count // 2]
            bottom[:, columns] = piece[count // 2 :]


def project_and_norm(tp, parts, outs, patches, gain):
    rows, depth = parts[0].shape
    width = patches.shape[1]
    count = rows // MERGE
    whole = lambda shape: pl.BlockSpec(shape, lambda i, t: (0, 0))
    return pl.pallas_call(
        norm_kernel,
        grid_spec=pltpu.PrefetchScalarGridSpec(
            num_scalar_prefetch=1,
            grid=(1,),
            in_specs=[whole((rows, depth))] * 4
            + [whole((depth, width))] * 4
            + [pl.BlockSpec((rows, width), lambda i, t: (t[0], 0)), whole((1, width))],
            out_specs=[
                whole((count, MERGE * width)),
                whole((count // 2, MERGE * width)),
                whole((count // 2, MERGE * width)),
            ],
            scratch_shapes=[pltpu.VMEM((width // 128, rows, 128), F32)],
        ),
        out_shape=[
            jax.ShapeDtypeStruct((count, MERGE * width), BF),
            jax.ShapeDtypeStruct((count // 2, MERGE * width), BF),
            jax.ShapeDtypeStruct((count // 2, MERGE * width), BF),
        ],
        compiler_params=pltpu.CompilerParams(vmem_limit_bytes=32 * 2**20),
        cost_estimate=pl.CostEstimate(
            flops=8 * rows * depth * width,
            bytes_accessed=8 * depth * (rows + width) + 4 * rows * width,
            transcendentals=rows,
        ),
        name="project_and_norm",
    )(tp.reshape(1).astype(jnp.int32), *parts, *outs, patches, gain[None, :])


def merge_kernel(*refs):
    blocks, (weight, send, outgoing, rows, total) = refs[:-5], refs[-5:]
    step = pl.program_id(0)
    first = 0
    for block in blocks:
        rows[first : first + block.shape[0], :] = block[...]
        first += block.shape[0]
    term = jnp.dot(rows[...], weight[...], preferred_element_type=F32)

    @pl.when(step == 0)
    def _():
        total[...] = term

    @pl.when(step > 0)
    def _():
        total[...] += term

    @pl.when(step == pl.num_programs(0) - 1)
    def _():
        image = total[...].astype(BF)
        outgoing[...] = jnp.dot(send[...], image, preferred_element_type=F32).astype(BF)


def merge_and_select(blocks, weight, send, tile=1280):
    depth, columns = weight.shape
    slots, count = send.shape
    return pl.pallas_call(
        merge_kernel,
        grid=(depth // tile,),
        out_shape=jax.ShapeDtypeStruct((slots, columns), BF),
        in_specs=[pl.BlockSpec((b.shape[0], tile), lambda i: (0, i)) for b in blocks]
        + [
            pl.BlockSpec((tile, columns), lambda i: (i, 0)),
            pl.BlockSpec((slots, count), lambda i: (0, 0), pipeline_mode=pl.Buffered(1)),
        ],
        out_specs=pl.BlockSpec((slots, columns), lambda i: (0, 0)),
        scratch_shapes=[pltpu.VMEM((count, tile), BF), pltpu.VMEM((count, columns), F32)],
        compiler_params=pltpu.CompilerParams(vmem_limit_bytes=48 * 2**20),
        cost_estimate=pl.CostEstimate(
            flops=2 * count * (depth + slots) * columns,
            bytes_accessed=2 * (count * depth + depth * columns + slots * columns),
            transcendentals=0,
        ),
        name="merge_rows",
    )(*blocks, weight, send)


def swap_tp(block, k):
    return lax.ppermute(block, TP, [(i, i ^ k) for i in range(4)])


def shift_y(block, d):
    return lax.ppermute(block, ("yh", "yl"), [(i, (i + d) % 4) for i in range(4)])


def swap_core(block):
    return lax.ppermute(block, "c", [(0, 1), (1, 0)])


def on_device(
    patches,
    image_ids,
    qkv_weight,
    out_weight,
    merge_gain,
    merge_weight,
    text_rows,
    image_refs,
    llm_gain,
):
    yh = lax.axis_index("yh")
    tp = lax.axis_index(TP)
    y = lax.axis_index(("yh", "yl"))
    core = lax.axis_index("c")

    half = merge_weight.shape[1] // 2
    own = lax.dynamic_slice_in_dim(merge_weight, yh * half, half, 1)
    other = lax.dynamic_slice_in_dim(merge_weight, (1 - yh) * half, half, 1)
    arrived = lax.ppermute(other, "yh", [(0, 1), (1, 0)])
    projected = project(patches, qkv_weight)
    arrived, projected = lax.optimization_barrier((arrived, projected))
    both = jnp.concatenate(
        [jnp.where(yh == 0, own, arrived), jnp.where(yh == 0, arrived, own)], axis=0
    )

    out_blocks = [out_weight] + [swap_tp(out_weight, k) for k in (1, 2, 3)]

    prompt_rows = image_refs.shape[0]
    usable = image_refs >= 0
    source = jnp.where(usable, image_refs // 256, -1)
    hits = (source[:, None] == jnp.arange(32)[None, :]).astype(BF)
    before = (jnp.arange(prompt_rows)[:, None] > jnp.arange(prompt_rows)[None, :]).astype(BF)
    earlier = jnp.dot(before, hits, preferred_element_type=F32)
    arrival = jnp.sum(earlier * hits.astype(F32), axis=1).astype(jnp.int32)
    slot = jnp.where(usable, source * 16 + arrival, -1)
    pick = (slot[:, None] == jnp.arange(512)[None, :]).astype(BF)
    names = jnp.where(usable, image_refs % 256 + 1, 0).astype(BF)
    table = jnp.dot(names[None, :], pick, preferred_element_type=F32).astype(jnp.int32)
    table = jnp.broadcast_to(table.reshape(16, 1, 32), (16, 2, 32)).reshape(32, 32)
    both, projected = lax.optimization_barrier((both, projected))
    weight = lax.all_gather(both, ("z", "x"), axis=0, tiled=True)

    context = vision_context(projected, image_ids)
    rows = context.shape[0] // 4
    parts = [
        lax.dynamic_slice_in_dim(context, (tp ^ k) * rows, rows, 0) for k in range(4)
    ]
    parts = [parts[0]] + [swap_tp(parts[k], k) for k in (1, 2, 3)]
    merged, top, bottom = project_and_norm(tp, parts, out_blocks, patches, merge_gain)
    table, merged, top, bottom = lax.optimization_barrier((table, merged, top, bottom))
    table = lax.all_to_all(table, SEC, split_axis=0, concat_axis=0, tiled=True)

    ring = [
        (0, 0, merged),
        (1, 0, shift_y(merged, 1)),
        (-1, 0, shift_y(merged, -1)),
        (2, 0, shift_y(top, 2)),
        (2, top.shape[0], shift_y(bottom, -2)),
    ]
    blocks = []
    ids = []
    for d, first, block in ring:
        blocks += [block, swap_core(block)]
        origin = (y - d + 4) % 4 * 128 + first
        ids += [origin + c * 64 + jnp.arange(block.shape[0]) for c in (core, 1 - core)]
    row_ids = jnp.concatenate(ids)

    wanted = table.reshape(32, 2, 16) - 1
    wanted = jnp.where(wanted >= 0, wanted + jnp.arange(2)[None, :, None] * 256, -1).reshape(-1)
    send = (wanted[:, None] == row_ids[None, :]).astype(BF)
    outgoing = merge_and_select(blocks, weight, send)
    received = lax.all_to_all(outgoing, SEC, split_axis=0, concat_axis=0, tiled=True)
    received = received.reshape(16, 2, 32, half)
    picked = jnp.concatenate(
        [
            jnp.dot(pick, received[:, h].reshape(512, half), preferred_element_type=F32).astype(BF)
            for h in range(2)
        ],
        axis=1,
    )
    prompt = jnp.where(usable[:, None], picked, text_rows)
    widened = prompt.astype(F32)
    squares = lax.psum(jnp.sum(widened * widened, axis=1), TP)
    total_width = widened.shape[1] * 4
    inverse = lax.rsqrt(squares / total_width + EPSILON)
    return (widened * inverse[:, None] * llm_gain[None, :]).astype(BF)


def solution(mesh):
    torus = Mesh(mesh.devices.reshape(4, 4, 2, 2, 2), ("z", "x", "yh", "yl", "c"))
    return jax.shard_map(
        on_device,
        mesh=torus,
        in_specs=(
            P(SEC, None),
            P(SEC, None),
            P(None, None, TP),
            P(TP, None),
            P(),
            P(SEC, TP),
            P(SEC, TP),
            P(SEC),
            P(TP),
        ),
        out_specs=P(SEC, TP),
        check_vma=False,
    )
```

```python
import functools

import jax
import jax.numpy as jnp
from jax import lax
from jax.experimental import pallas as pl
from jax.experimental.pallas import tpu as pltpu
from jax.sharding import Mesh, PartitionSpec as P

HEAD_DIM = 80
MERGE = 4
EPSILON = 1e-06
LOG2E = 1.4426950408889634
SEC = ("z", "x", "yh")
TP = ("yl", "c")
BF = jnp.bfloat16
F32 = jnp.float32


def attention_kernel(row_ids, column_ids, projected, context, keys, values):
    heads = keys.shape[0]
    row_count = projected.shape[1]
    one = jnp.ones((row_count, 128 - HEAD_DIM), BF)
    for head in range(heads):
        columns = slice(head * HEAD_DIM, (head + 1) * HEAD_DIM)
        keys[head] = projected[1, :, columns]
        values[head] = jnp.concatenate([projected[2, :, columns], one], axis=1)
    scale = HEAD_DIM ** (-0.5) * LOG2E
    block = min(256, row_count)

    def one_block(index, carry):
        rows = pl.ds(pl.multiple_of(index * block, block), block)
        same_image = row_ids[rows, :] == column_ids[...]
        outs = []
        for head in range(heads):
            query = projected[0, rows, head * HEAD_DIM : (head + 1) * HEAD_DIM]
            scores = lax.dot_general(
                query, keys[head], (((1,), (1,)), ((), ())), preferred_element_type=F32
            )
            scores = jnp.where(same_image, scores, -1e30)
            highest = jnp.max(scores, axis=1, keepdims=True)
            weights = jnp.exp2((scores - highest) * scale).astype(BF)
            summed = jnp.dot(weights, values[head], preferred_element_type=F32)
            outs.append(summed[:, :HEAD_DIM] / summed[:, HEAD_DIM : HEAD_DIM + 1])
        context[rows, :] = jnp.concatenate(outs, axis=1).astype(BF)
        return carry

    lax.fori_loop(0, row_count // block, one_block, 0)


def vision_context(projected, image_ids):
    row_count, width = projected.shape[1:]
    heads = width // HEAD_DIM
    patch_ids = jnp.repeat(image_ids.reshape(-1), MERGE)
    return pl.pallas_call(
        attention_kernel,
        out_shape=jax.ShapeDtypeStruct((row_count, width), BF),
        in_specs=[pl.BlockSpec(memory_space=pltpu.VMEM)] * 3,
        out_specs=pl.BlockSpec(memory_space=pltpu.VMEM),
        scratch_shapes=[
            pltpu.VMEM((heads, row_count, HEAD_DIM), BF),
            pltpu.VMEM((heads, row_count, 128), BF),
        ],
        compiler_params=pltpu.CompilerParams(vmem_limit_bytes=24 * 2**20),
        cost_estimate=pl.CostEstimate(
            flops=4 * heads * row_count * row_count * 256,
            bytes_accessed=8 * row_count * width,
            transcendentals=heads * row_count * row_count,
        ),
        name="vision_attention",
    )(patch_ids[:, None], patch_ids[None, :], projected)


def project_kernel(patches, weight, projected):
    projected[0] = lax.dot_general(
        patches[...], weight[0], (((1,), (1,)), ((), ())), preferred_element_type=F32
    ).astype(BF)


def project(patches, weight):
    rows, depth = patches.shape
    count, width, _ = weight.shape
    return pl.pallas_call(
        project_kernel,
        grid=(count,),
        out_shape=jax.ShapeDtypeStruct((count, rows, width), BF),
        in_specs=[
            pl.BlockSpec((rows, depth), lambda i: (0, 0), pipeline_mode=pl.Buffered(1)),
            pl.BlockSpec((1, width, depth), lambda i: (i, 0, 0)),
        ],
        out_specs=pl.BlockSpec((1, rows, width), lambda i: (i, 0, 0)),
        compiler_params=pltpu.CompilerParams(vmem_limit_bytes=14 * 2**20),
        cost_estimate=pl.CostEstimate(
            flops=2 * rows * depth * width * count,
            bytes_accessed=2 * (rows * depth + count * width * (depth + rows)),
            transcendentals=0,
        ),
        name="project_qkv",
    )(patches, weight)


def norm_kernel(*refs):
    tp, parts, outs, (patches, gain, merged, top, bottom, normed) = (
        refs[0], refs[1:5], refs[5:9], refs[9:],
    )
    attended = patches[...].astype(F32)
    for part, weight in zip(parts, outs):
        attended += jnp.dot(part[...], weight[...], preferred_element_type=F32)
    moment = jnp.mean(attended * attended, axis=1, keepdims=True)
    scaled = attended * lax.rsqrt(moment + EPSILON) * gain[...]
    count, width = merged.shape[0], scaled.shape[1]
    for q in range(width // 128):
        normed[q] = scaled[:, q * 128 : (q + 1) * 128]
    for j in range(MERGE):
        for q in range(width // 128):
            piece = normed[q, pl.ds(j, count, stride=MERGE), :].astype(BF)
            columns = slice(j * width + q * 128, j * width + (q + 1) * 128)
            merged[:, columns] = piece
            top[:, columns] = piece[: count // 2]
            bottom[:, columns] = piece[count // 2 :]


def project_and_norm(tp, parts, outs, patches, gain):
    rows, depth = parts[0].shape
    width = patches.shape[1]
    count = rows // MERGE
    whole = lambda shape: pl.BlockSpec(shape, lambda i, t: (0, 0))
    return pl.pallas_call(
        norm_kernel,
        grid_spec=pltpu.PrefetchScalarGridSpec(
            num_scalar_prefetch=1,
            grid=(1,),
            in_specs=[whole((rows, depth))] * 4
            + [whole((depth, width))] * 4
            + [pl.BlockSpec((rows, width), lambda i, t: (t[0], 0)), whole((1, width))],
            out_specs=[
                whole((count, MERGE * width)),
                whole((count // 2, MERGE * width)),
                whole((count // 2, MERGE * width)),
            ],
            scratch_shapes=[pltpu.VMEM((width // 128, rows, 128), F32)],
        ),
        out_shape=[
            jax.ShapeDtypeStruct((count, MERGE * width), BF),
            jax.ShapeDtypeStruct((count // 2, MERGE * width), BF),
            jax.ShapeDtypeStruct((count // 2, MERGE * width), BF),
        ],
        compiler_params=pltpu.CompilerParams(vmem_limit_bytes=24 * 2**20),
        cost_estimate=pl.CostEstimate(
            flops=8 * rows * depth * width,
            bytes_accessed=8 * depth * (rows + width) + 4 * rows * width,
            transcendentals=rows,
        ),
        name="project_and_norm",
    )(tp.reshape(1).astype(jnp.int32), *parts, *outs, patches, gain[None, :])


def merge_kernel(*refs):
    blocks, (weight, send, outgoing, rows, total) = refs[:-5], refs[-5:]
    step = pl.program_id(0)
    first = 0
    for block in blocks:
        rows[first : first + block.shape[0], :] = block[...]
        first += block.shape[0]
    term = jnp.dot(rows[...], weight[...], preferred_element_type=F32)

    @pl.when(step == 0)
    def _():
        total[...] = term

    @pl.when(step > 0)
    def _():
        total[...] += term

    @pl.when(step == pl.num_programs(0) - 1)
    def _():
        image = total[...].astype(BF)
        outgoing[...] = jnp.dot(send[...], image, preferred_element_type=F32).astype(BF)


def merge_and_select(blocks, weight, send, tile=1280):
    depth, columns = weight.shape
    slots, count = send.shape
    return pl.pallas_call(
        merge_kernel,
        grid=(depth // tile,),
        out_shape=jax.ShapeDtypeStruct((slots, columns), BF),
        in_specs=[pl.BlockSpec((b.shape[0], tile), lambda i: (0, i)) for b in blocks]
        + [
            pl.BlockSpec((tile, columns), lambda i: (i, 0)),
            pl.BlockSpec((slots, count), lambda i: (0, 0), pipeline_mode=pl.Buffered(1)),
        ],
        out_specs=pl.BlockSpec((slots, columns), lambda i: (0, 0)),
        scratch_shapes=[pltpu.VMEM((count, tile), BF), pltpu.VMEM((count, columns), F32)],
        compiler_params=pltpu.CompilerParams(vmem_limit_bytes=32 * 2**20),
        cost_estimate=pl.CostEstimate(
            flops=2 * count * (depth + slots) * columns,
            bytes_accessed=2 * (count * depth + depth * columns + slots * columns),
            transcendentals=0,
        ),
        name="merge_rows",
    )(*blocks, weight, send)


def pick_kernel(received, pick, usable, text, prompt, squares):
    arrived = received[...].reshape(pick.shape[1], received.shape[-1])
    picked = jnp.dot(pick[...], arrived, preferred_element_type=F32)
    value = jnp.where(usable[...] > 0, picked, text[...].astype(F32))
    prompt[...] = value.astype(BF)
    total = jnp.sum(value * value, axis=1, keepdims=True)

    @pl.when(pl.program_id(0) == 0)
    def _():
        squares[...] = total

    @pl.when(pl.program_id(0) > 0)
    def _():
        squares[...] += total


def pick_rows(received, pick, usable, text, offset):
    planes, halves, rows, part = received.shape
    count, slots = pick.shape
    return pl.pallas_call(
        pick_kernel,
        grid=(halves,),
        out_shape=[
            jax.ShapeDtypeStruct((count, halves * part), BF),
            jax.ShapeDtypeStruct((count, 1), F32),
        ],
        in_specs=[
            pl.BlockSpec((planes, 1, rows, part), lambda h: (0, h, 0, 0)),
            pl.BlockSpec((count, slots), lambda h: (0, 0), pipeline_mode=pl.Buffered(1)),
            pl.BlockSpec((count, 1), lambda h: (0, 0), pipeline_mode=pl.Buffered(1)),
            pl.BlockSpec((count, part), lambda h: (0, 2 * h + offset)),
        ],
        out_specs=[
            pl.BlockSpec((count, part), lambda h: (0, h)),
            pl.BlockSpec((count, 1), lambda h: (0, 0)),
        ],
        compiler_params=pltpu.CompilerParams(vmem_limit_bytes=14 * 2**20),
        cost_estimate=pl.CostEstimate(
            flops=2 * count * slots * halves * part,
            bytes_accessed=6 * count * halves * part,
            transcendentals=0,
        ),
        name="pick_rows",
    )(received, pick, usable, text)


def finish_kernel(early, late, squares, gain, out, *, width):
    inverse = lax.rsqrt(squares[...] / width + EPSILON)

    @pl.when(pl.program_id(0) % 2 == 0)
    def _():
        out[...] = (early[...].astype(F32) * inverse * gain[...]).astype(BF)

    @pl.when(pl.program_id(0) % 2 == 1)
    def _():
        out[...] = (late[...].astype(F32) * inverse * gain[...]).astype(BF)


def finish(early, late, squares, gain):
    count, width = early.shape
    part = width // 2
    return pl.pallas_call(
        functools.partial(finish_kernel, width=8 * width),
        grid=(4,),
        out_shape=jax.ShapeDtypeStruct((count, 2 * width), BF),
        in_specs=[
            pl.BlockSpec((count, part), lambda j: (0, j // 2)),
            pl.BlockSpec((count, part), lambda j: (0, j // 2)),
            pl.BlockSpec((count, 1), lambda j: (0, 0)),
            pl.BlockSpec((1, part), lambda j: (0, j)),
        ],
        out_specs=pl.BlockSpec((count, part), lambda j: (0, j)),
        compiler_params=pltpu.CompilerParams(vmem_limit_bytes=14 * 2**20),
        cost_estimate=pl.CostEstimate(
            flops=6 * count * width, bytes_accessed=8 * count * width, transcendentals=count
        ),
        name="finish",
    )(early, late, squares, gain[None, :])


def arrange_kernel(*refs):
    places, pieces, (whole, sems) = refs[0], refs[1:-2], refs[-2:]
    rows = whole.shape[0] // places.shape[0]
    copies = []
    for piece in pieces:
        for first in range(0, piece.shape[0], rows):
            index = len(copies)
            place = pl.multiple_of(places[index] * rows, rows)
            copy = pltpu.make_async_copy(
                piece.at[pl.ds(first, rows)], whole.at[pl.ds(place, rows)], sems.at[index]
            )
            copy.start()
            copies.append(copy)
    for copy in copies:
        copy.wait()


def arrange(places, pieces):
    rows = sum(piece.shape[0] for piece in pieces)
    columns = pieces[0].shape[1]
    return pl.pallas_call(
        arrange_kernel,
        out_shape=jax.ShapeDtypeStruct((rows, columns), BF),
        in_specs=[pl.BlockSpec(memory_space=pltpu.SMEM)]
        + [pl.BlockSpec(memory_space=pl.ANY)] * len(pieces),
        out_specs=pl.BlockSpec(memory_space=pl.ANY),
        scratch_shapes=[pltpu.SemaphoreType.DMA((places.shape[0],))],
        cost_estimate=pl.CostEstimate(
            flops=0, bytes_accessed=4 * rows * columns, transcendentals=0
        ),
        name="arrange_weight",
    )(places, *pieces)


def shift(block, axis, d):
    return lax.ppermute(block, axis, [(i, (i + d) % 4) for i in range(4)])


def ring(block, axis):
    n = block.shape[0] // 2
    before, after = shift(block, axis, 1), shift(block, axis, -1)
    return [block, before, after, shift(before[:n], axis, 1), shift(after[n:], axis, -1)]


def swap_tp(block, k):
    return lax.ppermute(block, TP, [(i, i ^ k) for i in range(4)])


def shift_y(block, d):
    return lax.ppermute(block, ("yh", "yl"), [(i, (i + d) % 4) for i in range(4)])


def swap_core(block):
    return lax.ppermute(block, "c", [(0, 1), (1, 0)])


def on_device(
    patches,
    image_ids,
    qkv_weight,
    out_weight,
    merge_gain,
    merge_weight,
    text_rows,
    image_refs,
    llm_gain,
):
    yh = lax.axis_index("yh")
    tp = lax.axis_index(TP)
    y = lax.axis_index(("yh", "yl"))
    core = lax.axis_index("c")

    half = merge_weight.shape[1] // 2
    part = half // 2
    own = lax.dynamic_slice_in_dim(merge_weight, yh * half, half, 1)
    other = lax.dynamic_slice_in_dim(merge_weight, (1 - yh) * half, half, 1)
    swap = lambda block: lax.ppermute(block, "yh", [(0, 1), (1, 0)])
    arrived = swap(other[:, :part])
    first_own = own[:, part:]
    first_other = swap(other[:, part:])
    is_own = (jnp.arange(2) == yh)[:, None, None]
    both = jnp.where(is_own, own[None, :, :part], arrived[None]).reshape(-1, part)
    weight = lax.all_gather(both, ("z", "x"), axis=0, tiled=True)
    own_z = ring(first_own, "z")
    other_x = ring(first_other, "x")
    own_zx = ring(jnp.concatenate(own_z, axis=0), "x")
    other_xz = ring(jnp.concatenate(other_x, axis=0), "z")
    near = jnp.array([0, -1, 1, 2])
    z_of = (lax.axis_index("z") + near) % 4
    x_of = (lax.axis_index("x") + near) % 4
    places = jnp.concatenate(
        [
            ((z_of[None, :] * 4 + x_of[:, None]) * 2 + yh).reshape(-1),
            ((z_of[:, None] * 4 + x_of[None, :]) * 2 + 1 - yh).reshape(-1),
        ]
    ).astype(jnp.int32)
    first_weight = arrange(places, own_zx + other_xz)

    out_weight, arrived = lax.optimization_barrier((out_weight, arrived))
    out_far = lax.ppermute(out_weight, "yl", [(0, 1), (1, 0)])
    out_blocks = [out_weight, swap_core(out_weight), out_far, swap_core(out_far)]

    projected = project(patches, jnp.swapaxes(qkv_weight, 1, 2))
    projected, both = lax.optimization_barrier((projected, both))

    prompt_rows = image_refs.shape[0]
    usable = image_refs >= 0
    source = jnp.where(usable, image_refs // 256, -1)
    hits = (source[:, None] == jnp.arange(32)[None, :]).astype(BF)
    before = (jnp.arange(prompt_rows)[:, None] > jnp.arange(prompt_rows)[None, :]).astype(BF)
    earlier = jnp.dot(before, hits, preferred_element_type=F32)
    arrival = jnp.sum(earlier * hits.astype(F32), axis=1).astype(jnp.int32)
    slot = jnp.where(usable, source * 16 + arrival, -1)
    pick = (slot[:, None] == jnp.arange(512)[None, :]).astype(BF)
    names = jnp.where(usable, image_refs % 256 + 1, 0).astype(BF)
    table = jnp.dot(names[None, :], pick, preferred_element_type=F32).astype(jnp.int32)
    table = jnp.broadcast_to(table.reshape(16, 1, 32), (16, 2, 32)).reshape(32, 32)
    context = vision_context(projected, image_ids)
    rows = context.shape[0] // 4
    parts = [
        lax.dynamic_slice_in_dim(context, (tp ^ k) * rows, rows, 0) for k in range(4)
    ]
    parts = [parts[0]] + [swap_tp(parts[k], k) for k in (1, 2, 3)]
    merged, top, bottom = project_and_norm(tp, parts, out_blocks, patches, merge_gain)
    table, merged, top, bottom = lax.optimization_barrier((table, merged, top, bottom))
    table = lax.all_to_all(table, SEC, split_axis=0, concat_axis=0, tiled=True)

    near_rows = [
        (0, 0, merged),
        (1, 0, shift_y(merged, 1)),
        (-1, 0, shift_y(merged, -1)),
        (2, 0, shift_y(top, 2)),
        (2, top.shape[0], shift_y(bottom, -2)),
    ]
    blocks = []
    ids = []
    for d, first, block in near_rows:
        blocks += [block, swap_core(block)]
        origin = (y - d + 4) % 4 * 128 + first
        ids += [origin + c * 64 + jnp.arange(block.shape[0]) for c in (core, 1 - core)]
    row_ids = jnp.concatenate(ids)

    wanted = table.reshape(32, 2, 16) - 1
    wanted = jnp.where(wanted >= 0, wanted + jnp.arange(2)[None, :, None] * 256, -1).reshape(-1)
    send = (wanted[:, None] == row_ids[None, :]).astype(BF)

    def route(weight):
        outgoing = merge_and_select(blocks, weight, send)
        received = lax.all_to_all(outgoing, SEC, split_axis=0, concat_axis=0, tiled=True)
        return received.reshape(16, 2, 32, -1)

    usable = usable.astype(jnp.int32)[:, None]
    late, late_squares = pick_rows(route(first_weight), pick, usable, text_rows, 1)
    early, early_squares = pick_rows(route(weight), pick, usable, text_rows, 0)
    squares = early_squares + late_squares
    flat = squares.reshape(4, -1)
    total = flat + swap_tp(flat, 1) + swap_tp(flat, 2) + swap_tp(flat, 3)
    return finish(early, late, total.reshape(squares.shape), llm_gain)


def solution(mesh):
    torus = Mesh(mesh.devices.reshape(4, 4, 2, 2, 2), ("z", "x", "yh", "yl", "c"))
    return jax.shard_map(
        on_device,
        mesh=torus,
        in_specs=(
            P(SEC, None),
            P(SEC, None),
            P(None, None, TP),
            P(TP, None),
            P(),
            P(SEC, TP),
            P(SEC, TP),
            P(SEC),
            P(TP),
        ),
        out_specs=P(SEC, TP),
        check_vma=False,
    )
```

```python
import functools

import jax
import jax.numpy as jnp
from jax import lax
from jax.experimental import pallas as pl
from jax.experimental.pallas import tpu as pltpu
from jax.sharding import Mesh, PartitionSpec as P

HEAD_DIM = 80
MERGE = 4
EPSILON = 1e-06
LOG2E = 1.4426950408889634
SEC = ("z", "x", "yh")
TP = ("yl", "c")
BF = jnp.bfloat16
FIRST = 256
F32 = jnp.float32


def attention_kernel(row_ids, column_ids, patches, weight, context, queries, keys, values):
    heads = keys.shape[0]
    row_count = patches.shape[0]
    block = min(256, row_count)
    one = jnp.ones((block, 128 - HEAD_DIM), BF)

    def project(index, carry):
        rows = pl.ds(pl.multiple_of(index * block, block), block)
        query, key, value = (
            lax.dot_general(
                patches[rows, :], weight[c], (((1,), (1,)), ((), ())), preferred_element_type=F32
            ).astype(BF)
            for c in range(3)
        )
        for head in range(heads):
            columns = slice(head * HEAD_DIM, (head + 1) * HEAD_DIM)
            queries[head, rows, :] = query[:, columns]
            keys[head, rows, :] = key[:, columns]
            values[head, rows, :] = jnp.concatenate([value[:, columns], one], axis=1)
        return carry

    lax.fori_loop(0, row_count // block, project, 0)
    scale = HEAD_DIM ** (-0.5) * LOG2E

    def one_block(index, carry):
        rows = pl.ds(pl.multiple_of(index * block, block), block)
        same_image = row_ids[rows, :] == column_ids[...]
        outs = []
        for head in range(heads):
            scores = lax.dot_general(
                queries[head, rows, :],
                keys[head],
                (((1,), (1,)), ((), ())),
                preferred_element_type=F32,
            )
            scores = jnp.where(same_image, scores, -1e30)
            highest = jnp.max(scores, axis=1, keepdims=True)
            weights = jnp.exp2((scores - highest) * scale).astype(BF)
            summed = jnp.dot(weights, values[head], preferred_element_type=F32)
            outs.append(summed[:, :HEAD_DIM] / summed[:, HEAD_DIM : HEAD_DIM + 1])
        context[rows, :] = jnp.concatenate(outs, axis=1).astype(BF)
        return carry

    lax.fori_loop(0, row_count // block, one_block, 0)


def vision_context(patches, weight, image_ids):
    row_count, depth = patches.shape
    width = weight.shape[1]
    heads = width // HEAD_DIM
    patch_ids = jnp.repeat(image_ids.reshape(-1), MERGE)
    return pl.pallas_call(
        attention_kernel,
        out_shape=jax.ShapeDtypeStruct((row_count, width), BF),
        in_specs=[pl.BlockSpec(memory_space=pltpu.VMEM)] * 4,
        out_specs=pl.BlockSpec(memory_space=pltpu.VMEM),
        scratch_shapes=[
            pltpu.VMEM((heads, row_count, HEAD_DIM), BF),
            pltpu.VMEM((heads, row_count, HEAD_DIM), BF),
            pltpu.VMEM((heads, row_count, 128), BF),
        ],
        compiler_params=pltpu.CompilerParams(vmem_limit_bytes=20 * 2**20),
        cost_estimate=pl.CostEstimate(
            flops=4 * heads * row_count * row_count * 256 + 6 * row_count * depth * width,
            bytes_accessed=2 * (row_count + 3 * width) * depth,
            transcendentals=heads * row_count * row_count,
        ),
        name="vision_attention",
    )(patch_ids[:, None], patch_ids[None, :], patches, weight)


def norm_kernel(*refs):
    tp, parts, outs, (patches, gain, merged, top, bottom, normed) = (
        refs[0], refs[1:5], refs[5:9], refs[9:],
    )
    attended = patches[...].astype(F32)
    for part, weight in zip(parts, outs):
        attended += jnp.dot(part[...], weight[...], preferred_element_type=F32)
    moment = jnp.mean(attended * attended, axis=1, keepdims=True)
    scaled = attended * lax.rsqrt(moment + EPSILON) * gain[...]
    count, width = merged.shape[0], scaled.shape[1]
    for q in range(width // 128):
        normed[q] = scaled[:, q * 128 : (q + 1) * 128]
    for j in range(MERGE):
        for q in range(width // 128):
            piece = normed[q, pl.ds(j, count, stride=MERGE), :].astype(BF)
            columns = slice(j * width + q * 128, j * width + (q + 1) * 128)
            merged[:, columns] = piece
            top[:, columns] = piece[: count // 2]
            bottom[:, columns] = piece[count // 2 :]


def project_and_norm(tp, parts, outs, patches, gain):
    rows, depth = parts[0].shape
    width = patches.shape[1]
    count = rows // MERGE
    whole = lambda shape: pl.BlockSpec(shape, lambda i, t: (0, 0))
    return pl.pallas_call(
        norm_kernel,
        grid_spec=pltpu.PrefetchScalarGridSpec(
            num_scalar_prefetch=1,
            grid=(1,),
            in_specs=[whole((rows, depth))] * 4
            + [whole((depth, width))] * 4
            + [pl.BlockSpec((rows, width), lambda i, t: (t[0], 0)), whole((1, width))],
            out_specs=[
                whole((count, MERGE * width)),
                whole((count // 2, MERGE * width)),
                whole((count // 2, MERGE * width)),
            ],
            scratch_shapes=[pltpu.VMEM((width // 128, rows, 128), F32)],
        ),
        out_shape=[
            jax.ShapeDtypeStruct((count, MERGE * width), BF),
            jax.ShapeDtypeStruct((count // 2, MERGE * width), BF),
            jax.ShapeDtypeStruct((count // 2, MERGE * width), BF),
        ],
        compiler_params=pltpu.CompilerParams(vmem_limit_bytes=18 * 2**20),
        cost_estimate=pl.CostEstimate(
            flops=8 * rows * depth * width,
            bytes_accessed=8 * depth * (rows + width) + 4 * rows * width,
            transcendentals=rows,
        ),
        name="project_and_norm",
    )(tp.reshape(1).astype(jnp.int32), *parts, *outs, patches, gain[None, :])


def first_merge_kernel(*refs):
    places, blocks, pieces, (send, outgoing, rows, whole) = (
        refs[0], refs[1:-9], refs[-9:-4], refs[-4:],
    )
    first = 0
    for block in blocks:
        rows[first : first + block.shape[0], :] = block[...]
        first += block.shape[0]
    unit = whole.shape[0] // places.shape[0]
    index = 0
    for piece in pieces:
        for first in range(0, piece.shape[0], unit):
            place = pl.multiple_of(places[index] * unit, unit)
            whole[pl.ds(place, unit), :] = piece[first : first + unit, :]
            index += 1
    depth = rows.shape[1]
    tile = depth // 4

    def step(k, total):
        first = pl.multiple_of(k * tile, tile)
        return total + jnp.dot(
            rows[:, pl.ds(first, tile)], whole[pl.ds(first, tile), :], preferred_element_type=F32
        )

    total = lax.fori_loop(0, 4, step, jnp.zeros((rows.shape[0], whole.shape[1]), F32))
    outgoing[...] = jnp.dot(
        send[...], total.astype(BF), preferred_element_type=F32
    ).astype(BF)


def first_merge(places, blocks, pieces, send):
    slots, count = send.shape
    depth, columns = blocks[0].shape[1], pieces[0].shape[1]
    vmem = pl.BlockSpec(memory_space=pltpu.VMEM)
    return pl.pallas_call(
        first_merge_kernel,
        out_shape=[
            jax.ShapeDtypeStruct((slots, columns), BF),
            jax.ShapeDtypeStruct((count, depth), BF),
        ],
        in_specs=[pl.BlockSpec(memory_space=pltpu.SMEM)]
        + [vmem] * (len(blocks) + len(pieces) + 1),
        out_specs=[vmem, vmem],
        scratch_shapes=[pltpu.VMEM((depth, columns), BF)],
        compiler_params=pltpu.CompilerParams(vmem_limit_bytes=20 * 2**20),
        cost_estimate=pl.CostEstimate(
            flops=2 * count * (depth + slots) * columns,
            bytes_accessed=2 * (count * depth + depth * columns + slots * columns),
            transcendentals=0,
        ),
        name="merge_first",
    )(places, *blocks, *pieces, send)


def merge_kernel(rows, weight, send, outgoing, total):
    step = pl.program_id(0)
    term = jnp.dot(rows[...], weight[...], preferred_element_type=F32)

    @pl.when(step == 0)
    def _():
        total[...] = term

    @pl.when(step > 0)
    def _():
        total[...] += term

    @pl.when(step == pl.num_programs(0) - 1)
    def _():
        image = total[...].astype(BF)
        outgoing[...] = jnp.dot(send[...], image, preferred_element_type=F32).astype(BF)


def merge_and_select(rows, weight, send, tile=1280):
    depth, columns = weight.shape
    slots, count = send.shape
    return pl.pallas_call(
        merge_kernel,
        grid=(depth // tile,),
        out_shape=jax.ShapeDtypeStruct((slots, columns), BF),
        in_specs=[
            pl.BlockSpec((count, tile), lambda i: (0, i)),
            pl.BlockSpec((tile, columns), lambda i: (i, 0)),
            pl.BlockSpec((slots, count), lambda i: (0, 0), pipeline_mode=pl.Buffered(1)),
        ],
        out_specs=pl.BlockSpec((slots, columns), lambda i: (0, 0)),
        scratch_shapes=[pltpu.VMEM((count, columns), F32)],
        compiler_params=pltpu.CompilerParams(vmem_limit_bytes=24 * 2**20),
        cost_estimate=pl.CostEstimate(
            flops=2 * count * (depth + slots) * columns,
            bytes_accessed=2 * (count * depth + depth * columns + slots * columns),
            transcendentals=0,
        ),
        name="merge_rows",
    )(rows, weight, send)


def pick_kernel(received, pick, usable, text, prompt, squares, *, first):
    arrived = received[...].reshape(pick.shape[1], received.shape[-1])
    picked = jnp.dot(pick[...], arrived, preferred_element_type=F32)
    own = text[:, first : first + picked.shape[1]].astype(F32)
    value = jnp.where(usable[...] > 0, picked, own)
    prompt[...] = value.astype(BF)
    total = jnp.sum(value * value, axis=1, keepdims=True)

    @pl.when(pl.program_id(0) == 0)
    def _():
        squares[...] = total

    @pl.when(pl.program_id(0) > 0)
    def _():
        squares[...] += total


def pick_rows(received, pick, usable, text, first):
    planes, halves, rows, part = received.shape
    count, slots = pick.shape
    half = text.shape[1] // halves
    return pl.pallas_call(
        functools.partial(pick_kernel, first=first),
        grid=(halves,),
        out_shape=[
            jax.ShapeDtypeStruct((count, halves * part), BF),
            jax.ShapeDtypeStruct((count, 1), F32),
        ],
        in_specs=[
            pl.BlockSpec((planes, 1, rows, part), lambda h: (0, h, 0, 0)),
            pl.BlockSpec((count, slots), lambda h: (0, 0), pipeline_mode=pl.Buffered(1)),
            pl.BlockSpec((count, 1), lambda h: (0, 0), pipeline_mode=pl.Buffered(1)),
            pl.BlockSpec((count, half), lambda h: (0, h)),
        ],
        out_specs=[
            pl.BlockSpec((count, part), lambda h: (0, h)),
            pl.BlockSpec((count, 1), lambda h: (0, 0)),
        ],
        compiler_params=pltpu.CompilerParams(vmem_limit_bytes=16 * 2**20),
        cost_estimate=pl.CostEstimate(
            flops=2 * count * slots * halves * part,
            bytes_accessed=6 * count * halves * part,
            transcendentals=0,
        ),
        name="pick_rows",
    )(received, pick, usable, text)


def finish_kernel(first, second, squares, gain, out, *, width):
    inverse = lax.rsqrt(squares[...] / width + EPSILON)
    part = first.shape[1]
    out[:, :part] = (first[...].astype(F32) * inverse * gain[:, :part]).astype(BF)
    out[:, part:] = (second[...].astype(F32) * inverse * gain[:, part:]).astype(BF)


def finish(first, second, squares, gain):
    count = first.shape[0]
    parts = first.shape[1] // 2, second.shape[1] // 2
    half = sum(parts)
    return pl.pallas_call(
        functools.partial(finish_kernel, width=8 * half),
        grid=(2,),
        out_shape=jax.ShapeDtypeStruct((count, 2 * half), BF),
        in_specs=[
            pl.BlockSpec((count, parts[0]), lambda h: (0, h)),
            pl.BlockSpec((count, parts[1]), lambda h: (0, h)),
            pl.BlockSpec((count, 1), lambda h: (0, 0)),
            pl.BlockSpec((1, half), lambda h: (0, h)),
        ],
        out_specs=pl.BlockSpec((count, half), lambda h: (0, h)),
        compiler_params=pltpu.CompilerParams(vmem_limit_bytes=14 * 2**20),
        cost_estimate=pl.CostEstimate(
            flops=6 * count * half, bytes_accessed=8 * count * half, transcendentals=count
        ),
        name="finish",
    )(first, second, squares, gain[None, :])


def shift(block, axis, d):
    return lax.ppermute(block, axis, [(i, (i + d) % 4) for i in range(4)])


def ring_near(block, axis):
    return [shift(block, axis, 1), shift(block, axis, -1)]


def ring_far(before, after, axis):
    n = before.shape[0] // 2
    return [shift(before[:n], axis, 1), shift(after[n:], axis, -1)]


def swap_tp(block, k):
    return lax.ppermute(block, TP, [(i, i ^ k) for i in range(4)])


def shift_y(block, d):
    return lax.ppermute(block, ("yh", "yl"), [(i, (i + d) % 4) for i in range(4)])


def swap_core(block):
    return lax.ppermute(block, "c", [(0, 1), (1, 0)])


def on_device(
    patches,
    image_ids,
    qkv_weight,
    out_weight,
    merge_gain,
    merge_weight,
    text_rows,
    image_refs,
    llm_gain,
):
    yh = lax.axis_index("yh")
    tp = lax.axis_index(TP)
    y = lax.axis_index(("yh", "yl"))
    core = lax.axis_index("c")

    half = merge_weight.shape[1] // 2
    own = lax.dynamic_slice_in_dim(merge_weight, yh * half, half, 1)
    other = lax.dynamic_slice_in_dim(merge_weight, (1 - yh) * half, half, 1)
    swap = lambda block: lax.ppermute(block, "yh", [(0, 1), (1, 0)])
    arrived = [swap(other[:, FIRST:]), swap(other[:, :FIRST])]

    prompt_rows = image_refs.shape[0]
    usable = image_refs >= 0
    source = jnp.where(usable, image_refs // 256, -1)
    hits = (source[:, None] == jnp.arange(32)[None, :]).astype(BF)
    before = (jnp.arange(prompt_rows)[:, None] > jnp.arange(prompt_rows)[None, :]).astype(BF)
    earlier = jnp.dot(before, hits, preferred_element_type=F32)
    arrival = jnp.sum(earlier * hits.astype(F32), axis=1).astype(jnp.int32)
    slot = jnp.where(usable, source * 16 + arrival, -1)
    pick = (slot[:, None] == jnp.arange(512)[None, :]).astype(BF)
    names = jnp.where(usable, image_refs % 256 + 1, 0).astype(BF)
    table = jnp.dot(names[None, :], pick, preferred_element_type=F32).astype(jnp.int32)
    table = jnp.broadcast_to(table.reshape(16, 1, 32), (16, 2, 32)).reshape(32, 32)
    usable = usable.astype(jnp.int32)[:, None]

    arrived, table, pick, usable, out_weight = lax.optimization_barrier(
        (arrived, table, pick, usable, out_weight)
    )
    is_own = (jnp.arange(2) == yh)[:, None, None]
    second = jnp.where(is_own, own[None, :, FIRST:], arrived[0][None]).reshape(-1, half - FIRST)
    first = jnp.where(is_own, own[None, :, :FIRST], arrived[1][None]).reshape(-1, FIRST)
    second_weight = lax.all_gather(second, ("z", "x"), axis=0, tiled=True)
    near_z = ring_near(first, "z")

    out_far = lax.ppermute(out_weight, "yl", [(0, 1), (1, 0)])
    out_blocks = [out_weight, swap_core(out_weight), out_far, swap_core(out_far)]

    patches, first, second = lax.optimization_barrier((patches, first, second))
    context = vision_context(patches, jnp.swapaxes(qkv_weight, 1, 2), image_ids)
    context, near_z = lax.optimization_barrier((context, near_z))
    far_z = ring_far(*near_z, "z")
    rows = context.shape[0] // 4
    parts = [
        lax.dynamic_slice_in_dim(context, (tp ^ k) * rows, rows, 0) for k in range(4)
    ]
    parts = [parts[0]] + [swap_tp(parts[k], k) for k in (1, 2, 3)]
    parts, far_z = lax.optimization_barrier((parts, far_z))
    all_z = jnp.concatenate([first] + near_z + far_z, axis=0)
    near_x = ring_near(all_z, "x")
    merged, top, bottom = project_and_norm(tp, parts, out_blocks, patches, merge_gain)

    table, merged, top, bottom = lax.optimization_barrier((table, merged, top, bottom))
    near_rows = [
        (0, 0, merged),
        (1, 0, shift_y(merged, 1)),
        (-1, 0, shift_y(merged, -1)),
        (2, 0, shift_y(top, 2)),
        (2, top.shape[0], shift_y(bottom, -2)),
    ]
    table = lax.all_to_all(table, SEC, split_axis=0, concat_axis=0, tiled=True)
    far_x = ring_far(*near_x, "x")
    near = jnp.array([0, -1, 1, 2])
    z_of = (lax.axis_index("z") + near) % 4
    x_of = (lax.axis_index("x") + near) % 4
    places = (z_of[None, :] * 4 + x_of[:, None]).reshape(-1).astype(jnp.int32)
    blocks = []
    ids = []
    for d, offset, block in near_rows:
        blocks += [block, swap_core(block)]
        origin = (y - d + 4) % 4 * 128 + offset
        ids += [origin + c * 64 + jnp.arange(block.shape[0]) for c in (core, 1 - core)]
    row_ids = jnp.concatenate(ids)

    wanted = table.reshape(32, 2, 16) - 1
    wanted = jnp.where(wanted >= 0, wanted + jnp.arange(2)[None, :, None] * 256, -1).reshape(-1)
    send = (wanted[:, None] == row_ids[None, :]).astype(BF)

    def route(outgoing, offset):
        received = lax.all_to_all(outgoing, SEC, split_axis=0, concat_axis=0, tiled=True)
        received = received.reshape(16, 2, 32, -1)
        return pick_rows(received, pick, usable, text_rows, offset)

    outgoing, all_rows = first_merge(places, blocks, [all_z] + near_x + far_x, send)
    first_prompt, first_squares = route(outgoing, 0)
    outgoing = merge_and_select(all_rows, second_weight, send)
    second_prompt, second_squares = route(outgoing, FIRST)
    squares = first_squares + second_squares
    flat = squares.reshape(4, -1)
    total = flat + swap_tp(flat, 1) + swap_tp(flat, 2) + swap_tp(flat, 3)
    return finish(first_prompt, second_prompt, total.reshape(squares.shape), llm_gain)


def solution(mesh):
    torus = Mesh(mesh.devices.reshape(4, 4, 2, 2, 2), ("z", "x", "yh", "yl", "c"))
    return jax.shard_map(
        on_device,
        mesh=torus,
        in_specs=(
            P(SEC, None),
            P(SEC, None),
            P(None, None, TP),
            P(TP, None),
            P(),
            P(SEC, TP),
            P(SEC, TP),
            P(SEC),
            P(TP),
        ),
        out_specs=P(SEC, TP),
        check_vma=False,
    )
```

```python
import functools

import jax
import jax.numpy as jnp
from jax import lax
from jax.experimental import pallas as pl
from jax.experimental.pallas import tpu as pltpu
from jax.sharding import Mesh, PartitionSpec as P

HEAD_DIM = 80
MERGE = 4
EPSILON = 1e-06
LOG2E = 1.4426950408889634
SEC = ("z", "x", "yh")
TP = ("yl", "c")
BF = jnp.bfloat16
F32 = jnp.float32


def attention_kernel(row_ids, column_ids, patches, weight, context, queries, keys, values):
    heads = keys.shape[0]
    row_count = patches.shape[0]
    block = min(256, row_count)
    one = jnp.ones((block, 128 - HEAD_DIM), BF)

    def project(index, carry):
        rows = pl.ds(pl.multiple_of(index * block, block), block)
        query, key, value = (
            lax.dot_general(
                patches[rows, :], weight[c], (((1,), (1,)), ((), ())), preferred_element_type=F32
            ).astype(BF)
            for c in range(3)
        )
        for head in range(heads):
            columns = slice(head * HEAD_DIM, (head + 1) * HEAD_DIM)
            queries[head, rows, :] = query[:, columns]
            keys[head, rows, :] = key[:, columns]
            values[head, rows, :] = jnp.concatenate([value[:, columns], one], axis=1)
        return carry

    lax.fori_loop(0, row_count // block, project, 0)
    scale = HEAD_DIM ** (-0.5) * LOG2E

    def one_block(index, carry):
        rows = pl.ds(pl.multiple_of(index * block, block), block)
        same_image = row_ids[rows, :] == column_ids[...]
        outs = []
        for head in range(heads):
            scores = lax.dot_general(
                queries[head, rows, :],
                keys[head],
                (((1,), (1,)), ((), ())),
                preferred_element_type=F32,
            )
            scores = jnp.where(same_image, scores, -1e30)
            highest = jnp.max(scores, axis=1, keepdims=True)
            weights = jnp.exp2((scores - highest) * scale).astype(BF)
            summed = jnp.dot(weights, values[head], preferred_element_type=F32)
            outs.append(summed[:, :HEAD_DIM] / summed[:, HEAD_DIM : HEAD_DIM + 1])
        context[rows, :] = jnp.concatenate(outs, axis=1).astype(BF)
        return carry

    lax.fori_loop(0, row_count // block, one_block, 0)


def vision_context(patches, weight, image_ids):
    row_count, depth = patches.shape
    width = weight.shape[1]
    heads = width // HEAD_DIM
    patch_ids = jnp.repeat(image_ids.reshape(-1), MERGE)
    return pl.pallas_call(
        attention_kernel,
        out_shape=jax.ShapeDtypeStruct((row_count, width), BF),
        in_specs=[pl.BlockSpec(memory_space=pltpu.VMEM)] * 4,
        out_specs=pl.BlockSpec(memory_space=pltpu.VMEM),
        scratch_shapes=[
            pltpu.VMEM((heads, row_count, HEAD_DIM), BF),
            pltpu.VMEM((heads, row_count, HEAD_DIM), BF),
            pltpu.VMEM((heads, row_count, 128), BF),
        ],
        compiler_params=pltpu.CompilerParams(vmem_limit_bytes=20 * 2**20),
        cost_estimate=pl.CostEstimate(
            flops=4 * heads * row_count * row_count * 256 + 6 * row_count * depth * width,
            bytes_accessed=2 * (row_count + 3 * width) * depth,
            transcendentals=heads * row_count * row_count,
        ),
        name="vision_attention",
    )(patch_ids[:, None], patch_ids[None, :], patches, weight)


def norm_kernel(*refs):
    tp, parts, outs, (patches, gain, merged, top, bottom, normed) = (
        refs[0], refs[1:5], refs[5:9], refs[9:],
    )
    attended = patches[...].astype(F32)
    for part, weight in zip(parts, outs):
        attended += jnp.dot(part[...], weight[...], preferred_element_type=F32)
    moment = jnp.mean(attended * attended, axis=1, keepdims=True)
    scaled = attended * lax.rsqrt(moment + EPSILON) * gain[...]
    count, width = merged.shape[0], scaled.shape[1]
    for q in range(width // 128):
        normed[q] = scaled[:, q * 128 : (q + 1) * 128]
    for j in range(MERGE):
        for q in range(width // 128):
            piece = normed[q, pl.ds(j, count, stride=MERGE), :].astype(BF)
            columns = slice(j * width + q * 128, j * width + (q + 1) * 128)
            merged[:, columns] = piece
            top[:, columns] = piece[: count // 2]
            bottom[:, columns] = piece[count // 2 :]


def project_and_norm(tp, parts, outs, patches, gain):
    rows, depth = parts[0].shape
    width = patches.shape[1]
    count = rows // MERGE
    whole = lambda shape: pl.BlockSpec(shape, lambda i, t: (0, 0))
    return pl.pallas_call(
        norm_kernel,
        grid_spec=pltpu.PrefetchScalarGridSpec(
            num_scalar_prefetch=1,
            grid=(1,),
            in_specs=[whole((rows, depth))] * 4
            + [whole((depth, width))] * 4
            + [pl.BlockSpec((rows, width), lambda i, t: (t[0], 0)), whole((1, width))],
            out_specs=[
                whole((count, MERGE * width)),
                whole((count // 2, MERGE * width)),
                whole((count // 2, MERGE * width)),
            ],
            scratch_shapes=[pltpu.VMEM((width // 128, rows, 128), F32)],
        ),
        out_shape=[
            jax.ShapeDtypeStruct((count, MERGE * width), BF),
            jax.ShapeDtypeStruct((count // 2, MERGE * width), BF),
            jax.ShapeDtypeStruct((count // 2, MERGE * width), BF),
        ],
        compiler_params=pltpu.CompilerParams(vmem_limit_bytes=18 * 2**20),
        cost_estimate=pl.CostEstimate(
            flops=8 * rows * depth * width,
            bytes_accessed=8 * depth * (rows + width) + 4 * rows * width,
            transcendentals=rows,
        ),
        name="project_and_norm",
    )(tp.reshape(1).astype(jnp.int32), *parts, *outs, patches, gain[None, :])


def merge_kernel(*refs):
    blocks, (weight, send, outgoing, rows, total) = refs[:-5], refs[-5:]
    step = pl.program_id(0)
    first = 0
    for block in blocks:
        rows[first : first + block.shape[0], :] = block[...]
        first += block.shape[0]
    term = jnp.dot(rows[...], weight[...], preferred_element_type=F32)

    @pl.when(step == 0)
    def _():
        total[...] = term

    @pl.when(step > 0)
    def _():
        total[...] += term

    @pl.when(step == pl.num_programs(0) - 1)
    def _():
        image = total[...].astype(BF)
        outgoing[...] = jnp.dot(send[...], image, preferred_element_type=F32).astype(BF)


def merge_and_select(blocks, weight, send, tile=640):
    depth, columns = weight.shape
    slots, count = send.shape
    return pl.pallas_call(
        merge_kernel,
        grid=(depth // tile,),
        out_shape=jax.ShapeDtypeStruct((slots, columns), BF),
        in_specs=[pl.BlockSpec((b.shape[0], tile), lambda i: (0, i)) for b in blocks]
        + [
            pl.BlockSpec((tile, columns), lambda i: (i, 0)),
            pl.BlockSpec((slots, count), lambda i: (0, 0), pipeline_mode=pl.Buffered(1)),
        ],
        out_specs=pl.BlockSpec((slots, columns), lambda i: (0, 0)),
        scratch_shapes=[pltpu.VMEM((count, tile), BF), pltpu.VMEM((count, columns), F32)],
        compiler_params=pltpu.CompilerParams(vmem_limit_bytes=24 * 2**20),
        cost_estimate=pl.CostEstimate(
            flops=2 * count * (depth + slots) * columns,
            bytes_accessed=2 * (count * depth + depth * columns + slots * columns),
            transcendentals=0,
        ),
        name="merge_rows",
    )(*blocks, weight, send)


def pick_kernel(received, pick, usable, text, prompt, squares):
    arrived = received[...].reshape(pick.shape[1], received.shape[-1])
    picked = jnp.dot(pick[...], arrived, preferred_element_type=F32)
    value = jnp.where(usable[...] > 0, picked, text[...].astype(F32))
    prompt[...] = value.astype(BF)
    total = jnp.sum(value * value, axis=1, keepdims=True)

    @pl.when(pl.program_id(0) == 0)
    def _():
        squares[...] = total

    @pl.when(pl.program_id(0) > 0)
    def _():
        squares[...] += total


def pick_rows(received, pick, usable, text):
    planes, halves, rows, part = received.shape
    count, slots = pick.shape
    return pl.pallas_call(
        pick_kernel,
        grid=(halves,),
        out_shape=[
            jax.ShapeDtypeStruct((count, halves * part), BF),
            jax.ShapeDtypeStruct((count, 1), F32),
        ],
        in_specs=[
            pl.BlockSpec((planes, 1, rows, part), lambda h: (0, h, 0, 0)),
            pl.BlockSpec((count, slots), lambda h: (0, 0), pipeline_mode=pl.Buffered(1)),
            pl.BlockSpec((count, 1), lambda h: (0, 0), pipeline_mode=pl.Buffered(1)),
            pl.BlockSpec((count, part), lambda h: (0, h)),
        ],
        out_specs=[
            pl.BlockSpec((count, part), lambda h: (0, h)),
            pl.BlockSpec((count, 1), lambda h: (0, 0)),
        ],
        compiler_params=pltpu.CompilerParams(vmem_limit_bytes=16 * 2**20),
        cost_estimate=pl.CostEstimate(
            flops=2 * count * slots * halves * part,
            bytes_accessed=6 * count * halves * part,
            transcendentals=0,
        ),
        name="pick_rows",
    )(received, pick, usable, text)


def finish_kernel(prompt, squares, gain, out, *, width):
    inverse = lax.rsqrt(squares[...] / width + EPSILON)
    out[...] = (prompt[...].astype(F32) * inverse * gain[...]).astype(BF)


def finish(prompt, squares, gain):
    count, width = prompt.shape
    part = width // 4
    return pl.pallas_call(
        functools.partial(finish_kernel, width=4 * width),
        grid=(4,),
        out_shape=jax.ShapeDtypeStruct((count, width), BF),
        in_specs=[
            pl.BlockSpec((count, part), lambda h: (0, h)),
            pl.BlockSpec((count, 1), lambda h: (0, 0)),
            pl.BlockSpec((1, part), lambda h: (0, h)),
        ],
        out_specs=pl.BlockSpec((count, part), lambda h: (0, h)),
        compiler_params=pltpu.CompilerParams(vmem_limit_bytes=10 * 2**20),
        cost_estimate=pl.CostEstimate(
            flops=3 * count * width, bytes_accessed=4 * count * width, transcendentals=count
        ),
        name="finish",
    )(prompt, squares, gain[None, :])


def swap_tp(block, k):
    return lax.ppermute(block, TP, [(i, i ^ k) for i in range(4)])


def shift_y(block, d):
    return lax.ppermute(block, ("yh", "yl"), [(i, (i + d) % 4) for i in range(4)])


def swap_core(block):
    return lax.ppermute(block, "c", [(0, 1), (1, 0)])


def on_device(
    patches,
    image_ids,
    qkv_weight,
    out_weight,
    merge_gain,
    merge_weight,
    text_rows,
    image_refs,
    llm_gain,
):
    yh = lax.axis_index("yh")
    tp = lax.axis_index(TP)
    y = lax.axis_index(("yh", "yl"))
    core = lax.axis_index("c")

    half = merge_weight.shape[1] // 2
    own = lax.dynamic_slice_in_dim(merge_weight, yh * half, half, 1)
    other = lax.dynamic_slice_in_dim(merge_weight, (1 - yh) * half, half, 1)
    arrived = lax.ppermute(other, "yh", [(0, 1), (1, 0)])

    prompt_rows = image_refs.shape[0]
    usable = image_refs >= 0
    source = jnp.where(usable, image_refs // 256, -1)
    hits = (source[:, None] == jnp.arange(32)[None, :]).astype(BF)
    before = (jnp.arange(prompt_rows)[:, None] > jnp.arange(prompt_rows)[None, :]).astype(BF)
    earlier = jnp.dot(before, hits, preferred_element_type=F32)
    arrival = jnp.sum(earlier * hits.astype(F32), axis=1).astype(jnp.int32)
    slot = jnp.where(usable, source * 16 + arrival, -1)
    pick = (slot[:, None] == jnp.arange(512)[None, :]).astype(BF)
    names = jnp.where(usable, image_refs % 256 + 1, 0).astype(BF)
    table = jnp.dot(names[None, :], pick, preferred_element_type=F32).astype(jnp.int32)
    table = jnp.broadcast_to(table.reshape(16, 1, 32), (16, 2, 32)).reshape(32, 32)
    usable = usable.astype(jnp.int32)[:, None]

    arrived, table, pick, usable, out_weight = lax.optimization_barrier(
        (arrived, table, pick, usable, out_weight)
    )
    is_own = (jnp.arange(2) == yh)[:, None, None]
    both = jnp.where(is_own, own[None], arrived[None]).reshape(-1, half)
    weight = lax.all_gather(both, ("z", "x"), axis=0, tiled=True)

    out_far = lax.ppermute(out_weight, "yl", [(0, 1), (1, 0)])
    out_blocks = [out_weight, swap_core(out_weight), out_far, swap_core(out_far)]

    patches, both = lax.optimization_barrier((patches, both))
    context = vision_context(patches, jnp.swapaxes(qkv_weight, 1, 2), image_ids)
    rows = context.shape[0] // 4
    parts = [
        lax.dynamic_slice_in_dim(context, (tp ^ k) * rows, rows, 0) for k in range(4)
    ]
    parts = [parts[0]] + [swap_tp(parts[k], k) for k in (1, 2, 3)]
    merged, top, bottom = project_and_norm(tp, parts, out_blocks, patches, merge_gain)

    table, merged, top, bottom = lax.optimization_barrier((table, merged, top, bottom))
    near_rows = [
        (0, 0, merged),
        (1, 0, shift_y(merged, 1)),
        (-1, 0, shift_y(merged, -1)),
        (2, 0, shift_y(top, 2)),
        (2, top.shape[0], shift_y(bottom, -2)),
    ]
    table = lax.all_to_all(table, SEC, split_axis=0, concat_axis=0, tiled=True)
    blocks = []
    ids = []
    for d, offset, block in near_rows:
        blocks += [block, swap_core(block)]
        origin = (y - d + 4) % 4 * 128 + offset
        ids += [origin + c * 64 + jnp.arange(block.shape[0]) for c in (core, 1 - core)]
    row_ids = jnp.concatenate(ids)

    wanted = table.reshape(32, 2, 16) - 1
    wanted = jnp.where(wanted >= 0, wanted + jnp.arange(2)[None, :, None] * 256, -1).reshape(-1)
    send = (wanted[:, None] == row_ids[None, :]).astype(BF)

    outgoing = merge_and_select(blocks, weight, send)
    received = lax.all_to_all(outgoing, SEC, split_axis=0, concat_axis=0, tiled=True)
    received = received.reshape(16, 2, 32, half)
    prompt, squares = pick_rows(received, pick, usable, text_rows)
    flat = squares.reshape(4, -1)
    total = flat + swap_tp(flat, 1) + swap_tp(flat, 2) + swap_tp(flat, 3)
    return finish(prompt, total.reshape(squares.shape), llm_gain)


def solution(mesh):
    torus = Mesh(mesh.devices.reshape(4, 4, 2, 2, 2), ("z", "x", "yh", "yl", "c"))
    return jax.shard_map(
        on_device,
        mesh=torus,
        in_specs=(
            P(SEC, None),
            P(SEC, None),
            P(None, None, TP),
            P(TP, None),
            P(),
            P(SEC, TP),
            P(SEC, TP),
            P(SEC),
            P(TP),
        ),
        out_specs=P(SEC, TP),
        check_vma=False,
    )
```

```python
import functools

import jax
import jax.numpy as jnp
from jax import lax
from jax.experimental import pallas as pl
from jax.experimental.pallas import tpu as pltpu
from jax.sharding import Mesh, PartitionSpec as P

HEAD_DIM = 80
MERGE = 4
EPSILON = 1e-06
LOG2E = 1.4426950408889634
SEC = ("z", "x", "yh")
TP = ("yl", "c")
BF = jnp.bfloat16
F32 = jnp.float32


def project_kernel(patches, weight, projected):
    projected[0] = lax.dot_general(
        patches[...], weight[0], (((1,), (1,)), ((), ())), preferred_element_type=F32
    ).astype(BF)


def project(patches, weight):
    rows, depth = patches.shape
    count, width, _ = weight.shape
    return pl.pallas_call(
        project_kernel,
        grid=(count,),
        out_shape=jax.ShapeDtypeStruct((count, rows, width), BF),
        in_specs=[
            pl.BlockSpec((rows, depth), lambda i: (0, 0), pipeline_mode=pl.Buffered(1)),
            pl.BlockSpec((1, width, depth), lambda i: (i, 0, 0)),
        ],
        out_specs=pl.BlockSpec((1, rows, width), lambda i: (i, 0, 0)),
        compiler_params=pltpu.CompilerParams(vmem_limit_bytes=14 * 2**20),
        cost_estimate=pl.CostEstimate(
            flops=2 * rows * depth * width * count,
            bytes_accessed=2 * (rows * depth + count * width * (depth + rows)),
            transcendentals=0,
        ),
        name="project_qkv",
    )(patches, weight)


def attention_kernel(row_ids, column_ids, projected, context, keys, values):
    heads = keys.shape[0]
    row_count = projected.shape[1]
    one = jnp.ones((row_count, 128 - HEAD_DIM), BF)
    for head in range(heads):
        columns = slice(head * HEAD_DIM, (head + 1) * HEAD_DIM)
        keys[head] = projected[1, :, columns]
        values[head] = jnp.concatenate([projected[2, :, columns], one], axis=1)
    scale = HEAD_DIM ** (-0.5) * LOG2E
    block = min(256, row_count)

    def one_block(index, carry):
        rows = pl.ds(pl.multiple_of(index * block, block), block)
        same_image = row_ids[rows, :] == column_ids[...]
        outs = []
        for head in range(heads):
            query = projected[0, rows, head * HEAD_DIM : (head + 1) * HEAD_DIM]
            scores = lax.dot_general(
                query, keys[head], (((1,), (1,)), ((), ())), preferred_element_type=F32
            )
            scores = jnp.where(same_image, scores, -1e30)
            highest = jnp.max(scores, axis=1, keepdims=True)
            weights = jnp.exp2((scores - highest) * scale).astype(BF)
            summed = jnp.dot(weights, values[head], preferred_element_type=F32)
            outs.append(summed[:, :HEAD_DIM] / summed[:, HEAD_DIM : HEAD_DIM + 1])
        context[rows, :] = jnp.concatenate(outs, axis=1).astype(BF)
        return carry

    lax.fori_loop(0, row_count // block, one_block, 0)


def vision_context(projected, patch_ids):
    row_count, width = projected.shape[1:]
    heads = width // HEAD_DIM
    return pl.pallas_call(
        attention_kernel,
        out_shape=jax.ShapeDtypeStruct((row_count, width), BF),
        in_specs=[pl.BlockSpec(memory_space=pltpu.VMEM)] * 3,
        out_specs=pl.BlockSpec(memory_space=pltpu.VMEM),
        scratch_shapes=[
            pltpu.VMEM((heads, row_count, HEAD_DIM), BF),
            pltpu.VMEM((heads, row_count, 128), BF),
        ],
        compiler_params=pltpu.CompilerParams(vmem_limit_bytes=20 * 2**20),
        cost_estimate=pl.CostEstimate(
            flops=4 * heads * row_count * row_count * 256,
            bytes_accessed=8 * row_count * width,
            transcendentals=heads * row_count * row_count,
        ),
        name="vision_attention",
    )(patch_ids[:, None], patch_ids[None, :], projected)


def norm_kernel(*refs):
    tp, parts, outs, (patches, gain, merged, top, bottom, normed) = (
        refs[0], refs[1:5], refs[5:9], refs[9:],
    )
    attended = patches[...].astype(F32)
    for part, weight in zip(parts, outs):
        attended += jnp.dot(part[...], weight[...], preferred_element_type=F32)
    moment = jnp.mean(attended * attended, axis=1, keepdims=True)
    scaled = attended * lax.rsqrt(moment + EPSILON) * gain[...]
    count, width = merged.shape[0], scaled.shape[1]
    for q in range(width // 128):
        normed[q] = scaled[:, q * 128 : (q + 1) * 128]
    for j in range(MERGE):
        for q in range(width // 128):
            piece = normed[q, pl.ds(j, count, stride=MERGE), :].astype(BF)
            columns = slice(j * width + q * 128, j * width + (q + 1) * 128)
            merged[:, columns] = piece
            top[:, columns] = piece[: count // 2]
            bottom[:, columns] = piece[count // 2 :]


def project_and_norm(tp, parts, outs, patches, gain):
    rows, depth = parts[0].shape
    width = patches.shape[1]
    count = rows // MERGE
    whole = lambda shape: pl.BlockSpec(shape, lambda i, t: (0, 0))
    return pl.pallas_call(
        norm_kernel,
        grid_spec=pltpu.PrefetchScalarGridSpec(
            num_scalar_prefetch=1,
            grid=(1,),
            in_specs=[whole((rows, depth))] * 4
            + [whole((depth, width))] * 4
            + [pl.BlockSpec((rows, width), lambda i, t: (t[0], 0)), whole((1, width))],
            out_specs=[
                whole((count, MERGE * width)),
                whole((count // 2, MERGE * width)),
                whole((count // 2, MERGE * width)),
            ],
            scratch_shapes=[pltpu.VMEM((width // 128, rows, 128), F32)],
        ),
        out_shape=[
            jax.ShapeDtypeStruct((count, MERGE * width), BF),
            jax.ShapeDtypeStruct((count // 2, MERGE * width), BF),
            jax.ShapeDtypeStruct((count // 2, MERGE * width), BF),
        ],
        compiler_params=pltpu.CompilerParams(vmem_limit_bytes=18 * 2**20),
        cost_estimate=pl.CostEstimate(
            flops=8 * rows * depth * width,
            bytes_accessed=8 * depth * (rows + width) + 4 * rows * width,
            transcendentals=rows,
        ),
        name="project_and_norm",
    )(tp.reshape(1).astype(jnp.int32), *parts, *outs, patches, gain[None, :])


def stack_kernel(*refs):
    first = 0
    for block in refs[:-1]:
        refs[-1][first : first + block.shape[0], :] = block[...]
        first += block.shape[0]


def stack_rows(blocks):
    count = sum(block.shape[0] for block in blocks)
    depth = blocks[0].shape[1]
    tile = depth // 4
    return pl.pallas_call(
        stack_kernel,
        grid=(depth // tile,),
        out_shape=jax.ShapeDtypeStruct((count, depth), BF),
        in_specs=[pl.BlockSpec((b.shape[0], tile), lambda i: (0, i)) for b in blocks],
        out_specs=pl.BlockSpec((count, tile), lambda i: (0, i)),
        compiler_params=pltpu.CompilerParams(vmem_limit_bytes=10 * 2**20),
        cost_estimate=pl.CostEstimate(
            flops=0, bytes_accessed=4 * count * depth, transcendentals=0
        ),
        name="stack_rows",
    )(*blocks)


def pick_kernel(received, pick, usable, text, prompt, squares):
    arrived = received[...].reshape(pick.shape[1], received.shape[-1])
    picked = jnp.dot(pick[...], arrived, preferred_element_type=F32)
    value = jnp.where(usable[...] > 0, picked, text[...].astype(F32))
    prompt[...] = value.astype(BF)
    total = jnp.sum(value * value, axis=1, keepdims=True)

    @pl.when(pl.program_id(0) == 0)
    def _():
        squares[...] = total

    @pl.when(pl.program_id(0) > 0)
    def _():
        squares[...] += total


def pick_rows(received, pick, usable, text):
    planes, halves, rows, part = received.shape
    count, slots = pick.shape
    return pl.pallas_call(
        pick_kernel,
        grid=(halves,),
        out_shape=[
            jax.ShapeDtypeStruct((count, halves * part), BF),
            jax.ShapeDtypeStruct((count, 1), F32),
        ],
        in_specs=[
            pl.BlockSpec((planes, 1, rows, part), lambda h: (0, h, 0, 0)),
            pl.BlockSpec((count, slots), lambda h: (0, 0), pipeline_mode=pl.Buffered(1)),
            pl.BlockSpec((count, 1), lambda h: (0, 0), pipeline_mode=pl.Buffered(1)),
            pl.BlockSpec((count, part), lambda h: (0, h)),
        ],
        out_specs=[
            pl.BlockSpec((count, part), lambda h: (0, h)),
            pl.BlockSpec((count, 1), lambda h: (0, 0)),
        ],
        compiler_params=pltpu.CompilerParams(vmem_limit_bytes=56 * 2**20),
        cost_estimate=pl.CostEstimate(
            flops=2 * count * slots * halves * part,
            bytes_accessed=6 * count * halves * part,
            transcendentals=0,
        ),
        name="pick_rows",
    )(received, pick, usable, text)


def finish_kernel(prompt, squares, gain, out, *, width):
    inverse = lax.rsqrt(squares[...] / width + EPSILON)
    out[...] = (prompt[...].astype(F32) * inverse * gain[...]).astype(BF)


def finish(prompt, squares, gain):
    count, width = prompt.shape
    part = width // 4
    return pl.pallas_call(
        functools.partial(finish_kernel, width=4 * width),
        grid=(4,),
        out_shape=jax.ShapeDtypeStruct((count, width), BF),
        in_specs=[
            pl.BlockSpec((count, part), lambda h: (0, h)),
            pl.BlockSpec((count, 1), lambda h: (0, 0)),
            pl.BlockSpec((1, part), lambda h: (0, h)),
        ],
        out_specs=pl.BlockSpec((count, part), lambda h: (0, h)),
        compiler_params=pltpu.CompilerParams(vmem_limit_bytes=56 * 2**20),
        cost_estimate=pl.CostEstimate(
            flops=3 * count * width, bytes_accessed=4 * count * width, transcendentals=count
        ),
        name="finish",
    )(prompt, squares, gain[None, :])


def swap_tp(block, k):
    return lax.ppermute(block, TP, [(i, i ^ k) for i in range(4)])


def shift_y(block, d):
    return lax.ppermute(block, ("yh", "yl"), [(i, (i + d) % 4) for i in range(4)])


def swap_core(block):
    return lax.ppermute(block, "c", [(0, 1), (1, 0)])


def on_device(
    patches,
    image_ids,
    qkv_weight,
    out_weight,
    merge_gain,
    merge_weight,
    text_rows,
    image_refs,
    llm_gain,
):
    yh = lax.axis_index("yh")
    tp = lax.axis_index(TP)
    y = lax.axis_index(("yh", "yl"))
    core = lax.axis_index("c")

    half = merge_weight.shape[1] // 2
    own = lax.dynamic_slice_in_dim(merge_weight, yh * half, half, 1)
    other = lax.dynamic_slice_in_dim(merge_weight, (1 - yh) * half, half, 1)
    arrived = lax.ppermute(other, "yh", [(0, 1), (1, 0)])

    prompt_rows = image_refs.shape[0]
    usable = image_refs >= 0
    source = jnp.where(usable, image_refs // 256, -1)
    hits = (source[:, None] == jnp.arange(32)[None, :]).astype(BF)
    before = (jnp.arange(prompt_rows)[:, None] > jnp.arange(prompt_rows)[None, :]).astype(BF)
    earlier = jnp.dot(before, hits, preferred_element_type=F32)
    arrival = jnp.sum(earlier * hits.astype(F32), axis=1).astype(jnp.int32)
    slot = jnp.where(usable, source * 16 + arrival, -1)
    pick = (slot[:, None] == jnp.arange(512)[None, :]).astype(BF)
    names = jnp.where(usable, image_refs % 256 + 1, 0).astype(BF)
    table = jnp.dot(names[None, :], pick, preferred_element_type=F32).astype(jnp.int32)
    table = jnp.broadcast_to(table.reshape(16, 1, 32), (16, 2, 32)).reshape(32, 32)
    usable = usable.astype(jnp.int32)[:, None]

    projected = project(patches, jnp.swapaxes(qkv_weight, 1, 2))
    arrived, table, pick, usable, out_weight, projected = lax.optimization_barrier(
        (arrived, table, pick, usable, out_weight, projected)
    )
    is_own = (jnp.arange(2) == yh)[:, None, None]
    both = jnp.where(is_own, own[None], arrived[None]).reshape(-1, half)
    weight = lax.all_gather(both, ("z", "x"), axis=0, tiled=True)

    out_far = lax.ppermute(out_weight, "yl", [(0, 1), (1, 0)])

    patch_ids = jnp.repeat(image_ids.reshape(-1), MERGE)
    patch_ids, both = lax.optimization_barrier((patch_ids, both))
    context = vision_context(projected, patch_ids)
    context, out_far = lax.optimization_barrier((context, out_far))
    out_blocks = [out_weight, swap_core(out_weight), out_far, swap_core(out_far)]
    rows = context.shape[0] // 4
    parts = [
        lax.dynamic_slice_in_dim(context, (tp ^ k) * rows, rows, 0) for k in range(4)
    ]
    parts = [parts[0]] + [swap_tp(parts[k], k) for k in (1, 2, 3)]
    merged, top, bottom = project_and_norm(tp, parts, out_blocks, patches, merge_gain)

    table, merged, top, bottom = lax.optimization_barrier((table, merged, top, bottom))
    near_rows = [
        (0, 0, merged),
        (1, 0, shift_y(merged, 1)),
        (-1, 0, shift_y(merged, -1)),
        (2, 0, shift_y(top, 2)),
        (2, top.shape[0], shift_y(bottom, -2)),
    ]
    table = lax.all_to_all(table, SEC, split_axis=0, concat_axis=0, tiled=True)
    blocks = []
    ids = []
    for d, offset, block in near_rows:
        blocks += [block, swap_core(block)]
        origin = (y - d + 4) % 4 * 128 + offset
        ids += [origin + c * 64 + jnp.arange(block.shape[0]) for c in (core, 1 - core)]
    row_ids = jnp.concatenate(ids)

    wanted = table.reshape(32, 2, 16) - 1
    wanted = jnp.where(wanted >= 0, wanted + jnp.arange(2)[None, :, None] * 256, -1).reshape(-1)
    send = (wanted[:, None] == row_ids[None, :]).astype(BF)

    image_rows = jnp.dot(stack_rows(blocks), weight, preferred_element_type=F32).astype(BF)
    outgoing = jnp.dot(send, image_rows, preferred_element_type=F32).astype(BF)
    received = lax.all_to_all(outgoing, SEC, split_axis=0, concat_axis=0, tiled=True)
    received = received.reshape(16, 2, 32, half)
    prompt, squares = pick_rows(received, pick, usable, text_rows)
    flat = squares.reshape(4, -1)
    total = flat + swap_tp(flat, 1) + swap_tp(flat, 2) + swap_tp(flat, 3)
    return finish(prompt, total.reshape(squares.shape), llm_gain)


def solution(mesh):
    torus = Mesh(mesh.devices.reshape(4, 4, 2, 2, 2), ("z", "x", "yh", "yl", "c"))
    return jax.shard_map(
        on_device,
        mesh=torus,
        in_specs=(
            P(SEC, None),
            P(SEC, None),
            P(None, None, TP),
            P(TP, None),
            P(),
            P(SEC, TP),
            P(SEC, TP),
            P(SEC),
            P(TP),
        ),
        out_specs=P(SEC, TP),
        check_vma=False,
    )
```

```python
import functools

import jax
import jax.numpy as jnp
from jax import lax
from jax.experimental import pallas as pl
from jax.experimental.pallas import tpu as pltpu
from jax.sharding import Mesh, PartitionSpec as P

HEAD_DIM = 80
MERGE = 4
EPSILON = 1e-06
LOG2E = 1.4426950408889634
SEC = ("z", "x", "yh")
TP = ("yl", "c")
BF = jnp.bfloat16
F32 = jnp.float32


def project_kernel(patches, weight, projected):
    projected[0] = lax.dot_general(
        patches[...], weight[0], (((1,), (1,)), ((), ())), preferred_element_type=F32
    ).astype(BF)


def project(patches, weight):
    rows, depth = patches.shape
    count, width, _ = weight.shape
    return pl.pallas_call(
        project_kernel,
        grid=(count,),
        out_shape=jax.ShapeDtypeStruct((count, rows, width), BF),
        in_specs=[
            pl.BlockSpec((rows, depth), lambda i: (0, 0), pipeline_mode=pl.Buffered(1)),
            pl.BlockSpec((1, width, depth), lambda i: (i, 0, 0)),
        ],
        out_specs=pl.BlockSpec((1, rows, width), lambda i: (i, 0, 0)),
        compiler_params=pltpu.CompilerParams(vmem_limit_bytes=14 * 2**20),
        cost_estimate=pl.CostEstimate(
            flops=2 * rows * depth * width * count,
            bytes_accessed=2 * (rows * depth + count * width * (depth + rows)),
            transcendentals=0,
        ),
        name="project_qkv",
    )(patches, weight)


def attention_kernel(row_ids, column_ids, projected, context, keys, values):
    heads = keys.shape[0]
    row_count = projected.shape[1]
    one = jnp.ones((row_count, 128 - HEAD_DIM), BF)
    for head in range(heads):
        columns = slice(head * HEAD_DIM, (head + 1) * HEAD_DIM)
        keys[head] = projected[1, :, columns]
        values[head] = jnp.concatenate([projected[2, :, columns], one], axis=1)
    scale = HEAD_DIM ** (-0.5) * LOG2E
    block = min(256, row_count)

    def one_block(index, carry):
        rows = pl.ds(pl.multiple_of(index * block, block), block)
        same_image = row_ids[rows, :] == column_ids[...]
        outs = []
        for head in range(heads):
            query = projected[0, rows, head * HEAD_DIM : (head + 1) * HEAD_DIM]
            scores = lax.dot_general(
                query, keys[head], (((1,), (1,)), ((), ())), preferred_element_type=F32
            )
            scores = jnp.where(same_image, scores, -1e30)
            highest = jnp.max(scores, axis=1, keepdims=True)
            weights = jnp.exp2((scores - highest) * scale).astype(BF)
            summed = jnp.dot(weights, values[head], preferred_element_type=F32)
            outs.append(summed[:, :HEAD_DIM] / summed[:, HEAD_DIM : HEAD_DIM + 1])
        context[rows, :] = jnp.concatenate(outs, axis=1).astype(BF)
        return carry

    lax.fori_loop(0, row_count // block, one_block, 0)


def vision_context(projected, patch_ids):
    row_count, width = projected.shape[1:]
    heads = width // HEAD_DIM
    return pl.pallas_call(
        attention_kernel,
        out_shape=jax.ShapeDtypeStruct((row_count, width), BF),
        in_specs=[pl.BlockSpec(memory_space=pltpu.VMEM)] * 3,
        out_specs=pl.BlockSpec(memory_space=pltpu.VMEM),
        scratch_shapes=[
            pltpu.VMEM((heads, row_count, HEAD_DIM), BF),
            pltpu.VMEM((heads, row_count, 128), BF),
        ],
        compiler_params=pltpu.CompilerParams(vmem_limit_bytes=20 * 2**20),
        cost_estimate=pl.CostEstimate(
            flops=4 * heads * row_count * row_count * 256,
            bytes_accessed=8 * row_count * width,
            transcendentals=heads * row_count * row_count,
        ),
        name="vision_attention",
    )(patch_ids[:, None], patch_ids[None, :], projected)


def norm_kernel(*refs):
    tp, parts, outs, (patches, gain, merged, top, bottom, normed) = (
        refs[0], refs[1:5], refs[5:9], refs[9:],
    )
    attended = patches[...].astype(F32)
    for part, weight in zip(parts, outs):
        attended += jnp.dot(part[...], weight[...], preferred_element_type=F32)
    moment = jnp.mean(attended * attended, axis=1, keepdims=True)
    scaled = attended * lax.rsqrt(moment + EPSILON) * gain[...]
    count, width = merged.shape[0], scaled.shape[1]
    for q in range(width // 128):
        normed[q] = scaled[:, q * 128 : (q + 1) * 128]
    for j in range(MERGE):
        for q in range(width // 128):
            piece = normed[q, pl.ds(j, count, stride=MERGE), :].astype(BF)
            columns = slice(j * width + q * 128, j * width + (q + 1) * 128)
            merged[:, columns] = piece
            top[:, columns] = piece[: count // 2]
            bottom[:, columns] = piece[count // 2 :]


def project_and_norm(tp, parts, outs, patches, gain):
    rows, depth = parts[0].shape
    width = patches.shape[1]
    count = rows // MERGE
    whole = lambda shape: pl.BlockSpec(shape, lambda i, t: (0, 0))
    return pl.pallas_call(
        norm_kernel,
        grid_spec=pltpu.PrefetchScalarGridSpec(
            num_scalar_prefetch=1,
            grid=(1,),
            in_specs=[whole((rows, depth))] * 4
            + [whole((depth, width))] * 4
            + [pl.BlockSpec((rows, width), lambda i, t: (t[0], 0)), whole((1, width))],
            out_specs=[
                whole((count, MERGE * width)),
                whole((count // 2, MERGE * width)),
                whole((count // 2, MERGE * width)),
            ],
            scratch_shapes=[pltpu.VMEM((width // 128, rows, 128), F32)],
        ),
        out_shape=[
            jax.ShapeDtypeStruct((count, MERGE * width), BF),
            jax.ShapeDtypeStruct((count // 2, MERGE * width), BF),
            jax.ShapeDtypeStruct((count // 2, MERGE * width), BF),
        ],
        compiler_params=pltpu.CompilerParams(vmem_limit_bytes=18 * 2**20),
        cost_estimate=pl.CostEstimate(
            flops=8 * rows * depth * width,
            bytes_accessed=8 * depth * (rows + width) + 4 * rows * width,
            transcendentals=rows,
        ),
        name="project_and_norm",
    )(tp.reshape(1).astype(jnp.int32), *parts, *outs, patches, gain[None, :])


def stack_kernel(*refs):
    first = 0
    for block in refs[:-1]:
        refs[-1][first : first + block.shape[0], :] = block[...]
        first += block.shape[0]


def stack_rows(blocks):
    count = sum(block.shape[0] for block in blocks)
    depth = blocks[0].shape[1]
    tile = depth // 4
    return pl.pallas_call(
        stack_kernel,
        grid=(depth // tile,),
        out_shape=jax.ShapeDtypeStruct((count, depth), BF),
        in_specs=[pl.BlockSpec((b.shape[0], tile), lambda i: (0, i)) for b in blocks],
        out_specs=pl.BlockSpec((count, tile), lambda i: (0, i)),
        compiler_params=pltpu.CompilerParams(vmem_limit_bytes=10 * 2**20),
        cost_estimate=pl.CostEstimate(
            flops=0, bytes_accessed=4 * count * depth, transcendentals=0
        ),
        name="stack_rows",
    )(*blocks)


def square_sums(block):
    value = block.astype(F32)
    return jnp.sum(value * value, axis=1, keepdims=True)


def diagonal():
    shape = (128, 128)
    return lax.broadcasted_iota(jnp.int32, shape, 0) == lax.broadcasted_iota(jnp.int32, shape, 1)


def to_lanes(column, out):
    eye = diagonal()
    for q in range(out.shape[0]):
        part = jnp.where(eye, column[q * 128 : (q + 1) * 128], 0.0)
        out[q : q + 1, :] = jnp.sum(part, axis=0, keepdims=True)


def to_column(lanes):
    eye = diagonal()
    return jnp.concatenate(
        [
            jnp.sum(jnp.where(eye, lanes[q : q + 1], 0.0), axis=1, keepdims=True)
            for q in range(lanes.shape[0])
        ],
        axis=0,
    )


def text_kernel(text, usable, squares):
    squares[...] = jnp.where(usable[...] > 0, 0.0, square_sums(text[...]))


def text_squares(text, usable):
    count, width = text.shape
    return pl.pallas_call(
        text_kernel,
        grid=(4,),
        out_shape=jax.ShapeDtypeStruct((count, 1), F32),
        in_specs=[
            pl.BlockSpec((count // 4, width), lambda i: (i, 0)),
            pl.BlockSpec((count // 4, 1), lambda i: (i, 0)),
        ],
        out_specs=pl.BlockSpec((count // 4, 1), lambda i: (i, 0)),
        compiler_params=pltpu.CompilerParams(vmem_limit_bytes=10 * 2**20),
        cost_estimate=pl.CostEstimate(
            flops=2 * count * width, bytes_accessed=2 * count * width, transcendentals=0
        ),
        name="text_squares",
    )(text, usable)


def squares_kernel(received, pick, from_text, squares, total):
    arrived = received[...].reshape(pick.shape[1], received.shape[-1])
    step = pl.program_id(0)

    @pl.when(step == 0)
    def _():
        total[...] = square_sums(arrived)

    @pl.when(step > 0)
    def _():
        total[...] += square_sums(arrived)

    @pl.when(step == pl.num_programs(0) - 1)
    def _():
        rest = jnp.broadcast_to(total[...], (total.shape[0], 128))
        chosen = jnp.broadcast_to(from_text[...], (pick.shape[0], 128))
        for _ in range(3):
            part = rest.astype(BF)
            chosen += jnp.dot(pick[...], part, preferred_element_type=F32)
            rest = rest - part.astype(F32)
        to_lanes(chosen[:, :1], squares)


def slot_squares(received, pick, from_text):
    planes, halves, rows, part = received.shape
    count, slots = pick.shape
    return pl.pallas_call(
        squares_kernel,
        grid=(halves,),
        out_shape=jax.ShapeDtypeStruct((count // 128, 128), F32),
        in_specs=[
            pl.BlockSpec((planes, 1, rows, part), lambda h: (0, h, 0, 0)),
            pl.BlockSpec((count, slots), lambda h: (0, 0), pipeline_mode=pl.Buffered(1)),
            pl.BlockSpec((count, 1), lambda h: (0, 0), pipeline_mode=pl.Buffered(1)),
        ],
        out_specs=pl.BlockSpec((count // 128, 128), lambda h: (0, 0)),
        scratch_shapes=[pltpu.VMEM((slots, 1), F32)],
        compiler_params=pltpu.CompilerParams(vmem_limit_bytes=14 * 2**20),
        cost_estimate=pl.CostEstimate(
            flops=2 * slots * halves * part,
            bytes_accessed=2 * slots * halves * part,
            transcendentals=0,
        ),
        name="slot_squares",
    )(received, pick, from_text)


def pick_kernel(received, pick, usable, text, prompt):
    arrived = received[...].reshape(pick.shape[1], received.shape[-1])
    picked = jnp.dot(pick[...], arrived, preferred_element_type=F32)
    prompt[...] = jnp.where(usable[...] > 0, picked, text[...].astype(F32)).astype(BF)


def pick_rows(received, pick, usable, text):
    planes, halves, rows, part = received.shape
    count, slots = pick.shape
    return pl.pallas_call(
        pick_kernel,
        grid=(halves,),
        out_shape=jax.ShapeDtypeStruct((count, halves * part), BF),
        in_specs=[
            pl.BlockSpec((planes, 1, rows, part), lambda h: (0, h, 0, 0)),
            pl.BlockSpec((count, slots), lambda h: (0, 0), pipeline_mode=pl.Buffered(1)),
            pl.BlockSpec((count, 1), lambda h: (0, 0), pipeline_mode=pl.Buffered(1)),
            pl.BlockSpec((count, part), lambda h: (0, h)),
        ],
        out_specs=pl.BlockSpec((count, part), lambda h: (0, h)),
        compiler_params=pltpu.CompilerParams(vmem_limit_bytes=14 * 2**20),
        cost_estimate=pl.CostEstimate(
            flops=2 * count * slots * halves * part,
            bytes_accessed=6 * count * halves * part,
            transcendentals=0,
        ),
        name="pick_rows",
    )(received, pick, usable, text)


def finish_kernel(prompt, own, core, far, both, gain, out, inverse, *, width):
    @pl.when(pl.program_id(0) == 0)
    def _():
        total = to_column(own[...] + core[...] + far[...] + both[...])
        inverse[...] = lax.rsqrt(total / width + EPSILON)

    out[...] = (prompt[...].astype(F32) * inverse[...] * gain[...]).astype(BF)


def finish(prompt, squares, gain):
    count, width = prompt.shape
    part = width // 4
    small = pl.BlockSpec((count // 128, 128), lambda h: (0, 0))
    return pl.pallas_call(
        functools.partial(finish_kernel, width=4 * width),
        grid=(4,),
        out_shape=jax.ShapeDtypeStruct((count, width), BF),
        in_specs=[pl.BlockSpec((count, part), lambda h: (0, h))]
        + [small] * 4
        + [pl.BlockSpec((1, part), lambda h: (0, h))],
        out_specs=pl.BlockSpec((count, part), lambda h: (0, h)),
        scratch_shapes=[pltpu.VMEM((count, 1), F32)],
        compiler_params=pltpu.CompilerParams(vmem_limit_bytes=10 * 2**20),
        cost_estimate=pl.CostEstimate(
            flops=3 * count * width, bytes_accessed=4 * count * width, transcendentals=count
        ),
        name="finish",
    )(prompt, *squares, gain[None, :])


def swap_tp(block, k):
    return lax.ppermute(block, TP, [(i, i ^ k) for i in range(4)])


def shift_y(block, d):
    return lax.ppermute(block, ("yh", "yl"), [(i, (i + d) % 4) for i in range(4)])


def swap_core(block):
    return lax.ppermute(block, "c", [(0, 1), (1, 0)])


def on_device(
    patches,
    image_ids,
    qkv_weight,
    out_weight,
    merge_gain,
    merge_weight,
    text_rows,
    image_refs,
    llm_gain,
):
    yh = lax.axis_index("yh")
    tp = lax.axis_index(TP)
    y = lax.axis_index(("yh", "yl"))
    core = lax.axis_index("c")

    half = merge_weight.shape[1] // 2
    own = lax.dynamic_slice_in_dim(merge_weight, yh * half, half, 1)
    other = lax.dynamic_slice_in_dim(merge_weight, (1 - yh) * half, half, 1)
    arrived = lax.ppermute(other, "yh", [(0, 1), (1, 0)])

    prompt_rows = image_refs.shape[0]
    usable = image_refs >= 0
    source = jnp.where(usable, image_refs // 256, -1)
    hits = (source[:, None] == jnp.arange(32)[None, :]).astype(BF)
    before = (jnp.arange(prompt_rows)[:, None] > jnp.arange(prompt_rows)[None, :]).astype(BF)
    earlier = jnp.dot(before, hits, preferred_element_type=F32)
    arrival = jnp.sum(earlier * hits.astype(F32), axis=1).astype(jnp.int32)
    slot = jnp.where(usable, source * 16 + arrival, -1)
    pick = (slot[:, None] == jnp.arange(512)[None, :]).astype(BF)
    names = jnp.where(usable, image_refs % 256 + 1, 0).astype(BF)
    table = jnp.dot(names[None, :], pick, preferred_element_type=F32).astype(jnp.int32)
    table = jnp.broadcast_to(table.reshape(16, 1, 32), (16, 2, 32)).reshape(32, 32)
    usable = usable.astype(jnp.int32)[:, None]

    arrived, table, pick, usable, out_weight = lax.optimization_barrier(
        (arrived, table, pick, usable, out_weight)
    )
    is_own = (jnp.arange(2) == yh)[:, None, None]
    both = jnp.where(is_own, own[None], arrived[None]).reshape(-1, half)
    weight = lax.all_gather(both, ("z", "x"), axis=0, tiled=True)

    out_far = lax.ppermute(out_weight, "yl", [(0, 1), (1, 0)])

    patch_ids = jnp.repeat(image_ids.reshape(-1), MERGE)
    patch_ids, patches, both = lax.optimization_barrier((patch_ids, patches, both))
    projected = project(patches, jnp.swapaxes(qkv_weight, 1, 2))
    context = vision_context(projected, patch_ids)
    rows = context.shape[0] // 4
    parts = [
        lax.dynamic_slice_in_dim(context, (tp ^ k) * rows, rows, 0) for k in range(4)
    ]
    parts = [parts[0]] + [swap_tp(parts[k], k) for k in (1, 2, 3)]
    parts[2], out_far = lax.optimization_barrier((parts[2], out_far))
    out_blocks = [out_weight, swap_core(out_weight), out_far, swap_core(out_far)]
    merged, top, bottom = project_and_norm(tp, parts, out_blocks, patches, merge_gain)

    table, merged, top, bottom = lax.optimization_barrier((table, merged, top, bottom))
    after, before = shift_y(merged, 1), shift_y(merged, -1)
    far = [shift_y(top, 2), shift_y(bottom, -2)]
    table = lax.all_to_all(table, SEC, split_axis=0, concat_axis=0, tiled=True)
    after, before, table = lax.optimization_barrier((after, before, table))
    near_rows = [
        (0, 0, merged),
        (1, 0, after),
        (-1, 0, before),
        (2, 0, far[0]),
        (2, top.shape[0], far[1]),
    ]
    blocks = []
    ids = []
    for d, offset, block in near_rows:
        blocks += [block, swap_core(block)]
        origin = (y - d + 4) % 4 * 128 + offset
        ids += [origin + c * 64 + jnp.arange(block.shape[0]) for c in (core, 1 - core)]
    row_ids = jnp.concatenate(ids)

    wanted = table.reshape(32, 2, 16) - 1
    wanted = jnp.where(wanted >= 0, wanted + jnp.arange(2)[None, :, None] * 256, -1).reshape(-1)
    send = (wanted[:, None] == row_ids[None, :]).astype(BF)

    image_rows = jnp.dot(stack_rows(blocks), weight, preferred_element_type=F32).astype(BF)
    image_rows, send = lax.optimization_barrier((image_rows, send))
    outgoing = jnp.dot(send, image_rows, preferred_element_type=F32).astype(BF)
    received = lax.all_to_all(outgoing, SEC, split_axis=0, concat_axis=0, tiled=True)
    received = received.reshape(16, 2, 32, half)
    squares = slot_squares(received, pick, text_squares(text_rows, usable))
    squares = [squares] + [swap_tp(squares, k) for k in (1, 2, 3)]
    return finish(pick_rows(received, pick, usable, text_rows), squares, llm_gain)


def solution(mesh):
    torus = Mesh(mesh.devices.reshape(4, 4, 2, 2, 2), ("z", "x", "yh", "yl", "c"))
    return jax.shard_map(
        on_device,
        mesh=torus,
        in_specs=(
            P(SEC, None),
            P(SEC, None),
            P(None, None, TP),
            P(TP, None),
            P(),
            P(SEC, TP),
            P(SEC, TP),
            P(SEC),
            P(TP),
        ),
        out_specs=P(SEC, TP),
        check_vma=False,
    )
```

```python
import functools

import jax
import jax.numpy as jnp
from jax import lax
from jax.experimental import pallas as pl
from jax.experimental.pallas import tpu as pltpu
from jax.sharding import Mesh, PartitionSpec as P

HEAD_DIM = 80
MERGE = 4
EPSILON = 1e-06
LOG2E = 1.4426950408889634
SEC = ("z", "x", "yh")
TP = ("yl", "c")
BF = jnp.bfloat16
F32 = jnp.float32


def project_kernel(patches, weight, projected):
    projected[0] = lax.dot_general(
        patches[...], weight[0], (((1,), (1,)), ((), ())), preferred_element_type=F32
    ).astype(BF)


def project(patches, weight):
    rows, depth = patches.shape
    count, width, _ = weight.shape
    return pl.pallas_call(
        project_kernel,
        grid=(count,),
        out_shape=jax.ShapeDtypeStruct((count, rows, width), BF),
        in_specs=[
            pl.BlockSpec((rows, depth), lambda i: (0, 0), pipeline_mode=pl.Buffered(1)),
            pl.BlockSpec((1, width, depth), lambda i: (i, 0, 0)),
        ],
        out_specs=pl.BlockSpec((1, rows, width), lambda i: (i, 0, 0)),
        compiler_params=pltpu.CompilerParams(vmem_limit_bytes=14 * 2**20),
        cost_estimate=pl.CostEstimate(
            flops=2 * rows * depth * width * count,
            bytes_accessed=2 * (rows * depth + count * width * (depth + rows)),
            transcendentals=0,
        ),
        name="project_qkv",
    )(patches, weight)


def attention_kernel(row_ids, column_ids, projected, context, keys, values):
    heads = keys.shape[0]
    row_count = projected.shape[1]
    one = jnp.ones((row_count, 128 - HEAD_DIM), BF)
    for head in range(heads):
        columns = slice(head * HEAD_DIM, (head + 1) * HEAD_DIM)
        keys[head] = projected[1, :, columns]
        values[head] = jnp.concatenate([projected[2, :, columns], one], axis=1)
    scale = HEAD_DIM ** (-0.5) * LOG2E
    block = min(256, row_count)

    def one_block(index, carry):
        rows = pl.ds(pl.multiple_of(index * block, block), block)
        same_image = row_ids[rows, :] == column_ids[...]
        outs = []
        for head in range(heads):
            query = projected[0, rows, head * HEAD_DIM : (head + 1) * HEAD_DIM]
            scores = lax.dot_general(
                query, keys[head], (((1,), (1,)), ((), ())), preferred_element_type=F32
            )
            scores = jnp.where(same_image, scores, -1e30)
            highest = jnp.max(scores, axis=1, keepdims=True)
            weights = jnp.exp2((scores - highest) * scale).astype(BF)
            summed = jnp.dot(weights, values[head], preferred_element_type=F32)
            outs.append(summed[:, :HEAD_DIM] / summed[:, HEAD_DIM : HEAD_DIM + 1])
        context[rows, :] = jnp.concatenate(outs, axis=1).astype(BF)
        return carry

    lax.fori_loop(0, row_count // block, one_block, 0)


def vision_context(projected, patch_ids):
    row_count, width = projected.shape[1:]
    heads = width // HEAD_DIM
    return pl.pallas_call(
        attention_kernel,
        out_shape=jax.ShapeDtypeStruct((row_count, width), BF),
        in_specs=[pl.BlockSpec(memory_space=pltpu.VMEM)] * 3,
        out_specs=pl.BlockSpec(memory_space=pltpu.VMEM),
        scratch_shapes=[
            pltpu.VMEM((heads, row_count, HEAD_DIM), BF),
            pltpu.VMEM((heads, row_count, 128), BF),
        ],
        compiler_params=pltpu.CompilerParams(vmem_limit_bytes=20 * 2**20),
        cost_estimate=pl.CostEstimate(
            flops=4 * heads * row_count * row_count * 256,
            bytes_accessed=8 * row_count * width,
            transcendentals=heads * row_count * row_count,
        ),
        name="vision_attention",
    )(patch_ids[:, None], patch_ids[None, :], projected)


def norm_kernel(*refs):
    parts, outs, (patches, gain, merged, normed) = refs[1:5], refs[5:11], refs[11:]
    outs = [outs[0][...], outs[1][...]] + [
        jnp.concatenate([outs[k][...], outs[k + 1][...]], axis=0) for k in (2, 4)
    ]
    attended = patches[...].astype(F32)
    for part, weight in zip(parts, outs):
        attended += jnp.dot(part[...], weight, preferred_element_type=F32)
    moment = jnp.mean(attended * attended, axis=1, keepdims=True)
    scaled = attended * lax.rsqrt(moment + EPSILON) * gain[...]
    count, width = merged.shape[0], scaled.shape[1]
    for q in range(width // 128):
        normed[q] = scaled[:, q * 128 : (q + 1) * 128]
    for j in range(MERGE):
        for q in range(width // 128):
            piece = normed[q, pl.ds(j, count, stride=MERGE), :].astype(BF)
            columns = slice(j * width + q * 128, j * width + (q + 1) * 128)
            merged[:, columns] = piece


def project_and_norm(tp, parts, outs, patches, gain):
    rows, depth = parts[0].shape
    width = patches.shape[1]
    count = rows // MERGE
    whole = lambda shape: pl.BlockSpec(shape, lambda i, t: (0, 0))
    return pl.pallas_call(
        norm_kernel,
        grid_spec=pltpu.PrefetchScalarGridSpec(
            num_scalar_prefetch=1,
            grid=(1,),
            in_specs=[whole((rows, depth))] * 4
            + [whole(out.shape) for out in outs]
            + [pl.BlockSpec((rows, width), lambda i, t: (t[0], 0)), whole((1, width))],
            out_specs=whole((count, MERGE * width)),
            scratch_shapes=[pltpu.VMEM((width // 128, rows, 128), F32)],
        ),
        out_shape=jax.ShapeDtypeStruct((count, MERGE * width), BF),
        compiler_params=pltpu.CompilerParams(vmem_limit_bytes=18 * 2**20),
        cost_estimate=pl.CostEstimate(
            flops=8 * rows * depth * width,
            bytes_accessed=8 * depth * (rows + width) + 4 * rows * width,
            transcendentals=rows,
        ),
        name="project_and_norm",
    )(tp.reshape(1).astype(jnp.int32), *parts, *outs, patches, gain[None, :])


def stack_kernel(*refs):
    first = 0
    for block in refs[:-1]:
        refs[-1][first : first + block.shape[0], :] = block[...]
        first += block.shape[0]


def stack_rows(blocks):
    count = sum(block.shape[0] for block in blocks)
    depth = blocks[0].shape[1]
    tile = depth // 4
    return pl.pallas_call(
        stack_kernel,
        grid=(depth // tile,),
        out_shape=pltpu.HBM((count, depth), BF),
        in_specs=[pl.BlockSpec((b.shape[0], tile), lambda i: (0, i)) for b in blocks],
        out_specs=pl.BlockSpec((count, tile), lambda i: (0, i)),
        compiler_params=pltpu.CompilerParams(vmem_limit_bytes=10 * 2**20),
        cost_estimate=pl.CostEstimate(
            flops=0, bytes_accessed=4 * count * depth, transcendentals=0
        ),
        name="stack_rows",
    )(*blocks)


def square_sums(block):
    value = block.astype(F32)
    return jnp.sum(value * value, axis=1, keepdims=True)


def diagonal():
    shape = (128, 128)
    return lax.broadcasted_iota(jnp.int32, shape, 0) == lax.broadcasted_iota(jnp.int32, shape, 1)


def to_lanes(column, out):
    eye = diagonal()
    for q in range(out.shape[0]):
        part = jnp.where(eye, column[q * 128 : (q + 1) * 128], 0.0)
        out[q : q + 1, :] = jnp.sum(part, axis=0, keepdims=True)


def to_column(lanes):
    eye = diagonal()
    return jnp.concatenate(
        [
            jnp.sum(jnp.where(eye, lanes[q : q + 1], 0.0), axis=1, keepdims=True)
            for q in range(lanes.shape[0])
        ],
        axis=0,
    )


def text_kernel(text, usable, squares):
    squares[...] = jnp.where(usable[...] > 0, 0.0, square_sums(text[...]))


def text_squares(text, usable):
    count, width = text.shape
    return pl.pallas_call(
        text_kernel,
        grid=(4,),
        out_shape=jax.ShapeDtypeStruct((count, 1), F32),
        in_specs=[
            pl.BlockSpec((count // 4, width), lambda i: (i, 0)),
            pl.BlockSpec((count // 4, 1), lambda i: (i, 0)),
        ],
        out_specs=pl.BlockSpec((count // 4, 1), lambda i: (i, 0)),
        compiler_params=pltpu.CompilerParams(vmem_limit_bytes=10 * 2**20),
        cost_estimate=pl.CostEstimate(
            flops=2 * count * width, bytes_accessed=2 * count * width, transcendentals=0
        ),
        name="text_squares",
    )(text, usable)


def squares_kernel(received, pick, from_text, squares, total):
    arrived = received[...].reshape(pick.shape[1], received.shape[-1])
    step = pl.program_id(0)

    @pl.when(step == 0)
    def _():
        total[...] = square_sums(arrived)

    @pl.when(step > 0)
    def _():
        total[...] += square_sums(arrived)

    @pl.when(step == pl.num_programs(0) - 1)
    def _():
        rest = jnp.broadcast_to(total[...], (total.shape[0], 128))
        chosen = jnp.broadcast_to(from_text[...], (pick.shape[0], 128))
        for _ in range(3):
            part = rest.astype(BF)
            chosen += jnp.dot(pick[...], part, preferred_element_type=F32)
            rest = rest - part.astype(F32)
        to_lanes(chosen[:, :1], squares)


def slot_squares(received, pick, from_text):
    planes, halves, rows, part = received.shape
    count, slots = pick.shape
    return pl.pallas_call(
        squares_kernel,
        grid=(halves,),
        out_shape=jax.ShapeDtypeStruct((count // 128, 128), F32),
        in_specs=[
            pl.BlockSpec((planes, 1, rows, part), lambda h: (0, h, 0, 0)),
            pl.BlockSpec((count, slots), lambda h: (0, 0), pipeline_mode=pl.Buffered(1)),
            pl.BlockSpec((count, 1), lambda h: (0, 0), pipeline_mode=pl.Buffered(1)),
        ],
        out_specs=pl.BlockSpec((count // 128, 128), lambda h: (0, 0)),
        scratch_shapes=[pltpu.VMEM((slots, 1), F32)],
        compiler_params=pltpu.CompilerParams(vmem_limit_bytes=14 * 2**20),
        cost_estimate=pl.CostEstimate(
            flops=2 * slots * halves * part,
            bytes_accessed=2 * slots * halves * part,
            transcendentals=0,
        ),
        name="slot_squares",
    )(received, pick, from_text)


def pick_kernel(received, pick, usable, text, prompt):
    arrived = received[...].reshape(pick.shape[1], received.shape[-1])
    picked = jnp.dot(pick[...], arrived, preferred_element_type=F32)
    prompt[...] = jnp.where(usable[...] > 0, picked, text[...].astype(F32)).astype(BF)


def pick_rows(received, pick, usable, text):
    planes, halves, rows, part = received.shape
    count, slots = pick.shape
    return pl.pallas_call(
        pick_kernel,
        grid=(halves,),
        out_shape=jax.ShapeDtypeStruct((count, halves * part), BF),
        in_specs=[
            pl.BlockSpec((planes, 1, rows, part), lambda h: (0, h, 0, 0)),
            pl.BlockSpec((count, slots), lambda h: (0, 0), pipeline_mode=pl.Buffered(1)),
            pl.BlockSpec((count, 1), lambda h: (0, 0), pipeline_mode=pl.Buffered(1)),
            pl.BlockSpec((count, part), lambda h: (0, h)),
        ],
        out_specs=pl.BlockSpec((count, part), lambda h: (0, h)),
        compiler_params=pltpu.CompilerParams(vmem_limit_bytes=14 * 2**20),
        cost_estimate=pl.CostEstimate(
            flops=2 * count * slots * halves * part,
            bytes_accessed=6 * count * halves * part,
            transcendentals=0,
        ),
        name="pick_rows",
    )(received, pick, usable, text)


def finish_kernel(prompt, own, core, far, both, gain, out, inverse, *, width):
    @pl.when(pl.program_id(0) == 0)
    def _():
        total = to_column(own[...] + core[...] + far[...] + both[...])
        inverse[...] = lax.rsqrt(total / width + EPSILON)

    out[...] = (prompt[...].astype(F32) * inverse[...] * gain[...]).astype(BF)


def finish(prompt, squares, gain):
    count, width = prompt.shape
    part = width // 4
    small = pl.BlockSpec((count // 128, 128), lambda h: (0, 0))
    return pl.pallas_call(
        functools.partial(finish_kernel, width=4 * width),
        grid=(4,),
        out_shape=jax.ShapeDtypeStruct((count, width), BF),
        in_specs=[pl.BlockSpec((count, part), lambda h: (0, h))]
        + [small] * 4
        + [pl.BlockSpec((1, part), lambda h: (0, h))],
        out_specs=pl.BlockSpec((count, part), lambda h: (0, h)),
        scratch_shapes=[pltpu.VMEM((count, 1), F32)],
        compiler_params=pltpu.CompilerParams(vmem_limit_bytes=10 * 2**20),
        cost_estimate=pl.CostEstimate(
            flops=3 * count * width, bytes_accessed=4 * count * width, transcendentals=count
        ),
        name="finish",
    )(prompt, *squares, gain[None, :])


def swap_tp(block, k):
    return lax.ppermute(block, TP, [(i, i ^ k) for i in range(4)])


def shift_y(block, d):
    return lax.ppermute(block, ("yh", "yl"), [(i, (i + d) % 4) for i in range(4)])


def swap_core(block):
    return lax.ppermute(block, "c", [(0, 1), (1, 0)])


def on_device(
    patches,
    image_ids,
    qkv_weight,
    out_weight,
    merge_gain,
    merge_weight,
    text_rows,
    image_refs,
    llm_gain,
):
    yh = lax.axis_index("yh")
    tp = lax.axis_index(TP)
    y = lax.axis_index(("yh", "yl"))
    core = lax.axis_index("c")

    half = merge_weight.shape[1] // 2
    own = lax.dynamic_slice_in_dim(merge_weight, yh * half, half, 1)
    other = lax.dynamic_slice_in_dim(merge_weight, (1 - yh) * half, half, 1)
    arrived = lax.ppermute(other, "yh", [(0, 1), (1, 0)])

    prompt_rows = image_refs.shape[0]
    usable = image_refs >= 0
    source = jnp.where(usable, image_refs // 256, -1)
    hits = (source[:, None] == jnp.arange(32)[None, :]).astype(BF)
    before = (jnp.arange(prompt_rows)[:, None] > jnp.arange(prompt_rows)[None, :]).astype(BF)
    earlier = jnp.dot(before, hits, preferred_element_type=F32)
    arrival = jnp.sum(earlier * hits.astype(F32), axis=1).astype(jnp.int32)
    slot = jnp.where(usable, source * 16 + arrival, -1)
    pick = (slot[:, None] == jnp.arange(512)[None, :]).astype(BF)
    names = jnp.where(usable, image_refs % 256 + 1, 0).astype(BF)
    table = jnp.dot(names[None, :], pick, preferred_element_type=F32).astype(jnp.int32)
    table = jnp.broadcast_to(table.reshape(16, 1, 32), (16, 2, 32)).reshape(32, 32)
    usable = usable.astype(jnp.int32)[:, None]

    arrived, table, pick, usable, out_weight = lax.optimization_barrier(
        (arrived, table, pick, usable, out_weight)
    )
    is_own = (jnp.arange(2) == yh)[:, None, None]
    both = jnp.where(is_own, own[None], arrived[None]).reshape(-1, half)
    weight = lax.all_gather(both, ("z", "x"), axis=0, tiled=True)

    middle = out_weight.shape[0] // 2
    out_far = [shift_y(out_weight[:middle], 1), shift_y(out_weight[middle:], -1)]

    patch_ids = jnp.repeat(image_ids.reshape(-1), MERGE)
    patch_ids, patches, both = lax.optimization_barrier((patch_ids, patches, both))
    projected = project(patches, jnp.swapaxes(qkv_weight, 1, 2))
    context = vision_context(projected, patch_ids)
    context, *out_far = lax.optimization_barrier((context, *out_far))
    rows = context.shape[0] // 4
    parts = [
        lax.dynamic_slice_in_dim(context, (tp ^ k) * rows, rows, 0) for k in range(4)
    ]
    parts = [parts[0]] + [swap_tp(parts[k], k) for k in (1, 2, 3)]
    out_blocks = [out_weight, swap_core(out_weight)] + out_far + [swap_core(b) for b in out_far]
    merged = project_and_norm(tp, parts, out_blocks, patches, merge_gain)

    table, merged = lax.optimization_barrier((table, merged))
    after, before = shift_y(merged, 1), shift_y(merged, -1)
    count = merged.shape[0] // 2
    far = [shift_y(after[:count], 1), shift_y(before[count:], -1)]
    table = lax.all_to_all(table, SEC, split_axis=0, concat_axis=0, tiled=True)
    after, before, table = lax.optimization_barrier((after, before, table))
    near_rows = [
        (0, 0, merged),
        (1, 0, after),
        (-1, 0, before),
        (2, 0, far[0]),
        (2, count, far[1]),
    ]
    blocks = []
    ids = []
    for d, offset, block in near_rows:
        blocks += [block, swap_core(block)]
        origin = (y - d + 4) % 4 * 128 + offset
        ids += [origin + c * 64 + jnp.arange(block.shape[0]) for c in (core, 1 - core)]
    row_ids = jnp.concatenate(ids)

    wanted = table.reshape(32, 2, 16) - 1
    wanted = jnp.where(wanted >= 0, wanted + jnp.arange(2)[None, :, None] * 256, -1).reshape(-1)
    send = (wanted[:, None] == row_ids[None, :]).astype(BF)

    image_rows = jnp.dot(stack_rows(blocks), weight, preferred_element_type=F32).astype(BF)
    image_rows, send = lax.optimization_barrier((image_rows, send))
    outgoing = jnp.dot(send, image_rows, preferred_element_type=F32).astype(BF)
    received = lax.all_to_all(outgoing, SEC, split_axis=0, concat_axis=0, tiled=True)
    received = received.reshape(16, 2, 32, half)
    squares = slot_squares(received, pick, text_squares(text_rows, usable))
    squares = [squares] + [swap_tp(squares, k) for k in (1, 2, 3)]
    return finish(pick_rows(received, pick, usable, text_rows), squares, llm_gain)


def solution(mesh):
    torus = Mesh(mesh.devices.reshape(4, 4, 2, 2, 2), ("z", "x", "yh", "yl", "c"))
    return jax.shard_map(
        on_device,
        mesh=torus,
        in_specs=(
            P(SEC, None),
            P(SEC, None),
            P(None, None, TP),
            P(TP, None),
            P(),
            P(SEC, TP),
            P(SEC, TP),
            P(SEC),
            P(TP),
        ),
        out_specs=P(SEC, TP),
        check_vma=False,
    )
```

```python
import functools

import jax
import jax.numpy as jnp
from jax import lax
from jax.experimental import pallas as pl
from jax.experimental.pallas import tpu as pltpu
from jax.sharding import Mesh, PartitionSpec as P

HEAD_DIM = 80
MERGE = 4
EPSILON = 1e-06
LOG2E = 1.4426950408889634
SEC = ("z", "x", "yh")
TP = ("yl", "c")
BF = jnp.bfloat16
F32 = jnp.float32


def attention_kernel(row_ids, column_ids, patches, weight, context, queries, keys, values):
    heads = keys.shape[0]
    row_count = patches.shape[0]
    block = min(256, row_count)
    one = jnp.ones((block, 128 - HEAD_DIM), BF)

    def project(index, carry):
        rows = pl.ds(pl.multiple_of(index * block, block), block)
        query, key, value = (
            lax.dot_general(
                patches[rows, :], weight[c], (((1,), (1,)), ((), ())), preferred_element_type=F32
            ).astype(BF)
            for c in range(3)
        )
        for head in range(heads):
            columns = slice(head * HEAD_DIM, (head + 1) * HEAD_DIM)
            queries[head, rows, :] = query[:, columns]
            keys[head, rows, :] = key[:, columns]
            values[head, rows, :] = jnp.concatenate([value[:, columns], one], axis=1)
        return carry

    lax.fori_loop(0, row_count // block, project, 0)
    scale = HEAD_DIM ** (-0.5) * LOG2E

    def one_block(index, carry):
        rows = pl.ds(pl.multiple_of(index * block, block), block)
        same_image = row_ids[rows, :] == column_ids[...]
        outs = []
        for head in range(heads):
            scores = lax.dot_general(
                queries[head, rows, :],
                keys[head],
                (((1,), (1,)), ((), ())),
                preferred_element_type=F32,
            )
            scores = jnp.where(same_image, scores, -1e30)
            highest = jnp.max(scores, axis=1, keepdims=True)
            weights = jnp.exp2((scores - highest) * scale).astype(BF)
            summed = jnp.dot(weights, values[head], preferred_element_type=F32)
            outs.append(summed[:, :HEAD_DIM] / summed[:, HEAD_DIM : HEAD_DIM + 1])
        context[rows, :] = jnp.concatenate(outs, axis=1).astype(BF)
        return carry

    lax.fori_loop(0, row_count // block, one_block, 0)


def vision_context(patches, weight, patch_ids):
    row_count, depth = patches.shape
    width = weight.shape[1]
    heads = width // HEAD_DIM
    return pl.pallas_call(
        attention_kernel,
        out_shape=jax.ShapeDtypeStruct((row_count, width), BF),
        in_specs=[pl.BlockSpec(memory_space=pltpu.VMEM)] * 4,
        out_specs=pl.BlockSpec(memory_space=pltpu.VMEM),
        scratch_shapes=[
            pltpu.VMEM((heads, row_count, HEAD_DIM), BF),
            pltpu.VMEM((heads, row_count, HEAD_DIM), BF),
            pltpu.VMEM((heads, row_count, 128), BF),
        ],
        compiler_params=pltpu.CompilerParams(vmem_limit_bytes=20 * 2**20),
        cost_estimate=pl.CostEstimate(
            flops=4 * heads * row_count * row_count * 256 + 6 * row_count * depth * width,
            bytes_accessed=2 * (row_count + 3 * width) * depth,
            transcendentals=heads * row_count * row_count,
        ),
        name="vision_attention",
    )(patch_ids[:, None], patch_ids[None, :], patches, weight)


def norm_kernel(*refs):
    parts, outs, (patches, gain, merged, normed) = refs[1:5], refs[5:11], refs[11:]
    outs = [outs[0][...], outs[1][...]] + [
        jnp.concatenate([outs[k][...], outs[k + 1][...]], axis=0) for k in (2, 4)
    ]
    attended = patches[...].astype(F32)
    for part, weight in zip(parts, outs):
        attended += jnp.dot(part[...], weight, preferred_element_type=F32)
    moment = jnp.mean(attended * attended, axis=1, keepdims=True)
    scaled = attended * lax.rsqrt(moment + EPSILON) * gain[...]
    count, width = merged.shape[0], scaled.shape[1]
    for q in range(width // 128):
        normed[q] = scaled[:, q * 128 : (q + 1) * 128]
    for j in range(MERGE):
        for q in range(width // 128):
            piece = normed[q, pl.ds(j, count, stride=MERGE), :].astype(BF)
            columns = slice(j * width + q * 128, j * width + (q + 1) * 128)
            merged[:, columns] = piece


def project_and_norm(tp, parts, outs, patches, gain):
    rows, depth = parts[0].shape
    width = patches.shape[1]
    count = rows // MERGE
    whole = lambda shape: pl.BlockSpec(shape, lambda i, t: (0, 0))
    return pl.pallas_call(
        norm_kernel,
        grid_spec=pltpu.PrefetchScalarGridSpec(
            num_scalar_prefetch=1,
            grid=(1,),
            in_specs=[whole((rows, depth))] * 4
            + [whole(out.shape) for out in outs]
            + [pl.BlockSpec((rows, width), lambda i, t: (t[0], 0)), whole((1, width))],
            out_specs=whole((count, MERGE * width)),
            scratch_shapes=[pltpu.VMEM((width // 128, rows, 128), F32)],
        ),
        out_shape=jax.ShapeDtypeStruct((count, MERGE * width), BF),
        compiler_params=pltpu.CompilerParams(vmem_limit_bytes=18 * 2**20),
        cost_estimate=pl.CostEstimate(
            flops=8 * rows * depth * width,
            bytes_accessed=8 * depth * (rows + width) + 4 * rows * width,
            transcendentals=rows,
        ),
        name="project_and_norm",
    )(tp.reshape(1).astype(jnp.int32), *parts, *outs, patches, gain[None, :])


def stack_kernel(*refs):
    first = 0
    for block in refs[:-1]:
        refs[-1][first : first + block.shape[0], :] = block[...]
        first += block.shape[0]


def stack_rows(blocks):
    count = sum(block.shape[0] for block in blocks)
    depth = blocks[0].shape[1]
    tile = depth // 4
    return pl.pallas_call(
        stack_kernel,
        grid=(depth // tile,),
        out_shape=jax.ShapeDtypeStruct((count, depth), BF),
        in_specs=[pl.BlockSpec((b.shape[0], tile), lambda i: (0, i)) for b in blocks],
        out_specs=pl.BlockSpec((count, tile), lambda i: (0, i)),
        compiler_params=pltpu.CompilerParams(vmem_limit_bytes=10 * 2**20),
        cost_estimate=pl.CostEstimate(
            flops=0, bytes_accessed=4 * count * depth, transcendentals=0
        ),
        name="stack_rows",
    )(*blocks)


def merge_kernel(rows, weight, send, outgoing, held, sems, *, first):
    depth, columns = held.shape
    steps = sems.shape[0]
    tile = depth // steps
    copies = [
        pltpu.make_async_copy(
            weight.at[pl.ds(k * tile, tile), pl.ds(first, columns)],
            held.at[pl.ds(k * tile, tile)],
            sems.at[k],
        )
        for k in range(steps)
    ]
    for copy in copies:
        copy.start()
    total = jnp.zeros((rows.shape[0], columns), F32)
    for k, copy in enumerate(copies):
        copy.wait()
        part = slice(k * tile, (k + 1) * tile)
        total += jnp.dot(rows[:, part], held[part, :], preferred_element_type=F32)
    outgoing[...] = jnp.dot(
        send[...], total.astype(BF), preferred_element_type=F32
    ).astype(BF)


def merge_and_select(rows, weight, send, first, columns):
    slots, count = send.shape
    depth = weight.shape[0]
    vmem = pl.BlockSpec(memory_space=pltpu.VMEM)
    return pl.pallas_call(
        functools.partial(merge_kernel, first=first),
        out_shape=jax.ShapeDtypeStruct((slots, columns), BF),
        in_specs=[vmem, pl.BlockSpec(memory_space=pltpu.HBM), vmem],
        out_specs=vmem,
        scratch_shapes=[pltpu.VMEM((depth, columns), BF), pltpu.SemaphoreType.DMA((4,))],
        compiler_params=pltpu.CompilerParams(vmem_limit_bytes=24 * 2**20),
        cost_estimate=pl.CostEstimate(
            flops=2 * count * (depth + slots) * columns,
            bytes_accessed=2 * (count * depth + depth * columns + slots * columns),
            transcendentals=0,
        ),
        name="merge_rows",
    )(rows, weight, send)


def square_sums(block):
    value = block.astype(F32)
    return jnp.sum(value * value, axis=1, keepdims=True)


def diagonal():
    shape = (128, 128)
    return lax.broadcasted_iota(jnp.int32, shape, 0) == lax.broadcasted_iota(jnp.int32, shape, 1)


def to_lanes(column, out):
    eye = diagonal()
    for q in range(out.shape[0]):
        part = jnp.where(eye, column[q * 128 : (q + 1) * 128], 0.0)
        out[q : q + 1, :] = jnp.sum(part, axis=0, keepdims=True)


def to_column(lanes):
    eye = diagonal()
    return jnp.concatenate(
        [
            jnp.sum(jnp.where(eye, lanes[q : q + 1], 0.0), axis=1, keepdims=True)
            for q in range(lanes.shape[0])
        ],
        axis=0,
    )


def text_kernel(text, usable, squares):
    total = jnp.where(usable[...] > 0, 0.0, square_sums(text[...]))
    to_lanes(total, squares.at[pl.ds(pl.program_id(0), 1)])


def text_squares(text, usable):
    count, width = text.shape
    return pl.pallas_call(
        text_kernel,
        grid=(count // 128,),
        out_shape=jax.ShapeDtypeStruct((count // 128, 128), F32),
        in_specs=[
            pl.BlockSpec((128, width), lambda i: (i, 0)),
            pl.BlockSpec((128, 1), lambda i: (i, 0)),
        ],
        out_specs=pl.BlockSpec((count // 128, 128), lambda i: (0, 0)),
        compiler_params=pltpu.CompilerParams(vmem_limit_bytes=10 * 2**20),
        cost_estimate=pl.CostEstimate(
            flops=2 * count * width, bytes_accessed=2 * count * width, transcendentals=0
        ),
        name="text_squares",
    )(text, usable)


def squares_kernel(received, pick, base, squares, total):
    arrived = received[...].reshape(pick.shape[1], received.shape[-1])
    step = pl.program_id(0)

    @pl.when(step == 0)
    def _():
        total[...] = square_sums(arrived)

    @pl.when(step > 0)
    def _():
        total[...] += square_sums(arrived)

    @pl.when(step == pl.num_programs(0) - 1)
    def _():
        rest = jnp.broadcast_to(total[...], (total.shape[0], 128))
        chosen = jnp.zeros((pick.shape[0], 128), F32)
        for _ in range(3):
            part = rest.astype(BF)
            chosen += jnp.dot(pick[...], part, preferred_element_type=F32)
            rest = rest - part.astype(F32)
        to_lanes(chosen[:, :1], squares)
        squares[...] += base[...]


def slot_squares(received, pick, base):
    planes, halves, rows, part = received.shape
    count, slots = pick.shape
    return pl.pallas_call(
        squares_kernel,
        grid=(halves,),
        out_shape=jax.ShapeDtypeStruct((count // 128, 128), F32),
        in_specs=[
            pl.BlockSpec((planes, 1, rows, part), lambda h: (0, h, 0, 0)),
            pl.BlockSpec((count, slots), lambda h: (0, 0), pipeline_mode=pl.Buffered(1)),
            pl.BlockSpec((count // 128, 128), lambda h: (0, 0)),
        ],
        out_specs=pl.BlockSpec((count // 128, 128), lambda h: (0, 0)),
        scratch_shapes=[pltpu.VMEM((slots, 1), F32)],
        compiler_params=pltpu.CompilerParams(vmem_limit_bytes=12 * 2**20),
        cost_estimate=pl.CostEstimate(
            flops=2 * slots * halves * part,
            bytes_accessed=2 * slots * halves * part,
            transcendentals=0,
        ),
        name="slot_squares",
    )(received, pick, base)


def pick_kernel(received, pick, usable, text, prompt):
    arrived = received[...].reshape(pick.shape[1], received.shape[-1])
    picked = jnp.dot(pick[...], arrived, preferred_element_type=F32)
    prompt[...] = jnp.where(usable[...] > 0, picked, text[...].astype(F32)).astype(BF)


def pick_rows(received, pick, usable, text, index):
    planes, halves, rows, part = received.shape
    count, slots = pick.shape
    parts = text.shape[1] // (halves * part)
    return pl.pallas_call(
        pick_kernel,
        grid=(halves,),
        out_shape=jax.ShapeDtypeStruct((count, halves * part), BF),
        in_specs=[
            pl.BlockSpec((planes, 1, rows, part), lambda h: (0, h, 0, 0)),
            pl.BlockSpec((count, slots), lambda h: (0, 0), pipeline_mode=pl.Buffered(1)),
            pl.BlockSpec((count, 1), lambda h: (0, 0), pipeline_mode=pl.Buffered(1)),
            pl.BlockSpec((count, part), lambda h: (0, h * parts + index)),
        ],
        out_specs=pl.BlockSpec((count, part), lambda h: (0, h)),
        compiler_params=pltpu.CompilerParams(vmem_limit_bytes=14 * 2**20),
        cost_estimate=pl.CostEstimate(
            flops=2 * count * slots * halves * part,
            bytes_accessed=6 * count * halves * part,
            transcendentals=0,
        ),
        name="pick_rows",
    )(received, pick, usable, text)


def finish_kernel(first, second, own, core, far, both, gain, out, inverse, *, width):
    @pl.when(pl.program_id(0) == 0)
    def _():
        total = to_column(own[...] + core[...] + far[...] + both[...])
        inverse[...] = lax.rsqrt(total / width + EPSILON)

    part = first.shape[1]
    out[:, :part] = (first[...].astype(F32) * inverse[...] * gain[:, :part]).astype(BF)
    out[:, part:] = (second[...].astype(F32) * inverse[...] * gain[:, part:]).astype(BF)


def finish(first, second, squares, gain):
    count, width = first.shape
    part = width // 2
    small = pl.BlockSpec((count // 128, 128), lambda h: (0, 0))
    return pl.pallas_call(
        functools.partial(finish_kernel, width=8 * width),
        grid=(2,),
        out_shape=jax.ShapeDtypeStruct((count, 2 * width), BF),
        in_specs=[pl.BlockSpec((count, part), lambda h: (0, h))] * 2
        + [small] * 4
        + [pl.BlockSpec((1, 2 * part), lambda h: (0, h))],
        out_specs=pl.BlockSpec((count, 2 * part), lambda h: (0, h)),
        scratch_shapes=[pltpu.VMEM((count, 1), F32)],
        compiler_params=pltpu.CompilerParams(vmem_limit_bytes=12 * 2**20),
        cost_estimate=pl.CostEstimate(
            flops=6 * count * width, bytes_accessed=8 * count * width, transcendentals=count
        ),
        name="finish",
    )(first, second, *squares, gain[None, :])


def swap_tp(block, k):
    return lax.ppermute(block, TP, [(i, i ^ k) for i in range(4)])


def shift_y(block, d):
    return lax.ppermute(block, ("yh", "yl"), [(i, (i + d) % 4) for i in range(4)])


def swap_core(block):
    return lax.ppermute(block, "c", [(0, 1), (1, 0)])


def on_device(
    patches,
    image_ids,
    qkv_weight,
    out_weight,
    merge_gain,
    merge_weight,
    text_rows,
    image_refs,
    llm_gain,
):
    yh = lax.axis_index("yh")
    tp = lax.axis_index(TP)
    y = lax.axis_index(("yh", "yl"))
    core = lax.axis_index("c")

    half = merge_weight.shape[1] // 2
    own = lax.dynamic_slice_in_dim(merge_weight, yh * half, half, 1)
    other = lax.dynamic_slice_in_dim(merge_weight, (1 - yh) * half, half, 1)
    arrived = lax.ppermute(other, "yh", [(0, 1), (1, 0)])

    prompt_rows = image_refs.shape[0]
    usable = image_refs >= 0
    source = jnp.where(usable, image_refs // 256, -1)
    hits = (source[:, None] == jnp.arange(32)[None, :]).astype(BF)
    before = (jnp.arange(prompt_rows)[:, None] > jnp.arange(prompt_rows)[None, :]).astype(BF)
    earlier = jnp.dot(before, hits, preferred_element_type=F32)
    arrival = jnp.sum(earlier * hits.astype(F32), axis=1).astype(jnp.int32)
    slot = jnp.where(usable, source * 16 + arrival, -1)
    pick = (slot[:, None] == jnp.arange(512)[None, :]).astype(BF)
    names = jnp.where(usable, image_refs % 256 + 1, 0).astype(BF)
    table = jnp.dot(names[None, :], pick, preferred_element_type=F32).astype(jnp.int32)
    table = jnp.broadcast_to(table.reshape(16, 1, 32), (16, 2, 32)).reshape(32, 32)
    usable = usable.astype(jnp.int32)[:, None]

    arrived, table, pick, usable, out_weight = lax.optimization_barrier(
        (arrived, table, pick, usable, out_weight)
    )
    is_own = (jnp.arange(2) == yh)[:, None, None]
    both = jnp.where(is_own, own[None], arrived[None]).reshape(-1, half)
    weight = lax.all_gather(both, ("z", "x"), axis=0, tiled=True)

    middle = out_weight.shape[0] // 2
    out_far = [shift_y(out_weight[:middle], 1), shift_y(out_weight[middle:], -1)]

    patch_ids = jnp.repeat(image_ids.reshape(-1), MERGE)
    patch_ids, patches, both = lax.optimization_barrier((patch_ids, patches, both))
    context = vision_context(patches, jnp.swapaxes(qkv_weight, 1, 2), patch_ids)
    context, *out_far = lax.optimization_barrier((context, *out_far))
    rows = context.shape[0] // 4
    parts = [
        lax.dynamic_slice_in_dim(context, (tp ^ k) * rows, rows, 0) for k in range(4)
    ]
    parts = [parts[0]] + [swap_tp(parts[k], k) for k in (1, 2, 3)]
    out_blocks = [out_weight, swap_core(out_weight)] + out_far + [swap_core(b) for b in out_far]
    merged = project_and_norm(tp, parts, out_blocks, patches, merge_gain)

    table, merged = lax.optimization_barrier((table, merged))
    after, before = shift_y(merged, 1), shift_y(merged, -1)
    count = merged.shape[0] // 2
    far = [shift_y(after[:count], 1), shift_y(before[count:], -1)]
    table = lax.all_to_all(table, SEC, split_axis=0, concat_axis=0, tiled=True)
    after, before, table = lax.optimization_barrier((after, before, table))
    near_rows = [
        (0, 0, merged),
        (1, 0, after),
        (-1, 0, before),
        (2, 0, far[0]),
        (2, count, far[1]),
    ]
    blocks = []
    ids = []
    for d, offset, block in near_rows:
        blocks += [block, swap_core(block)]
        origin = (y - d + 4) % 4 * 128 + offset
        ids += [origin + c * 64 + jnp.arange(block.shape[0]) for c in (core, 1 - core)]
    row_ids = jnp.concatenate(ids)

    wanted = table.reshape(32, 2, 16) - 1
    wanted = jnp.where(wanted >= 0, wanted + jnp.arange(2)[None, :, None] * 256, -1).reshape(-1)
    send = (wanted[:, None] == row_ids[None, :]).astype(BF)

    rows = stack_rows(blocks)
    squares = text_squares(text_rows, usable)
    prompts = []
    for index in range(2):
        outgoing = merge_and_select(rows, weight, send, index * half // 2, half // 2)
        received = lax.all_to_all(outgoing, SEC, split_axis=0, concat_axis=0, tiled=True)
        received = received.reshape(16, 2, 32, half // 2)
        squares = slot_squares(received, pick, squares)
        prompts.append(pick_rows(received, pick, usable, text_rows, index))
    squares = [squares] + [swap_tp(squares, k) for k in (1, 2, 3)]
    return finish(*prompts, squares, llm_gain)


def solution(mesh):
    torus = Mesh(mesh.devices.reshape(4, 4, 2, 2, 2), ("z", "x", "yh", "yl", "c"))
    return jax.shard_map(
        on_device,
        mesh=torus,
        in_specs=(
            P(SEC, None),
            P(SEC, None),
            P(None, None, TP),
            P(TP, None),
            P(),
            P(SEC, TP),
            P(SEC, TP),
            P(SEC),
            P(TP),
        ),
        out_specs=P(SEC, TP),
        check_vma=False,
    )
```

```python
import functools

import jax
import jax.numpy as jnp
from jax import lax
from jax.experimental import pallas as pl
from jax.experimental.pallas import tpu as pltpu
from jax.sharding import Mesh, PartitionSpec as P

HEAD_DIM = 80
MERGE = 4
EPSILON = 1e-06
LOG2E = 1.4426950408889634
SEC = ("z", "x", "yh")
TP = ("yl", "c")
BF = jnp.bfloat16
F32 = jnp.float32


def attention_kernel(row_ids, column_ids, patches, weight, context, queries, keys, values):
    heads = keys.shape[0]
    row_count = patches.shape[0]
    block = min(256, row_count)
    one = jnp.ones((block, 128 - HEAD_DIM), BF)

    def project(index, carry):
        rows = pl.ds(pl.multiple_of(index * block, block), block)
        query, key, value = (
            lax.dot_general(
                patches[rows, :], weight[c], (((1,), (1,)), ((), ())), preferred_element_type=F32
            ).astype(BF)
            for c in range(3)
        )
        for head in range(heads):
            columns = slice(head * HEAD_DIM, (head + 1) * HEAD_DIM)
            queries[head, rows, :] = query[:, columns]
            keys[head, rows, :] = key[:, columns]
            values[head, rows, :] = jnp.concatenate([value[:, columns], one], axis=1)
        return carry

    lax.fori_loop(0, row_count // block, project, 0)
    scale = HEAD_DIM ** (-0.5) * LOG2E

    def one_block(index, carry):
        rows = pl.ds(pl.multiple_of(index * block, block), block)
        same_image = row_ids[rows, :] == column_ids[...]
        outs = []
        for head in range(heads):
            scores = lax.dot_general(
                queries[head, rows, :],
                keys[head],
                (((1,), (1,)), ((), ())),
                preferred_element_type=F32,
            )
            scores = jnp.where(same_image, scores, -1e30)
            highest = jnp.max(scores, axis=1, keepdims=True)
            weights = jnp.exp2((scores - highest) * scale).astype(BF)
            summed = jnp.dot(weights, values[head], preferred_element_type=F32)
            outs.append(summed[:, :HEAD_DIM] / summed[:, HEAD_DIM : HEAD_DIM + 1])
        context[rows, :] = jnp.concatenate(outs, axis=1).astype(BF)
        return carry

    lax.fori_loop(0, row_count // block, one_block, 0)


def vision_context(patches, weight, patch_ids):
    row_count, depth = patches.shape
    width = weight.shape[1]
    heads = width // HEAD_DIM
    return pl.pallas_call(
        attention_kernel,
        out_shape=jax.ShapeDtypeStruct((row_count, width), BF),
        in_specs=[pl.BlockSpec(memory_space=pltpu.VMEM)] * 4,
        out_specs=pl.BlockSpec(memory_space=pltpu.VMEM),
        scratch_shapes=[
            pltpu.VMEM((heads, row_count, HEAD_DIM), BF),
            pltpu.VMEM((heads, row_count, HEAD_DIM), BF),
            pltpu.VMEM((heads, row_count, 128), BF),
        ],
        compiler_params=pltpu.CompilerParams(vmem_limit_bytes=20 * 2**20),
        cost_estimate=pl.CostEstimate(
            flops=4 * heads * row_count * row_count * 256 + 6 * row_count * depth * width,
            bytes_accessed=2 * (row_count + 3 * width) * depth,
            transcendentals=heads * row_count * row_count,
        ),
        name="vision_attention",
    )(patch_ids[:, None], patch_ids[None, :], patches, weight)


def norm_kernel(*refs):
    parts, outs, (patches, gain, merged, normed) = refs[1:5], refs[5:11], refs[11:]
    outs = [outs[0][...], outs[1][...]] + [
        jnp.concatenate([outs[k][...], outs[k + 1][...]], axis=0) for k in (2, 4)
    ]
    attended = patches[...].astype(F32)
    for part, weight in zip(parts, outs):
        attended += jnp.dot(part[...], weight, preferred_element_type=F32)
    moment = jnp.mean(attended * attended, axis=1, keepdims=True)
    scaled = attended * lax.rsqrt(moment + EPSILON) * gain[...]
    count, width = merged.shape[0], scaled.shape[1]
    for q in range(width // 128):
        normed[q] = scaled[:, q * 128 : (q + 1) * 128]
    for j in range(MERGE):
        for q in range(width // 128):
            piece = normed[q, pl.ds(j, count, stride=MERGE), :].astype(BF)
            columns = slice(j * width + q * 128, j * width + (q + 1) * 128)
            merged[:, columns] = piece


def project_and_norm(tp, parts, outs, patches, gain):
    rows, depth = parts[0].shape
    width = patches.shape[1]
    count = rows // MERGE
    whole = lambda shape: pl.BlockSpec(shape, lambda i, t: (0, 0))
    return pl.pallas_call(
        norm_kernel,
        grid_spec=pltpu.PrefetchScalarGridSpec(
            num_scalar_prefetch=1,
            grid=(1,),
            in_specs=[whole((rows, depth))] * 4
            + [whole(out.shape) for out in outs]
            + [pl.BlockSpec((rows, width), lambda i, t: (t[0], 0)), whole((1, width))],
            out_specs=whole((count, MERGE * width)),
            scratch_shapes=[pltpu.VMEM((width // 128, rows, 128), F32)],
        ),
        out_shape=jax.ShapeDtypeStruct((count, MERGE * width), BF),
        compiler_params=pltpu.CompilerParams(vmem_limit_bytes=18 * 2**20),
        cost_estimate=pl.CostEstimate(
            flops=8 * rows * depth * width,
            bytes_accessed=8 * depth * (rows + width) + 4 * rows * width,
            transcendentals=rows,
        ),
        name="project_and_norm",
    )(tp.reshape(1).astype(jnp.int32), *parts, *outs, patches, gain[None, :])


def stack_kernel(*refs):
    first = 0
    for block in refs[:-1]:
        refs[-1][first : first + block.shape[0], :] = block[...]
        first += block.shape[0]


def stack_rows(blocks):
    count = sum(block.shape[0] for block in blocks)
    depth = blocks[0].shape[1]
    tile = depth // 4
    return pl.pallas_call(
        stack_kernel,
        grid=(depth // tile,),
        out_shape=jax.ShapeDtypeStruct((count, depth), BF),
        in_specs=[pl.BlockSpec((b.shape[0], tile), lambda i: (0, i)) for b in blocks],
        out_specs=pl.BlockSpec((count, tile), lambda i: (0, i)),
        compiler_params=pltpu.CompilerParams(vmem_limit_bytes=10 * 2**20),
        cost_estimate=pl.CostEstimate(
            flops=0, bytes_accessed=4 * count * depth, transcendentals=0
        ),
        name="stack_rows",
    )(*blocks)


def merge_kernel(rows, weight, send, outgoing, held, sems):
    depth, columns = held.shape
    steps = sems.shape[0]
    tile = depth // steps
    copies = [
        pltpu.make_async_copy(
            weight.at[pl.ds(k * tile, tile)], held.at[pl.ds(k * tile, tile)], sems.at[k]
        )
        for k in range(steps)
    ]
    for copy in copies:
        copy.start()
    total = jnp.zeros((rows.shape[0], columns), F32)
    for k, copy in enumerate(copies):
        copy.wait()
        part = slice(k * tile, (k + 1) * tile)
        total += jnp.dot(rows[:, part], held[part, :], preferred_element_type=F32)
    outgoing[...] = jnp.dot(
        send[...], total.astype(BF), preferred_element_type=F32
    ).astype(BF)


def merge_and_select(rows, weight, send):
    slots, count = send.shape
    depth, columns = weight.shape
    vmem = pl.BlockSpec(memory_space=pltpu.VMEM)
    return pl.pallas_call(
        merge_kernel,
        out_shape=jax.ShapeDtypeStruct((slots, columns), BF),
        in_specs=[vmem, pl.BlockSpec(memory_space=pltpu.HBM), vmem],
        out_specs=vmem,
        scratch_shapes=[pltpu.VMEM((depth, columns), BF), pltpu.SemaphoreType.DMA((4,))],
        compiler_params=pltpu.CompilerParams(vmem_limit_bytes=44 * 2**20),
        cost_estimate=pl.CostEstimate(
            flops=2 * count * (depth + slots) * columns,
            bytes_accessed=2 * (count * depth + depth * columns + slots * columns),
            transcendentals=0,
        ),
        name="merge_rows",
    )(rows, weight, send)


def square_sums(block):
    value = block.astype(F32)
    return jnp.sum(value * value, axis=1, keepdims=True)


def diagonal():
    shape = (128, 128)
    return lax.broadcasted_iota(jnp.int32, shape, 0) == lax.broadcasted_iota(jnp.int32, shape, 1)


def to_lanes(column, out):
    eye = diagonal()
    for q in range(out.shape[0]):
        part = jnp.where(eye, column[q * 128 : (q + 1) * 128], 0.0)
        out[q : q + 1, :] = jnp.sum(part, axis=0, keepdims=True)


def to_column(lanes):
    eye = diagonal()
    return jnp.concatenate(
        [
            jnp.sum(jnp.where(eye, lanes[q : q + 1], 0.0), axis=1, keepdims=True)
            for q in range(lanes.shape[0])
        ],
        axis=0,
    )


def text_kernel(text, usable, squares):
    total = jnp.where(usable[...] > 0, 0.0, square_sums(text[...]))
    to_lanes(total, squares.at[pl.ds(pl.program_id(0), 1)])


def text_squares(text, usable):
    count, width = text.shape
    return pl.pallas_call(
        text_kernel,
        grid=(count // 128,),
        out_shape=jax.ShapeDtypeStruct((count // 128, 128), F32),
        in_specs=[
            pl.BlockSpec((128, width), lambda i: (i, 0)),
            pl.BlockSpec((128, 1), lambda i: (i, 0)),
        ],
        out_specs=pl.BlockSpec((count // 128, 128), lambda i: (0, 0)),
        compiler_params=pltpu.CompilerParams(vmem_limit_bytes=10 * 2**20),
        cost_estimate=pl.CostEstimate(
            flops=2 * count * width, bytes_accessed=2 * count * width, transcendentals=0
        ),
        name="text_squares",
    )(text, usable)


def squares_kernel(received, pick, base, squares, total):
    arrived = received[...].reshape(pick.shape[1], received.shape[-1])
    step = pl.program_id(0)

    @pl.when(step == 0)
    def _():
        total[...] = square_sums(arrived)

    @pl.when(step > 0)
    def _():
        total[...] += square_sums(arrived)

    @pl.when(step == pl.num_programs(0) - 1)
    def _():
        rest = jnp.broadcast_to(total[...], (total.shape[0], 128))
        chosen = jnp.zeros((pick.shape[0], 128), F32)
        for _ in range(3):
            part = rest.astype(BF)
            chosen += jnp.dot(pick[...], part, preferred_element_type=F32)
            rest = rest - part.astype(F32)
        to_lanes(chosen[:, :1], squares)
        squares[...] += base[...]


def slot_squares(received, pick, base):
    planes, halves, rows, part = received.shape
    count, slots = pick.shape
    return pl.pallas_call(
        squares_kernel,
        grid=(halves,),
        out_shape=jax.ShapeDtypeStruct((count // 128, 128), F32),
        in_specs=[
            pl.BlockSpec((planes, 1, rows, part), lambda h: (0, h, 0, 0)),
            pl.BlockSpec((count, slots), lambda h: (0, 0), pipeline_mode=pl.Buffered(1)),
            pl.BlockSpec((count // 128, 128), lambda h: (0, 0)),
        ],
        out_specs=pl.BlockSpec((count // 128, 128), lambda h: (0, 0)),
        scratch_shapes=[pltpu.VMEM((slots, 1), F32)],
        compiler_params=pltpu.CompilerParams(vmem_limit_bytes=12 * 2**20),
        cost_estimate=pl.CostEstimate(
            flops=2 * slots * halves * part,
            bytes_accessed=2 * slots * halves * part,
            transcendentals=0,
        ),
        name="slot_squares",
    )(received, pick, base)


def pick_kernel(received, pick, usable, text, prompt):
    arrived = received[...].reshape(pick.shape[1], received.shape[-1])
    picked = jnp.dot(pick[...], arrived, preferred_element_type=F32)
    prompt[...] = jnp.where(usable[...] > 0, picked, text[...].astype(F32)).astype(BF)


def pick_rows(received, pick, usable, text):
    planes, halves, rows, part = received.shape
    count, slots = pick.shape
    return pl.pallas_call(
        pick_kernel,
        grid=(halves,),
        out_shape=jax.ShapeDtypeStruct((count, halves * part), BF),
        in_specs=[
            pl.BlockSpec((planes, 1, rows, part), lambda h: (0, h, 0, 0)),
            pl.BlockSpec((count, slots), lambda h: (0, 0), pipeline_mode=pl.Buffered(1)),
            pl.BlockSpec((count, 1), lambda h: (0, 0), pipeline_mode=pl.Buffered(1)),
            pl.BlockSpec((count, part), lambda h: (0, h)),
        ],
        out_specs=pl.BlockSpec((count, part), lambda h: (0, h)),
        compiler_params=pltpu.CompilerParams(vmem_limit_bytes=14 * 2**20),
        cost_estimate=pl.CostEstimate(
            flops=2 * count * slots * halves * part,
            bytes_accessed=6 * count * halves * part,
            transcendentals=0,
        ),
        name="pick_rows",
    )(received, pick, usable, text)


def finish_kernel(prompt, own, core, far, both, gain, out, inverse, *, width):
    @pl.when(pl.program_id(0) == 0)
    def _():
        total = to_column(own[...] + core[...] + far[...] + both[...])
        inverse[...] = lax.rsqrt(total / width + EPSILON)

    out[...] = (prompt[...].astype(F32) * inverse[...] * gain[...]).astype(BF)


def finish(prompt, squares, gain):
    count, width = prompt.shape
    part = width // 4
    small = pl.BlockSpec((count // 128, 128), lambda h: (0, 0))
    return pl.pallas_call(
        functools.partial(finish_kernel, width=4 * width),
        grid=(4,),
        out_shape=jax.ShapeDtypeStruct((count, width), BF),
        in_specs=[pl.BlockSpec((count, part), lambda h: (0, h))]
        + [small] * 4
        + [pl.BlockSpec((1, part), lambda h: (0, h))],
        out_specs=pl.BlockSpec((count, part), lambda h: (0, h)),
        scratch_shapes=[pltpu.VMEM((count, 1), F32)],
        compiler_params=pltpu.CompilerParams(vmem_limit_bytes=10 * 2**20),
        cost_estimate=pl.CostEstimate(
            flops=3 * count * width, bytes_accessed=4 * count * width, transcendentals=count
        ),
        name="finish",
    )(prompt, *squares, gain[None, :])


def swap_tp(block, k):
    return lax.ppermute(block, TP, [(i, i ^ k) for i in range(4)])


def shift_y(block, d):
    return lax.ppermute(block, ("yh", "yl"), [(i, (i + d) % 4) for i in range(4)])


def swap_core(block):
    return lax.ppermute(block, "c", [(0, 1), (1, 0)])


def on_device(
    patches,
    image_ids,
    qkv_weight,
    out_weight,
    merge_gain,
    merge_weight,
    text_rows,
    image_refs,
    llm_gain,
):
    yh = lax.axis_index("yh")
    tp = lax.axis_index(TP)
    y = lax.axis_index(("yh", "yl"))
    core = lax.axis_index("c")

    half = merge_weight.shape[1] // 2
    own = lax.dynamic_slice_in_dim(merge_weight, yh * half, half, 1)
    other = lax.dynamic_slice_in_dim(merge_weight, (1 - yh) * half, half, 1)
    arrived = lax.ppermute(other, "yh", [(0, 1), (1, 0)])

    prompt_rows = image_refs.shape[0]
    usable = image_refs >= 0
    source = jnp.where(usable, image_refs // 256, -1)
    hits = (source[:, None] == jnp.arange(32)[None, :]).astype(BF)
    before = (jnp.arange(prompt_rows)[:, None] > jnp.arange(prompt_rows)[None, :]).astype(BF)
    earlier = jnp.dot(before, hits, preferred_element_type=F32)
    arrival = jnp.sum(earlier * hits.astype(F32), axis=1).astype(jnp.int32)
    slot = jnp.where(usable, source * 16 + arrival, -1)
    pick = (slot[:, None] == jnp.arange(512)[None, :]).astype(BF)
    names = jnp.where(usable, image_refs % 256 + 1, 0).astype(BF)
    table = jnp.dot(names[None, :], pick, preferred_element_type=F32).astype(jnp.int32)
    table = jnp.broadcast_to(table.reshape(16, 1, 32), (16, 2, 32)).reshape(32, 32)
    usable = usable.astype(jnp.int32)[:, None]

    arrived, table, pick, usable, out_weight = lax.optimization_barrier(
        (arrived, table, pick, usable, out_weight)
    )
    is_own = (jnp.arange(2) == yh)[:, None, None]
    both = jnp.where(is_own, own[None], arrived[None]).reshape(-1, half)
    weight = lax.all_gather(both, ("z", "x"), axis=0, tiled=True)

    middle = out_weight.shape[0] // 2
    out_far = [shift_y(out_weight[:middle], 1), shift_y(out_weight[middle:], -1)]

    patch_ids = jnp.repeat(image_ids.reshape(-1), MERGE)
    patch_ids, patches, both = lax.optimization_barrier((patch_ids, patches, both))
    context = vision_context(patches, jnp.swapaxes(qkv_weight, 1, 2), patch_ids)
    context, *out_far = lax.optimization_barrier((context, *out_far))
    rows = context.shape[0] // 4
    parts = [
        lax.dynamic_slice_in_dim(context, (tp ^ k) * rows, rows, 0) for k in range(4)
    ]
    parts = [parts[0]] + [swap_tp(parts[k], k) for k in (1, 2, 3)]
    out_blocks = [out_weight, swap_core(out_weight)] + out_far + [swap_core(b) for b in out_far]
    merged = project_and_norm(tp, parts, out_blocks, patches, merge_gain)

    table, merged = lax.optimization_barrier((table, merged))
    after, before = shift_y(merged, 1), shift_y(merged, -1)
    count = merged.shape[0] // 2
    far = [shift_y(after[:count], 1), shift_y(before[count:], -1)]
    table = lax.all_to_all(table, SEC, split_axis=0, concat_axis=0, tiled=True)
    after, before, table = lax.optimization_barrier((after, before, table))
    near_rows = [
        (0, 0, merged),
        (1, 0, after),
        (-1, 0, before),
        (2, 0, far[0]),
        (2, count, far[1]),
    ]
    blocks = []
    ids = []
    for d, offset, block in near_rows:
        blocks += [block, swap_core(block)]
        origin = (y - d + 4) % 4 * 128 + offset
        ids += [origin + c * 64 + jnp.arange(block.shape[0]) for c in (core, 1 - core)]
    row_ids = jnp.concatenate(ids)

    wanted = table.reshape(32, 2, 16) - 1
    wanted = jnp.where(wanted >= 0, wanted + jnp.arange(2)[None, :, None] * 256, -1).reshape(-1)
    send = (wanted[:, None] == row_ids[None, :]).astype(BF)

    outgoing = merge_and_select(stack_rows(blocks), weight, send)
    received = lax.all_to_all(outgoing, SEC, split_axis=0, concat_axis=0, tiled=True)
    received = received.reshape(16, 2, 32, half)
    squares = slot_squares(received, pick, text_squares(text_rows, usable))
    squares = [squares] + [swap_tp(squares, k) for k in (1, 2, 3)]
    return finish(pick_rows(received, pick, usable, text_rows), squares, llm_gain)


def solution(mesh):
    torus = Mesh(mesh.devices.reshape(4, 4, 2, 2, 2), ("z", "x", "yh", "yl", "c"))
    return jax.shard_map(
        on_device,
        mesh=torus,
        in_specs=(
            P(SEC, None),
            P(SEC, None),
            P(None, None, TP),
            P(TP, None),
            P(),
            P(SEC, TP),
            P(SEC, TP),
            P(SEC),
            P(TP),
        ),
        out_specs=P(SEC, TP),
        check_vma=False,
    )
```

```python
import functools

import jax
import jax.numpy as jnp
from jax import lax
from jax.experimental import pallas as pl
from jax.experimental.pallas import tpu as pltpu
from jax.sharding import Mesh, PartitionSpec as P

HEAD_DIM = 80
MERGE = 4
EPSILON = 1e-06
LOG2E = 1.4426950408889634
SEC = ("z", "x", "yh")
TP = ("yl", "c")
BF = jnp.bfloat16
F32 = jnp.float32


def attention_kernel(row_ids, column_ids, patches, weight, context, queries, keys, values):
    heads = keys.shape[0]
    row_count = patches.shape[0]
    block = min(256, row_count)
    one = jnp.ones((block, 128 - HEAD_DIM), BF)

    def project(index, carry):
        rows = pl.ds(pl.multiple_of(index * block, block), block)
        query, key, value = (
            lax.dot_general(
                patches[rows, :], weight[c], (((1,), (1,)), ((), ())), preferred_element_type=F32
            ).astype(BF)
            for c in range(3)
        )
        for head in range(heads):
            columns = slice(head * HEAD_DIM, (head + 1) * HEAD_DIM)
            queries[head, rows, :] = query[:, columns]
            keys[head, rows, :] = key[:, columns]
            values[head, rows, :] = jnp.concatenate([value[:, columns], one], axis=1)
        return carry

    lax.fori_loop(0, row_count // block, project, 0)
    scale = HEAD_DIM ** (-0.5) * LOG2E

    def one_block(index, carry):
        rows = pl.ds(pl.multiple_of(index * block, block), block)
        same_image = row_ids[rows, :] == column_ids[...]
        outs = []
        for head in range(heads):
            scores = lax.dot_general(
                queries[head, rows, :],
                keys[head],
                (((1,), (1,)), ((), ())),
                preferred_element_type=F32,
            )
            scores = jnp.where(same_image, scores, -1e30)
            highest = jnp.max(scores, axis=1, keepdims=True)
            weights = jnp.exp2((scores - highest) * scale).astype(BF)
            summed = jnp.dot(weights, values[head], preferred_element_type=F32)
            outs.append(summed[:, :HEAD_DIM] / summed[:, HEAD_DIM : HEAD_DIM + 1])
        context[rows, :] = jnp.concatenate(outs, axis=1).astype(BF)
        return carry

    lax.fori_loop(0, row_count // block, one_block, 0)


def vision_context(patches, weight, patch_ids):
    row_count, depth = patches.shape
    width = weight.shape[1]
    heads = width // HEAD_DIM
    return pl.pallas_call(
        attention_kernel,
        out_shape=jax.ShapeDtypeStruct((row_count, width), BF),
        in_specs=[pl.BlockSpec(memory_space=pltpu.VMEM)] * 4,
        out_specs=pl.BlockSpec(memory_space=pltpu.VMEM),
        scratch_shapes=[
            pltpu.VMEM((heads, row_count, HEAD_DIM), BF),
            pltpu.VMEM((heads, row_count, HEAD_DIM), BF),
            pltpu.VMEM((heads, row_count, 128), BF),
        ],
        compiler_params=pltpu.CompilerParams(vmem_limit_bytes=20 * 2**20),
        cost_estimate=pl.CostEstimate(
            flops=4 * heads * row_count * row_count * 256 + 6 * row_count * depth * width,
            bytes_accessed=2 * (row_count + 3 * width) * depth,
            transcendentals=heads * row_count * row_count,
        ),
        name="vision_attention",
    )(patch_ids[:, None], patch_ids[None, :], patches, weight)


def norm_kernel(*refs):
    parts, outs, (patches, gain, merged, normed) = refs[1:5], refs[5:11], refs[11:]
    outs = [outs[0][...], outs[1][...]] + [
        jnp.concatenate([outs[k][...], outs[k + 1][...]], axis=0) for k in (2, 4)
    ]
    attended = patches[...].astype(F32)
    for part, weight in zip(parts, outs):
        attended += jnp.dot(part[...], weight, preferred_element_type=F32)
    moment = jnp.mean(attended * attended, axis=1, keepdims=True)
    scaled = attended * lax.rsqrt(moment + EPSILON) * gain[...]
    count, width = merged.shape[0], scaled.shape[1]
    for q in range(width // 128):
        normed[q] = scaled[:, q * 128 : (q + 1) * 128]
    for j in range(MERGE):
        for q in range(width // 128):
            piece = normed[q, pl.ds(j, count, stride=MERGE), :].astype(BF)
            columns = slice(j * width + q * 128, j * width + (q + 1) * 128)
            merged[:, columns] = piece


def project_and_norm(tp, parts, outs, patches, gain):
    rows, depth = parts[0].shape
    width = patches.shape[1]
    count = rows // MERGE
    whole = lambda shape: pl.BlockSpec(shape, lambda i, t: (0, 0))
    return pl.pallas_call(
        norm_kernel,
        grid_spec=pltpu.PrefetchScalarGridSpec(
            num_scalar_prefetch=1,
            grid=(1,),
            in_specs=[whole((rows, depth))] * 4
            + [whole(out.shape) for out in outs]
            + [pl.BlockSpec((rows, width), lambda i, t: (t[0], 0)), whole((1, width))],
            out_specs=whole((count, MERGE * width)),
            scratch_shapes=[pltpu.VMEM((width // 128, rows, 128), F32)],
        ),
        out_shape=jax.ShapeDtypeStruct((count, MERGE * width), BF),
        compiler_params=pltpu.CompilerParams(vmem_limit_bytes=18 * 2**20),
        cost_estimate=pl.CostEstimate(
            flops=8 * rows * depth * width,
            bytes_accessed=8 * depth * (rows + width) + 4 * rows * width,
            transcendentals=rows,
        ),
        name="project_and_norm",
    )(tp.reshape(1).astype(jnp.int32), *parts, *outs, patches, gain[None, :])


def stack_kernel(*refs):
    first = 0
    for block in refs[:-1]:
        refs[-1][first : first + block.shape[0], :] = block[...]
        first += block.shape[0]


def stack_rows(blocks):
    count = sum(block.shape[0] for block in blocks)
    depth = blocks[0].shape[1]
    tile = depth // 4
    return pl.pallas_call(
        stack_kernel,
        grid=(depth // tile,),
        out_shape=pltpu.HBM((count, depth), BF),
        in_specs=[pl.BlockSpec((b.shape[0], tile), lambda i: (0, i)) for b in blocks],
        out_specs=pl.BlockSpec((count, tile), lambda i: (0, i)),
        compiler_params=pltpu.CompilerParams(vmem_limit_bytes=10 * 2**20),
        cost_estimate=pl.CostEstimate(
            flops=0, bytes_accessed=4 * count * depth, transcendentals=0
        ),
        name="stack_rows",
    )(*blocks)


def merge_kernel(rows, weight, send, outgoing, rows_held, weight_held, sent, sems):
    depth = weight_held.shape[0]
    steps = sems.shape[0] // 2
    tile = depth // steps
    copies = []
    for k in range(steps):
        part = pl.ds(k * tile, tile)
        copies += [
            pltpu.make_async_copy(rows.at[:, part], rows_held.at[:, part], sems.at[2 * k]),
            pltpu.make_async_copy(weight.at[part], weight_held.at[part], sems.at[2 * k + 1]),
        ]
    for copy in copies:
        copy.start()
    total = jnp.zeros((rows_held.shape[0], weight_held.shape[1]), F32)
    for k in range(steps):
        copies[2 * k].wait()
        copies[2 * k + 1].wait()
        part = slice(k * tile, (k + 1) * tile)
        total += jnp.dot(
            rows_held[:, part], weight_held[part, :], preferred_element_type=F32
        )
    image = total.astype(BF)
    pieces = 4
    count = sent.shape[0] // pieces
    copies = []
    for k in range(pieces):
        part = pl.ds(k * count, count)
        sent[part, :] = jnp.dot(send[part, :], image, preferred_element_type=F32).astype(BF)
        copy = pltpu.make_async_copy(sent.at[part], outgoing.at[part], sems.at[k])
        copy.start()
        copies.append(copy)
    for copy in copies:
        copy.wait()


def merge_and_select(rows, weight, send):
    slots, count = send.shape
    depth, columns = weight.shape
    hbm = pl.BlockSpec(memory_space=pltpu.HBM)
    return pl.pallas_call(
        merge_kernel,
        out_shape=pltpu.HBM((slots, columns), BF),
        in_specs=[hbm, hbm, pl.BlockSpec(memory_space=pltpu.VMEM)],
        out_specs=hbm,
        scratch_shapes=[
            pltpu.VMEM((count, depth), BF),
            pltpu.VMEM((depth, columns), BF),
            pltpu.VMEM((slots, columns), BF),
            pltpu.SemaphoreType.DMA((8,)),
        ],
        compiler_params=pltpu.CompilerParams(vmem_limit_bytes=44 * 2**20),
        cost_estimate=pl.CostEstimate(
            flops=2 * count * (depth + slots) * columns,
            bytes_accessed=2 * (count * depth + depth * columns + slots * columns),
            transcendentals=0,
        ),
        name="merge_rows",
    )(rows, weight, send)


def square_sums(block):
    value = block.astype(F32)
    return jnp.sum(value * value, axis=1, keepdims=True)


def diagonal():
    shape = (128, 128)
    return lax.broadcasted_iota(jnp.int32, shape, 0) == lax.broadcasted_iota(jnp.int32, shape, 1)


def to_lanes(column, out):
    eye = diagonal()
    for q in range(out.shape[0]):
        part = jnp.where(eye, column[q * 128 : (q + 1) * 128], 0.0)
        out[q : q + 1, :] = jnp.sum(part, axis=0, keepdims=True)


def to_column(lanes):
    eye = diagonal()
    return jnp.concatenate(
        [
            jnp.sum(jnp.where(eye, lanes[q : q + 1], 0.0), axis=1, keepdims=True)
            for q in range(lanes.shape[0])
        ],
        axis=0,
    )


def text_kernel(text, usable, squares):
    total = jnp.where(usable[...] > 0, 0.0, square_sums(text[...]))
    to_lanes(total, squares.at[pl.ds(pl.program_id(0), 1)])


def text_squares(text, usable):
    count, width = text.shape
    return pl.pallas_call(
        text_kernel,
        grid=(count // 128,),
        out_shape=jax.ShapeDtypeStruct((count // 128, 128), F32),
        in_specs=[
            pl.BlockSpec((128, width), lambda i: (i, 0)),
            pl.BlockSpec((128, 1), lambda i: (i, 0)),
        ],
        out_specs=pl.BlockSpec((count // 128, 128), lambda i: (0, 0)),
        compiler_params=pltpu.CompilerParams(vmem_limit_bytes=10 * 2**20),
        cost_estimate=pl.CostEstimate(
            flops=2 * count * width, bytes_accessed=2 * count * width, transcendentals=0
        ),
        name="text_squares",
    )(text, usable)


def squares_kernel(received, pick, base, squares, total):
    arrived = received[...].reshape(pick.shape[1], received.shape[-1])
    step = pl.program_id(0)

    @pl.when(step == 0)
    def _():
        total[...] = square_sums(arrived)

    @pl.when(step > 0)
    def _():
        total[...] += square_sums(arrived)

    @pl.when(step == pl.num_programs(0) - 1)
    def _():
        rest = jnp.broadcast_to(total[...], (total.shape[0], 128))
        chosen = jnp.zeros((pick.shape[0], 128), F32)
        for _ in range(3):
            part = rest.astype(BF)
            chosen += jnp.dot(pick[...], part, preferred_element_type=F32)
            rest = rest - part.astype(F32)
        to_lanes(chosen[:, :1], squares)
        squares[...] += base[...]


def slot_squares(received, pick, base):
    planes, halves, rows, part = received.shape
    count, slots = pick.shape
    return pl.pallas_call(
        squares_kernel,
        grid=(halves,),
        out_shape=jax.ShapeDtypeStruct((count // 128, 128), F32),
        in_specs=[
            pl.BlockSpec((planes, 1, rows, part), lambda h: (0, h, 0, 0)),
            pl.BlockSpec((count, slots), lambda h: (0, 0), pipeline_mode=pl.Buffered(1)),
            pl.BlockSpec((count // 128, 128), lambda h: (0, 0)),
        ],
        out_specs=pl.BlockSpec((count // 128, 128), lambda h: (0, 0)),
        scratch_shapes=[pltpu.VMEM((slots, 1), F32)],
        compiler_params=pltpu.CompilerParams(vmem_limit_bytes=12 * 2**20),
        cost_estimate=pl.CostEstimate(
            flops=2 * slots * halves * part,
            bytes_accessed=2 * slots * halves * part,
            transcendentals=0,
        ),
        name="slot_squares",
    )(received, pick, base)


def pick_kernel(received, pick, usable, text, prompt):
    arrived = received[...].reshape(pick.shape[1], received.shape[-1])
    picked = jnp.dot(pick[...], arrived, preferred_element_type=F32)
    prompt[...] = jnp.where(usable[...] > 0, picked, text[...].astype(F32)).astype(BF)


def pick_rows(received, pick, usable, text):
    planes, halves, rows, part = received.shape
    count, slots = pick.shape
    return pl.pallas_call(
        pick_kernel,
        grid=(halves,),
        out_shape=jax.ShapeDtypeStruct((count, halves * part), BF),
        in_specs=[
            pl.BlockSpec((planes, 1, rows, part), lambda h: (0, h, 0, 0)),
            pl.BlockSpec((count, slots), lambda h: (0, 0), pipeline_mode=pl.Buffered(1)),
            pl.BlockSpec((count, 1), lambda h: (0, 0), pipeline_mode=pl.Buffered(1)),
            pl.BlockSpec((count, part), lambda h: (0, h)),
        ],
        out_specs=pl.BlockSpec((count, part), lambda h: (0, h)),
        compiler_params=pltpu.CompilerParams(vmem_limit_bytes=14 * 2**20),
        cost_estimate=pl.CostEstimate(
            flops=2 * count * slots * halves * part,
            bytes_accessed=6 * count * halves * part,
            transcendentals=0,
        ),
        name="pick_rows",
    )(received, pick, usable, text)


def finish_kernel(prompt, own, core, far, both, gain, out, inverse, *, width):
    @pl.when(pl.program_id(0) == 0)
    def _():
        total = to_column(own[...] + core[...] + far[...] + both[...])
        inverse[...] = lax.rsqrt(total / width + EPSILON)

    out[...] = (prompt[...].astype(F32) * inverse[...] * gain[...]).astype(BF)


def finish(prompt, squares, gain):
    count, width = prompt.shape
    part = width // 4
    small = pl.BlockSpec((count // 128, 128), lambda h: (0, 0))
    return pl.pallas_call(
        functools.partial(finish_kernel, width=4 * width),
        grid=(4,),
        out_shape=jax.ShapeDtypeStruct((count, width), BF),
        in_specs=[pl.BlockSpec((count, part), lambda h: (0, h))]
        + [small] * 4
        + [pl.BlockSpec((1, part), lambda h: (0, h))],
        out_specs=pl.BlockSpec((count, part), lambda h: (0, h)),
        scratch_shapes=[pltpu.VMEM((count, 1), F32)],
        compiler_params=pltpu.CompilerParams(vmem_limit_bytes=10 * 2**20),
        cost_estimate=pl.CostEstimate(
            flops=3 * count * width, bytes_accessed=4 * count * width, transcendentals=count
        ),
        name="finish",
    )(prompt, *squares, gain[None, :])


def swap_tp(block, k):
    return lax.ppermute(block, TP, [(i, i ^ k) for i in range(4)])


def shift_y(block, d):
    return lax.ppermute(block, ("yh", "yl"), [(i, (i + d) % 4) for i in range(4)])


def swap_core(block):
    return lax.ppermute(block, "c", [(0, 1), (1, 0)])


def on_device(
    patches,
    image_ids,
    qkv_weight,
    out_weight,
    merge_gain,
    merge_weight,
    text_rows,
    image_refs,
    llm_gain,
):
    yh = lax.axis_index("yh")
    tp = lax.axis_index(TP)
    y = lax.axis_index(("yh", "yl"))
    core = lax.axis_index("c")

    half = merge_weight.shape[1] // 2
    own = lax.dynamic_slice_in_dim(merge_weight, yh * half, half, 1)
    other = lax.dynamic_slice_in_dim(merge_weight, (1 - yh) * half, half, 1)
    arrived = lax.ppermute(other, "yh", [(0, 1), (1, 0)])

    prompt_rows = image_refs.shape[0]
    usable = image_refs >= 0
    source = jnp.where(usable, image_refs // 256, -1)
    hits = (source[:, None] == jnp.arange(32)[None, :]).astype(BF)
    before = (jnp.arange(prompt_rows)[:, None] > jnp.arange(prompt_rows)[None, :]).astype(BF)
    earlier = jnp.dot(before, hits, preferred_element_type=F32)
    arrival = jnp.sum(earlier * hits.astype(F32), axis=1).astype(jnp.int32)
    slot = jnp.where(usable, source * 16 + arrival, -1)
    pick = (slot[:, None] == jnp.arange(512)[None, :]).astype(BF)
    names = jnp.where(usable, image_refs % 256 + 1, 0).astype(BF)
    table = jnp.dot(names[None, :], pick, preferred_element_type=F32).astype(jnp.int32)
    table = jnp.broadcast_to(table.reshape(16, 1, 32), (16, 2, 32)).reshape(32, 32)
    usable = usable.astype(jnp.int32)[:, None]

    arrived, table, pick, usable, out_weight = lax.optimization_barrier(
        (arrived, table, pick, usable, out_weight)
    )
    is_own = (jnp.arange(2) == yh)[:, None, None]
    both = jnp.where(is_own, own[None], arrived[None]).reshape(-1, half)
    weight = lax.all_gather(both, ("z", "x"), axis=0, tiled=True)

    middle = out_weight.shape[0] // 2
    out_far = [shift_y(out_weight[:middle], 1), shift_y(out_weight[middle:], -1)]

    patch_ids = jnp.repeat(image_ids.reshape(-1), MERGE)
    patch_ids, patches, both = lax.optimization_barrier((patch_ids, patches, both))
    context = vision_context(patches, jnp.swapaxes(qkv_weight, 1, 2), patch_ids)
    context, *out_far = lax.optimization_barrier((context, *out_far))
    rows = context.shape[0] // 4
    parts = [
        lax.dynamic_slice_in_dim(context, (tp ^ k) * rows, rows, 0) for k in range(4)
    ]
    parts = [parts[0]] + [swap_tp(parts[k], k) for k in (1, 2, 3)]
    out_blocks = [out_weight, swap_core(out_weight)] + out_far + [swap_core(b) for b in out_far]
    merged = project_and_norm(tp, parts, out_blocks, patches, merge_gain)

    table, merged = lax.optimization_barrier((table, merged))
    after, before = shift_y(merged, 1), shift_y(merged, -1)
    count = merged.shape[0] // 2
    far = [shift_y(after[:count], 1), shift_y(before[count:], -1)]
    table = lax.all_to_all(table, SEC, split_axis=0, concat_axis=0, tiled=True)
    after, before, table = lax.optimization_barrier((after, before, table))
    near_rows = [
        (0, 0, merged),
        (1, 0, after),
        (-1, 0, before),
        (2, 0, far[0]),
        (2, count, far[1]),
    ]
    blocks = []
    ids = []
    for d, offset, block in near_rows:
        blocks += [block, swap_core(block)]
        origin = (y - d + 4) % 4 * 128 + offset
        ids += [origin + c * 64 + jnp.arange(block.shape[0]) for c in (core, 1 - core)]
    row_ids = jnp.concatenate(ids)

    wanted = table.reshape(32, 2, 16) - 1
    wanted = jnp.where(wanted >= 0, wanted + jnp.arange(2)[None, :, None] * 256, -1).reshape(-1)
    send = (wanted[:, None] == row_ids[None, :]).astype(BF)

    outgoing = merge_and_select(stack_rows(blocks), weight, send)
    received = lax.all_to_all(outgoing, SEC, split_axis=0, concat_axis=0, tiled=True)
    received = received.reshape(16, 2, 32, half)
    squares = slot_squares(received, pick, text_squares(text_rows, usable))
    squares = [squares] + [swap_tp(squares, k) for k in (1, 2, 3)]
    return finish(pick_rows(received, pick, usable, text_rows), squares, llm_gain)


def solution(mesh):
    torus = Mesh(mesh.devices.reshape(4, 4, 2, 2, 2), ("z", "x", "yh", "yl", "c"))
    return jax.shard_map(
        on_device,
        mesh=torus,
        in_specs=(
            P(SEC, None),
            P(SEC, None),
            P(None, None, TP),
            P(TP, None),
            P(),
            P(SEC, TP),
            P(SEC, TP),
            P(SEC),
            P(TP),
        ),
        out_specs=P(SEC, TP),
        check_vma=False,
    )
```

```python
import functools

import jax
import jax.numpy as jnp
from jax import lax
from jax.experimental import pallas as pl
from jax.experimental.pallas import tpu as pltpu
from jax.sharding import Mesh, PartitionSpec as P

HEAD_DIM = 80
MERGE = 4
EPSILON = 1e-06
LOG2E = 1.4426950408889634
SEC = ("z", "x", "yh")
TP = ("yl", "c")
BF = jnp.bfloat16
F32 = jnp.float32


def attention_kernel(row_ids, column_ids, patches, weight, context, queries, keys, values):
    heads = keys.shape[0]
    row_count = patches.shape[0]
    block = min(256, row_count)
    one = jnp.ones((block, 128 - HEAD_DIM), BF)

    def project(index, carry):
        rows = pl.ds(pl.multiple_of(index * block, block), block)
        query, key, value = (
            lax.dot_general(
                patches[rows, :], weight[c], (((1,), (1,)), ((), ())), preferred_element_type=F32
            ).astype(BF)
            for c in range(3)
        )
        for head in range(heads):
            columns = slice(head * HEAD_DIM, (head + 1) * HEAD_DIM)
            queries[head, rows, :] = query[:, columns]
            keys[head, rows, :] = key[:, columns]
            values[head, rows, :] = jnp.concatenate([value[:, columns], one], axis=1)
        return carry

    lax.fori_loop(0, row_count // block, project, 0)
    scale = HEAD_DIM ** (-0.5) * LOG2E

    def one_block(index, carry):
        rows = pl.ds(pl.multiple_of(index * block, block), block)
        same_image = row_ids[rows, :] == column_ids[...]
        outs = []
        for head in range(heads):
            scores = lax.dot_general(
                queries[head, rows, :],
                keys[head],
                (((1,), (1,)), ((), ())),
                preferred_element_type=F32,
            )
            scores = jnp.where(same_image, scores, -1e30)
            highest = jnp.max(scores, axis=1, keepdims=True)
            weights = jnp.exp2((scores - highest) * scale).astype(BF)
            summed = jnp.dot(weights, values[head], preferred_element_type=F32)
            outs.append(summed[:, :HEAD_DIM] / summed[:, HEAD_DIM : HEAD_DIM + 1])
        context[rows, :] = jnp.concatenate(outs, axis=1).astype(BF)
        return carry

    lax.fori_loop(0, row_count // block, one_block, 0)


def vision_context(patches, weight, patch_ids):
    row_count, depth = patches.shape
    width = weight.shape[1]
    heads = width // HEAD_DIM
    return pl.pallas_call(
        attention_kernel,
        out_shape=jax.ShapeDtypeStruct((row_count, width), BF),
        in_specs=[pl.BlockSpec(memory_space=pltpu.VMEM)] * 4,
        out_specs=pl.BlockSpec(memory_space=pltpu.VMEM),
        scratch_shapes=[
            pltpu.VMEM((heads, row_count, HEAD_DIM), BF),
            pltpu.VMEM((heads, row_count, HEAD_DIM), BF),
            pltpu.VMEM((heads, row_count, 128), BF),
        ],
        compiler_params=pltpu.CompilerParams(vmem_limit_bytes=20 * 2**20),
        cost_estimate=pl.CostEstimate(
            flops=4 * heads * row_count * row_count * 256 + 6 * row_count * depth * width,
            bytes_accessed=2 * (row_count + 3 * width) * depth,
            transcendentals=heads * row_count * row_count,
        ),
        name="vision_attention",
    )(patch_ids[:, None], patch_ids[None, :], patches, weight)


def norm_kernel(*refs):
    parts, outs, (patches, gain, merged, normed) = refs[1:5], refs[5:11], refs[11:]
    outs = [outs[0][...], outs[1][...]] + [
        jnp.concatenate([outs[k][...], outs[k + 1][...]], axis=0) for k in (2, 4)
    ]
    attended = patches[...].astype(F32)
    for part, weight in zip(parts, outs):
        attended += jnp.dot(part[...], weight, preferred_element_type=F32)
    moment = jnp.mean(attended * attended, axis=1, keepdims=True)
    scaled = attended * lax.rsqrt(moment + EPSILON) * gain[...]
    count, width = merged.shape[0], scaled.shape[1]
    for q in range(width // 128):
        normed[q] = scaled[:, q * 128 : (q + 1) * 128]
    for j in range(MERGE):
        for q in range(width // 128):
            piece = normed[q, pl.ds(j, count, stride=MERGE), :].astype(BF)
            columns = slice(j * width + q * 128, j * width + (q + 1) * 128)
            merged[:, columns] = piece


def project_and_norm(tp, parts, outs, patches, gain):
    rows, depth = parts[0].shape
    width = patches.shape[1]
    count = rows // MERGE
    whole = lambda shape: pl.BlockSpec(shape, lambda i, t: (0, 0))
    return pl.pallas_call(
        norm_kernel,
        grid_spec=pltpu.PrefetchScalarGridSpec(
            num_scalar_prefetch=1,
            grid=(1,),
            in_specs=[whole((rows, depth))] * 4
            + [whole(out.shape) for out in outs]
            + [pl.BlockSpec((rows, width), lambda i, t: (t[0], 0)), whole((1, width))],
            out_specs=whole((count, MERGE * width)),
            scratch_shapes=[pltpu.VMEM((width // 128, rows, 128), F32)],
        ),
        out_shape=jax.ShapeDtypeStruct((count, MERGE * width), BF),
        compiler_params=pltpu.CompilerParams(vmem_limit_bytes=18 * 2**20),
        cost_estimate=pl.CostEstimate(
            flops=8 * rows * depth * width,
            bytes_accessed=8 * depth * (rows + width) + 4 * rows * width,
            transcendentals=rows,
        ),
        name="project_and_norm",
    )(tp.reshape(1).astype(jnp.int32), *parts, *outs, patches, gain[None, :])


def stack_kernel(*refs):
    first = 0
    for block in refs[:-1]:
        refs[-1][first : first + block.shape[0], :] = block[...]
        first += block.shape[0]


def stack_rows(blocks):
    count = sum(block.shape[0] for block in blocks)
    depth = blocks[0].shape[1]
    tile = depth // 4
    return pl.pallas_call(
        stack_kernel,
        grid=(depth // tile,),
        out_shape=pltpu.HBM((count, depth), BF),
        in_specs=[pl.BlockSpec((b.shape[0], tile), lambda i: (0, i)) for b in blocks],
        out_specs=pl.BlockSpec((count, tile), lambda i: (0, i)),
        compiler_params=pltpu.CompilerParams(vmem_limit_bytes=10 * 2**20),
        cost_estimate=pl.CostEstimate(
            flops=0, bytes_accessed=4 * count * depth, transcendentals=0
        ),
        name="stack_rows",
    )(*blocks)


def merge_kernel(rows, weight, send, outgoing, rows_held, weight_held, send_held, sent, sems):
    depth = weight_held.shape[0]
    steps = (sems.shape[0] - 1) // 2
    tile = depth // steps
    copies = []
    for k in range(steps):
        part = pl.ds(k * tile, tile)
        copies += [
            pltpu.make_async_copy(rows.at[:, part], rows_held.at[:, part], sems.at[2 * k]),
            pltpu.make_async_copy(weight.at[part], weight_held.at[part], sems.at[2 * k + 1]),
        ]
    copies.append(pltpu.make_async_copy(send, send_held, sems.at[2 * steps]))
    for copy in copies:
        copy.start()
    total = jnp.zeros((rows_held.shape[0], weight_held.shape[1]), F32)
    for k in range(steps):
        copies[2 * k].wait()
        copies[2 * k + 1].wait()
        part = slice(k * tile, (k + 1) * tile)
        total += jnp.dot(
            rows_held[:, part], weight_held[part, :], preferred_element_type=F32
        )
    image = total.astype(BF)
    copies[-1].wait()
    pieces = 4
    count = sent.shape[0] // pieces
    copies = []
    for k in range(pieces):
        part = pl.ds(k * count, count)
        sent[part, :] = jnp.dot(
            send_held[part, :], image, preferred_element_type=F32
        ).astype(BF)
        copy = pltpu.make_async_copy(sent.at[part], outgoing.at[part], sems.at[k])
        copy.start()
        copies.append(copy)
    for copy in copies:
        copy.wait()


def merge_and_select(rows, weight, send):
    slots, count = send.shape
    depth, columns = weight.shape
    hbm = pl.BlockSpec(memory_space=pltpu.HBM)
    return pl.pallas_call(
        merge_kernel,
        out_shape=pltpu.HBM((slots, columns), BF),
        in_specs=[hbm, hbm, hbm],
        out_specs=hbm,
        scratch_shapes=[
            pltpu.VMEM((count, depth), BF),
            pltpu.VMEM((depth, columns), BF),
            pltpu.VMEM((slots, count), BF),
            pltpu.VMEM((slots, columns), BF),
            pltpu.SemaphoreType.DMA((9,)),
        ],
        compiler_params=pltpu.CompilerParams(vmem_limit_bytes=60 * 2**20),
        cost_estimate=pl.CostEstimate(
            flops=2 * count * (depth + slots) * columns,
            bytes_accessed=2 * (count * depth + depth * columns + slots * columns),
            transcendentals=0,
        ),
        name="merge_rows",
    )(rows, weight, send)


def square_sums(block):
    value = block.astype(F32)
    return jnp.sum(value * value, axis=1, keepdims=True)


def diagonal():
    shape = (128, 128)
    return lax.broadcasted_iota(jnp.int32, shape, 0) == lax.broadcasted_iota(jnp.int32, shape, 1)


def to_lanes(column, out):
    eye = diagonal()
    for q in range(out.shape[0]):
        part = jnp.where(eye, column[q * 128 : (q + 1) * 128], 0.0)
        out[q : q + 1, :] = jnp.sum(part, axis=0, keepdims=True)


def to_column(lanes):
    eye = diagonal()
    return jnp.concatenate(
        [
            jnp.sum(jnp.where(eye, lanes[q : q + 1], 0.0), axis=1, keepdims=True)
            for q in range(lanes.shape[0])
        ],
        axis=0,
    )


def text_kernel(text, usable, squares):
    total = jnp.where(usable[...] > 0, 0.0, square_sums(text[...]))
    to_lanes(total, squares.at[pl.ds(pl.program_id(0), 1)])


def text_squares(text, usable):
    count, width = text.shape
    return pl.pallas_call(
        text_kernel,
        grid=(count // 128,),
        out_shape=jax.ShapeDtypeStruct((count // 128, 128), F32),
        in_specs=[
            pl.BlockSpec((128, width), lambda i: (i, 0)),
            pl.BlockSpec((128, 1), lambda i: (i, 0)),
        ],
        out_specs=pl.BlockSpec((count // 128, 128), lambda i: (0, 0)),
        compiler_params=pltpu.CompilerParams(vmem_limit_bytes=10 * 2**20),
        cost_estimate=pl.CostEstimate(
            flops=2 * count * width, bytes_accessed=2 * count * width, transcendentals=0
        ),
        name="text_squares",
    )(text, usable)


def squares_kernel(received, pick, base, squares, total):
    arrived = received[...].reshape(pick.shape[1], received.shape[-1])
    step = pl.program_id(0)

    @pl.when(step == 0)
    def _():
        total[...] = square_sums(arrived)

    @pl.when(step > 0)
    def _():
        total[...] += square_sums(arrived)

    @pl.when(step == pl.num_programs(0) - 1)
    def _():
        rest = jnp.broadcast_to(total[...], (total.shape[0], 128))
        chosen = jnp.zeros((pick.shape[0], 128), F32)
        for _ in range(3):
            part = rest.astype(BF)
            chosen += jnp.dot(pick[...], part, preferred_element_type=F32)
            rest = rest - part.astype(F32)
        to_lanes(chosen[:, :1], squares)
        squares[...] += base[...]


def slot_squares(received, pick, base):
    planes, halves, rows, part = received.shape
    count, slots = pick.shape
    return pl.pallas_call(
        squares_kernel,
        grid=(halves,),
        out_shape=jax.ShapeDtypeStruct((count // 128, 128), F32),
        in_specs=[
            pl.BlockSpec((planes, 1, rows, part), lambda h: (0, h, 0, 0)),
            pl.BlockSpec((count, slots), lambda h: (0, 0), pipeline_mode=pl.Buffered(1)),
            pl.BlockSpec((count // 128, 128), lambda h: (0, 0)),
        ],
        out_specs=pl.BlockSpec((count // 128, 128), lambda h: (0, 0)),
        scratch_shapes=[pltpu.VMEM((slots, 1), F32)],
        compiler_params=pltpu.CompilerParams(vmem_limit_bytes=12 * 2**20),
        cost_estimate=pl.CostEstimate(
            flops=2 * slots * halves * part,
            bytes_accessed=2 * slots * halves * part,
            transcendentals=0,
        ),
        name="slot_squares",
    )(received, pick, base)


def pick_kernel(received, pick, usable, text, prompt):
    arrived = received[...].reshape(pick.shape[1], received.shape[-1])
    picked = jnp.dot(pick[...], arrived, preferred_element_type=F32)
    prompt[...] = jnp.where(usable[...] > 0, picked, text[...].astype(F32)).astype(BF)


def pick_rows(received, pick, usable, text):
    planes, halves, rows, part = received.shape
    count, slots = pick.shape
    return pl.pallas_call(
        pick_kernel,
        grid=(halves,),
        out_shape=jax.ShapeDtypeStruct((count, halves * part), BF),
        in_specs=[
            pl.BlockSpec((planes, 1, rows, part), lambda h: (0, h, 0, 0)),
            pl.BlockSpec((count, slots), lambda h: (0, 0), pipeline_mode=pl.Buffered(1)),
            pl.BlockSpec((count, 1), lambda h: (0, 0), pipeline_mode=pl.Buffered(1)),
            pl.BlockSpec((count, part), lambda h: (0, h)),
        ],
        out_specs=pl.BlockSpec((count, part), lambda h: (0, h)),
        compiler_params=pltpu.CompilerParams(vmem_limit_bytes=14 * 2**20),
        cost_estimate=pl.CostEstimate(
            flops=2 * count * slots * halves * part,
            bytes_accessed=6 * count * halves * part,
            transcendentals=0,
        ),
        name="pick_rows",
    )(received, pick, usable, text)


def finish_kernel(prompt, own, core, far, both, gain, out, inverse, *, width):
    @pl.when(pl.program_id(0) == 0)
    def _():
        total = to_column(own[...] + core[...] + far[...] + both[...])
        inverse[...] = lax.rsqrt(total / width + EPSILON)

    out[...] = (prompt[...].astype(F32) * inverse[...] * gain[...]).astype(BF)


def finish(prompt, squares, gain):
    count, width = prompt.shape
    part = width // 4
    small = pl.BlockSpec((count // 128, 128), lambda h: (0, 0))
    return pl.pallas_call(
        functools.partial(finish_kernel, width=4 * width),
        grid=(4,),
        out_shape=jax.ShapeDtypeStruct((count, width), BF),
        in_specs=[pl.BlockSpec((count, part), lambda h: (0, h))]
        + [small] * 4
        + [pl.BlockSpec((1, part), lambda h: (0, h))],
        out_specs=pl.BlockSpec((count, part), lambda h: (0, h)),
        scratch_shapes=[pltpu.VMEM((count, 1), F32)],
        compiler_params=pltpu.CompilerParams(vmem_limit_bytes=10 * 2**20),
        cost_estimate=pl.CostEstimate(
            flops=3 * count * width, bytes_accessed=4 * count * width, transcendentals=count
        ),
        name="finish",
    )(prompt, *squares, gain[None, :])


def swap_tp(block, k):
    return lax.ppermute(block, TP, [(i, i ^ k) for i in range(4)])


def shift_y(block, d):
    return lax.ppermute(block, ("yh", "yl"), [(i, (i + d) % 4) for i in range(4)])


def swap_core(block):
    return lax.ppermute(block, "c", [(0, 1), (1, 0)])


def on_device(
    patches,
    image_ids,
    qkv_weight,
    out_weight,
    merge_gain,
    merge_weight,
    text_rows,
    image_refs,
    llm_gain,
):
    yh = lax.axis_index("yh")
    tp = lax.axis_index(TP)
    y = lax.axis_index(("yh", "yl"))
    core = lax.axis_index("c")

    half = merge_weight.shape[1] // 2
    own = lax.dynamic_slice_in_dim(merge_weight, yh * half, half, 1)
    other = lax.dynamic_slice_in_dim(merge_weight, (1 - yh) * half, half, 1)
    arrived = lax.ppermute(other, "yh", [(0, 1), (1, 0)])

    prompt_rows = image_refs.shape[0]
    usable = image_refs >= 0
    source = jnp.where(usable, image_refs // 256, -1)
    hits = (source[:, None] == jnp.arange(32)[None, :]).astype(BF)
    before = (jnp.arange(prompt_rows)[:, None] > jnp.arange(prompt_rows)[None, :]).astype(BF)
    earlier = jnp.dot(before, hits, preferred_element_type=F32)
    arrival = jnp.sum(earlier * hits.astype(F32), axis=1).astype(jnp.int32)
    slot = jnp.where(usable, source * 16 + arrival, -1)
    pick = (slot[:, None] == jnp.arange(512)[None, :]).astype(BF)
    names = jnp.where(usable, image_refs % 256 + 1, 0).astype(BF)
    table = jnp.dot(names[None, :], pick, preferred_element_type=F32).astype(jnp.int32)
    table = jnp.broadcast_to(table.reshape(16, 1, 32), (16, 2, 32)).reshape(32, 32)
    usable = usable.astype(jnp.int32)[:, None]

    arrived, table, pick, usable, out_weight = lax.optimization_barrier(
        (arrived, table, pick, usable, out_weight)
    )
    is_own = (jnp.arange(2) == yh)[:, None, None]
    both = jnp.where(is_own, own[None], arrived[None]).reshape(-1, half)
    weight = lax.all_gather(both, ("z", "x"), axis=0, tiled=True)

    middle = out_weight.shape[0] // 2
    out_far = [shift_y(out_weight[:middle], 1), shift_y(out_weight[middle:], -1)]

    patch_ids = jnp.repeat(image_ids.reshape(-1), MERGE)
    patch_ids, patches, both = lax.optimization_barrier((patch_ids, patches, both))
    context = vision_context(patches, jnp.swapaxes(qkv_weight, 1, 2), patch_ids)
    context, *out_far = lax.optimization_barrier((context, *out_far))
    rows = context.shape[0] // 4
    parts = [
        lax.dynamic_slice_in_dim(context, (tp ^ k) * rows, rows, 0) for k in range(4)
    ]
    parts = [parts[0]] + [swap_tp(parts[k], k) for k in (1, 2, 3)]
    out_blocks = [out_weight, swap_core(out_weight)] + out_far + [swap_core(b) for b in out_far]
    merged = project_and_norm(tp, parts, out_blocks, patches, merge_gain)

    table, merged = lax.optimization_barrier((table, merged))
    after, before = shift_y(merged, 1), shift_y(merged, -1)
    count = merged.shape[0] // 2
    far = [shift_y(after[:count], 1), shift_y(before[count:], -1)]
    table = lax.all_to_all(table, SEC, split_axis=0, concat_axis=0, tiled=True)
    after, before, table = lax.optimization_barrier((after, before, table))
    near_rows = [
        (0, 0, merged),
        (1, 0, after),
        (-1, 0, before),
        (2, 0, far[0]),
        (2, count, far[1]),
    ]
    blocks = []
    ids = []
    for d, offset, block in near_rows:
        blocks += [block, swap_core(block)]
        origin = (y - d + 4) % 4 * 128 + offset
        ids += [origin + c * 64 + jnp.arange(block.shape[0]) for c in (core, 1 - core)]
    row_ids = jnp.concatenate(ids)

    wanted = table.reshape(32, 2, 16) - 1
    wanted = jnp.where(wanted >= 0, wanted + jnp.arange(2)[None, :, None] * 256, -1).reshape(-1)
    send = (wanted[:, None] == row_ids[None, :]).astype(BF)

    outgoing = merge_and_select(stack_rows(blocks), weight, send)
    received = lax.all_to_all(outgoing, SEC, split_axis=0, concat_axis=0, tiled=True)
    received = received.reshape(16, 2, 32, half)
    squares = slot_squares(received, pick, text_squares(text_rows, usable))
    squares = [squares] + [swap_tp(squares, k) for k in (1, 2, 3)]
    return finish(pick_rows(received, pick, usable, text_rows), squares, llm_gain)


def solution(mesh):
    torus = Mesh(mesh.devices.reshape(4, 4, 2, 2, 2), ("z", "x", "yh", "yl", "c"))
    return jax.shard_map(
        on_device,
        mesh=torus,
        in_specs=(
            P(SEC, None),
            P(SEC, None),
            P(None, None, TP),
            P(TP, None),
            P(),
            P(SEC, TP),
            P(SEC, TP),
            P(SEC),
            P(TP),
        ),
        out_specs=P(SEC, TP),
        check_vma=False,
    )
```

```python
import functools

import jax
import jax.numpy as jnp
from jax import lax
from jax.experimental import pallas as pl
from jax.experimental.pallas import tpu as pltpu
from jax.sharding import Mesh, PartitionSpec as P

HEAD_DIM = 80
MERGE = 4
EPSILON = 1e-06
LOG2E = 1.4426950408889634
SEC = ("z", "x", "yh")
TP = ("yl", "c")
BF = jnp.bfloat16
F32 = jnp.float32


def attention_kernel(row_ids, column_ids, patches, weight, context, queries, keys, values):
    heads = keys.shape[0]
    row_count = patches.shape[0]
    block = min(256, row_count)
    one = jnp.ones((block, 128 - HEAD_DIM), BF)

    def project(index, carry):
        rows = pl.ds(pl.multiple_of(index * block, block), block)
        query, key, value = (
            lax.dot_general(
                patches[rows, :], weight[c], (((1,), (1,)), ((), ())), preferred_element_type=F32
            ).astype(BF)
            for c in range(3)
        )
        for head in range(heads):
            columns = slice(head * HEAD_DIM, (head + 1) * HEAD_DIM)
            queries[head, rows, :] = query[:, columns]
            keys[head, rows, :] = key[:, columns]
            values[head, rows, :] = jnp.concatenate([value[:, columns], one], axis=1)
        return carry

    lax.fori_loop(0, row_count // block, project, 0)
    scale = HEAD_DIM ** (-0.5) * LOG2E

    def one_block(index, carry):
        rows = pl.ds(pl.multiple_of(index * block, block), block)
        same_image = row_ids[rows, :] == column_ids[...]
        outs = []
        for head in range(heads):
            scores = lax.dot_general(
                queries[head, rows, :],
                keys[head],
                (((1,), (1,)), ((), ())),
                preferred_element_type=F32,
            )
            scores = jnp.where(same_image, scores, -1e30)
            highest = jnp.max(scores, axis=1, keepdims=True)
            weights = jnp.exp2((scores - highest) * scale).astype(BF)
            summed = jnp.dot(weights, values[head], preferred_element_type=F32)
            outs.append(summed[:, :HEAD_DIM] / summed[:, HEAD_DIM : HEAD_DIM + 1])
        context[rows, :] = jnp.concatenate(outs, axis=1).astype(BF)
        return carry

    lax.fori_loop(0, row_count // block, one_block, 0)


def vision_context(patches, weight, patch_ids):
    row_count, depth = patches.shape
    width = weight.shape[1]
    heads = width // HEAD_DIM
    return pl.pallas_call(
        attention_kernel,
        out_shape=jax.ShapeDtypeStruct((row_count, width), BF),
        in_specs=[pl.BlockSpec(memory_space=pltpu.VMEM)] * 4,
        out_specs=pl.BlockSpec(memory_space=pltpu.VMEM),
        scratch_shapes=[
            pltpu.VMEM((heads, row_count, HEAD_DIM), BF),
            pltpu.VMEM((heads, row_count, HEAD_DIM), BF),
            pltpu.VMEM((heads, row_count, 128), BF),
        ],
        compiler_params=pltpu.CompilerParams(vmem_limit_bytes=20 * 2**20),
        cost_estimate=pl.CostEstimate(
            flops=4 * heads * row_count * row_count * 256 + 6 * row_count * depth * width,
            bytes_accessed=2 * (row_count + 3 * width) * depth,
            transcendentals=heads * row_count * row_count,
        ),
        name="vision_attention",
    )(patch_ids[:, None], patch_ids[None, :], patches, weight)


def norm_kernel(*refs):
    parts, outs, (patches, gain, merged, normed) = refs[1:5], refs[5:11], refs[11:]
    outs = [outs[0][...], outs[1][...]] + [
        jnp.concatenate([outs[k][...], outs[k + 1][...]], axis=0) for k in (2, 4)
    ]
    attended = patches[...].astype(F32)
    for part, weight in zip(parts, outs):
        attended += jnp.dot(part[...], weight, preferred_element_type=F32)
    moment = jnp.mean(attended * attended, axis=1, keepdims=True)
    scaled = attended * lax.rsqrt(moment + EPSILON) * gain[...]
    count, width = merged.shape[0], scaled.shape[1]
    for q in range(width // 128):
        normed[q] = scaled[:, q * 128 : (q + 1) * 128]
    for j in range(MERGE):
        for q in range(width // 128):
            piece = normed[q, pl.ds(j, count, stride=MERGE), :].astype(BF)
            columns = slice(j * width + q * 128, j * width + (q + 1) * 128)
            merged[:, columns] = piece


def project_and_norm(tp, parts, outs, patches, gain):
    rows, depth = parts[0].shape
    width = patches.shape[1]
    count = rows // MERGE
    whole = lambda shape: pl.BlockSpec(shape, lambda i, t: (0, 0))
    return pl.pallas_call(
        norm_kernel,
        grid_spec=pltpu.PrefetchScalarGridSpec(
            num_scalar_prefetch=1,
            grid=(1,),
            in_specs=[whole((rows, depth))] * 4
            + [whole(out.shape) for out in outs]
            + [pl.BlockSpec((rows, width), lambda i, t: (t[0], 0)), whole((1, width))],
            out_specs=whole((count, MERGE * width)),
            scratch_shapes=[pltpu.VMEM((width // 128, rows, 128), F32)],
        ),
        out_shape=jax.ShapeDtypeStruct((count, MERGE * width), BF),
        compiler_params=pltpu.CompilerParams(vmem_limit_bytes=18 * 2**20),
        cost_estimate=pl.CostEstimate(
            flops=8 * rows * depth * width,
            bytes_accessed=8 * depth * (rows + width) + 4 * rows * width,
            transcendentals=rows,
        ),
        name="project_and_norm",
    )(tp.reshape(1).astype(jnp.int32), *parts, *outs, patches, gain[None, :])


def stack_kernel(*refs):
    first = 0
    for block in refs[:-1]:
        refs[-1][first : first + block.shape[0], :] = block[...]
        first += block.shape[0]


def stack_rows(blocks):
    count = sum(block.shape[0] for block in blocks)
    depth = blocks[0].shape[1]
    tile = depth // 4
    return pl.pallas_call(
        stack_kernel,
        grid=(depth // tile,),
        out_shape=pltpu.HBM((count, depth), BF),
        in_specs=[pl.BlockSpec((b.shape[0], tile), lambda i: (0, i)) for b in blocks],
        out_specs=pl.BlockSpec((count, tile), lambda i: (0, i)),
        compiler_params=pltpu.CompilerParams(vmem_limit_bytes=10 * 2**20),
        cost_estimate=pl.CostEstimate(
            flops=0, bytes_accessed=4 * count * depth, transcendentals=0
        ),
        name="stack_rows",
    )(*blocks)


def merge_kernel(rows, weight, send, outgoing, rows_held, weight_held, send_held, sent, sems):
    depth = weight_held.shape[0]
    steps = (sems.shape[0] - 1) // 2
    tile = depth // steps
    copies = []
    for k in range(steps):
        part = pl.ds(k * tile, tile)
        copies += [
            pltpu.make_async_copy(rows.at[:, part], rows_held.at[:, part], sems.at[2 * k]),
            pltpu.make_async_copy(weight.at[part], weight_held.at[part], sems.at[2 * k + 1]),
        ]
    copies.append(pltpu.make_async_copy(send, send_held, sems.at[2 * steps]))
    for copy in copies:
        copy.start()
    total = jnp.zeros((rows_held.shape[0], weight_held.shape[1]), F32)
    for k in range(steps):
        copies[2 * k].wait()
        copies[2 * k + 1].wait()
        part = slice(k * tile, (k + 1) * tile)
        total += jnp.dot(
            rows_held[:, part], weight_held[part, :], preferred_element_type=F32
        )
    image = total.astype(BF)
    copies[-1].wait()
    pieces = 4
    count = sent.shape[0] // pieces
    copies = []
    for k in range(pieces):
        part = pl.ds(k * count, count)
        sent[part, :] = jnp.dot(
            send_held[part, :], image, preferred_element_type=F32
        ).astype(BF)
        copy = pltpu.make_async_copy(sent.at[part], outgoing.at[part], sems.at[k])
        copy.start()
        copies.append(copy)
    for copy in copies:
        copy.wait()


def merge_and_select(rows, weight, send):
    slots, count = send.shape
    depth, columns = weight.shape
    hbm = pl.BlockSpec(memory_space=pltpu.HBM)
    return pl.pallas_call(
        merge_kernel,
        out_shape=pltpu.HBM((slots, columns), BF),
        in_specs=[hbm, hbm, hbm],
        out_specs=hbm,
        scratch_shapes=[
            pltpu.VMEM((count, depth), BF),
            pltpu.VMEM((depth, columns), BF),
            pltpu.VMEM((slots, count), BF),
            pltpu.VMEM((slots, columns), BF),
            pltpu.SemaphoreType.DMA((9,)),
        ],
        compiler_params=pltpu.CompilerParams(vmem_limit_bytes=60 * 2**20),
        cost_estimate=pl.CostEstimate(
            flops=2 * count * (depth + slots) * columns,
            bytes_accessed=2 * (count * depth + depth * columns + slots * columns),
            transcendentals=0,
        ),
        name="merge_rows",
    )(rows, weight, send)


def square_sums(block):
    value = block.astype(F32)
    return jnp.sum(value * value, axis=1, keepdims=True)


def diagonal():
    shape = (128, 128)
    return lax.broadcasted_iota(jnp.int32, shape, 0) == lax.broadcasted_iota(jnp.int32, shape, 1)


def to_lanes(column, out):
    eye = diagonal()
    for q in range(out.shape[0]):
        part = jnp.where(eye, column[q * 128 : (q + 1) * 128], 0.0)
        out[q : q + 1, :] = jnp.sum(part, axis=0, keepdims=True)


def to_column(lanes):
    eye = diagonal()
    return jnp.concatenate(
        [
            jnp.sum(jnp.where(eye, lanes[q : q + 1], 0.0), axis=1, keepdims=True)
            for q in range(lanes.shape[0])
        ],
        axis=0,
    )


def text_kernel(text, usable, squares):
    total = jnp.where(usable[...] > 0, 0.0, square_sums(text[...]))
    to_lanes(total, squares.at[pl.ds(pl.program_id(0), 1)])


def text_squares(text, usable):
    count, width = text.shape
    return pl.pallas_call(
        text_kernel,
        grid=(count // 128,),
        out_shape=jax.ShapeDtypeStruct((count // 128, 128), F32),
        in_specs=[
            pl.BlockSpec((128, width), lambda i: (i, 0)),
            pl.BlockSpec((128, 1), lambda i: (i, 0)),
        ],
        out_specs=pl.BlockSpec((count // 128, 128), lambda i: (0, 0)),
        compiler_params=pltpu.CompilerParams(vmem_limit_bytes=10 * 2**20),
        cost_estimate=pl.CostEstimate(
            flops=2 * count * width, bytes_accessed=2 * count * width, transcendentals=0
        ),
        name="text_squares",
    )(text, usable)


def squares_kernel(received, pick, base, squares, total):
    arrived = received[...].reshape(pick.shape[1], received.shape[-1])
    step = pl.program_id(0)

    @pl.when(step == 0)
    def _():
        total[...] = square_sums(arrived)

    @pl.when(step > 0)
    def _():
        total[...] += square_sums(arrived)

    @pl.when(step == pl.num_programs(0) - 1)
    def _():
        rest = jnp.broadcast_to(total[...], (total.shape[0], 128))
        chosen = jnp.zeros((pick.shape[0], 128), F32)
        for _ in range(3):
            part = rest.astype(BF)
            chosen += jnp.dot(pick[...], part, preferred_element_type=F32)
            rest = rest - part.astype(F32)
        to_lanes(chosen[:, :1], squares)
        squares[...] += base[...]


def slot_squares(received, pick, base):
    planes, halves, rows, part = received.shape
    count, slots = pick.shape
    return pl.pallas_call(
        squares_kernel,
        grid=(halves,),
        out_shape=jax.ShapeDtypeStruct((count // 128, 128), F32),
        in_specs=[
            pl.BlockSpec((planes, 1, rows, part), lambda h: (0, h, 0, 0)),
            pl.BlockSpec((count, slots), lambda h: (0, 0), pipeline_mode=pl.Buffered(1)),
            pl.BlockSpec((count // 128, 128), lambda h: (0, 0)),
        ],
        out_specs=pl.BlockSpec((count // 128, 128), lambda h: (0, 0)),
        scratch_shapes=[pltpu.VMEM((slots, 1), F32)],
        compiler_params=pltpu.CompilerParams(vmem_limit_bytes=12 * 2**20),
        cost_estimate=pl.CostEstimate(
            flops=2 * slots * halves * part,
            bytes_accessed=2 * slots * halves * part,
            transcendentals=0,
        ),
        name="slot_squares",
    )(received, pick, base)


def pick_kernel(received, pick, usable, text, prompt):
    arrived = received[...].reshape(pick.shape[1], received.shape[-1])
    picked = jnp.dot(pick[...], arrived, preferred_element_type=F32)
    prompt[...] = jnp.where(usable[...] > 0, picked, text[...].astype(F32)).astype(BF)


def pick_rows(received, pick, usable, text):
    planes, halves, rows, part = received.shape
    count, slots = pick.shape
    return pl.pallas_call(
        pick_kernel,
        grid=(halves,),
        out_shape=jax.ShapeDtypeStruct((count, halves * part), BF),
        in_specs=[
            pl.BlockSpec((planes, 1, rows, part), lambda h: (0, h, 0, 0)),
            pl.BlockSpec((count, slots), lambda h: (0, 0), pipeline_mode=pl.Buffered(1)),
            pl.BlockSpec((count, 1), lambda h: (0, 0), pipeline_mode=pl.Buffered(1)),
            pl.BlockSpec((count, part), lambda h: (0, h)),
        ],
        out_specs=pl.BlockSpec((count, part), lambda h: (0, h)),
        compiler_params=pltpu.CompilerParams(vmem_limit_bytes=14 * 2**20),
        cost_estimate=pl.CostEstimate(
            flops=2 * count * slots * halves * part,
            bytes_accessed=6 * count * halves * part,
            transcendentals=0,
        ),
        name="pick_rows",
    )(received, pick, usable, text)


def finish_kernel(prompt, own, core, far, both, gain, out, inverse, *, width):
    @pl.when(pl.program_id(0) == 0)
    def _():
        total = to_column(own[...] + core[...] + far[...] + both[...])
        inverse[...] = lax.rsqrt(total / width + EPSILON)

    out[...] = (prompt[...].astype(F32) * inverse[...] * gain[...]).astype(BF)


def finish(prompt, squares, gain):
    count, width = prompt.shape
    part = width // 4
    small = pl.BlockSpec((count // 128, 128), lambda h: (0, 0))
    return pl.pallas_call(
        functools.partial(finish_kernel, width=4 * width),
        grid=(4,),
        out_shape=jax.ShapeDtypeStruct((count, width), BF),
        in_specs=[pl.BlockSpec((count, part), lambda h: (0, h))]
        + [small] * 4
        + [pl.BlockSpec((1, part), lambda h: (0, h))],
        out_specs=pl.BlockSpec((count, part), lambda h: (0, h)),
        scratch_shapes=[pltpu.VMEM((count, 1), F32)],
        compiler_params=pltpu.CompilerParams(vmem_limit_bytes=10 * 2**20),
        cost_estimate=pl.CostEstimate(
            flops=3 * count * width, bytes_accessed=4 * count * width, transcendentals=count
        ),
        name="finish",
    )(prompt, *squares, gain[None, :])


def swap_tp(block, k):
    return lax.ppermute(block, TP, [(i, i ^ k) for i in range(4)])


def shift_y(block, d):
    return lax.ppermute(block, ("yh", "yl"), [(i, (i + d) % 4) for i in range(4)])


def swap_core(block):
    return lax.ppermute(block, "c", [(0, 1), (1, 0)])


def on_device(
    patches,
    image_ids,
    qkv_weight,
    out_weight,
    merge_gain,
    merge_weight,
    text_rows,
    image_refs,
    llm_gain,
):
    yh = lax.axis_index("yh")
    tp = lax.axis_index(TP)
    y = lax.axis_index(("yh", "yl"))
    core = lax.axis_index("c")

    half = merge_weight.shape[1] // 2
    other = lax.dynamic_slice_in_dim(merge_weight, (1 - yh) * half, half, 1)
    arrived = lax.ppermute(other, "yh", [(0, 1), (1, 0)])

    prompt_rows = image_refs.shape[0]
    usable = image_refs >= 0
    source = jnp.where(usable, image_refs // 256, -1)
    hits = (source[:, None] == jnp.arange(32)[None, :]).astype(BF)
    before = (jnp.arange(prompt_rows)[:, None] > jnp.arange(prompt_rows)[None, :]).astype(BF)
    earlier = jnp.dot(before, hits, preferred_element_type=F32)
    arrival = jnp.sum(earlier * hits.astype(F32), axis=1).astype(jnp.int32)
    slot = jnp.where(usable, source * 16 + arrival, -1)
    pick = (slot[:, None] == jnp.arange(512)[None, :]).astype(BF)
    names = jnp.where(usable, image_refs % 256 + 1, 0).astype(BF)
    table = jnp.dot(names[None, :], pick, preferred_element_type=F32).astype(jnp.int32)
    usable = usable.astype(jnp.int32)[:, None]

    arrived, table, pick, usable, out_weight, merge_weight = lax.optimization_barrier(
        (arrived, table, pick, usable, out_weight, merge_weight)
    )
    own = lax.dynamic_slice_in_dim(merge_weight, yh * half, half, 1)
    is_own = (jnp.arange(2) == yh)[:, None, None]
    both = jnp.where(is_own, own[None], arrived[None]).reshape(-1, half)
    weight = lax.all_gather(both, ("z", "x"), axis=0, tiled=True)

    middle = out_weight.shape[0] // 2
    out_far = [shift_y(out_weight[:middle], 1), shift_y(out_weight[middle:], -1)]

    patch_ids = jnp.repeat(image_ids.reshape(-1), MERGE)
    patch_ids, patches, both = lax.optimization_barrier((patch_ids, patches, both))
    context = vision_context(patches, jnp.swapaxes(qkv_weight, 1, 2), patch_ids)
    context, *out_far = lax.optimization_barrier((context, *out_far))
    rows = context.shape[0] // 4
    parts = [
        lax.dynamic_slice_in_dim(context, (tp ^ k) * rows, rows, 0) for k in range(4)
    ]
    parts = [parts[0]] + [swap_tp(parts[k], k) for k in (1, 2, 3)]
    out_blocks = [out_weight, swap_core(out_weight)] + out_far + [swap_core(b) for b in out_far]
    merged = project_and_norm(tp, parts, out_blocks, patches, merge_gain)

    table, merged = lax.optimization_barrier((table, merged))
    table = jnp.broadcast_to(table.reshape(16, 1, 32), (16, 2, 32)).reshape(32, 32)
    after, before = shift_y(merged, 1), shift_y(merged, -1)
    count = merged.shape[0] // 2
    far = [shift_y(after[:count], 1), shift_y(before[count:], -1)]
    table = lax.all_to_all(table, SEC, split_axis=0, concat_axis=0, tiled=True)
    after, before, table = lax.optimization_barrier((after, before, table))
    near_rows = [
        (0, 0, merged),
        (1, 0, after),
        (-1, 0, before),
        (2, 0, far[0]),
        (2, count, far[1]),
    ]
    blocks = []
    ids = []
    for d, offset, block in near_rows:
        blocks += [block, swap_core(block)]
        origin = (y - d + 4) % 4 * 128 + offset
        ids += [origin + c * 64 + jnp.arange(block.shape[0]) for c in (core, 1 - core)]
    row_ids = jnp.concatenate(ids)

    wanted = table.reshape(32, 2, 16) - 1
    wanted = jnp.where(wanted >= 0, wanted + jnp.arange(2)[None, :, None] * 256, -1).reshape(-1)
    send = (wanted[:, None] == row_ids[None, :]).astype(BF)

    from_text = text_squares(text_rows, usable)
    from_text, send = lax.optimization_barrier((from_text, send))
    outgoing = merge_and_select(stack_rows(blocks), weight, send)
    received = lax.all_to_all(outgoing, SEC, split_axis=0, concat_axis=0, tiled=True)
    received = received.reshape(16, 2, 32, half)
    squares = slot_squares(received, pick, from_text)
    squares = [squares] + [swap_tp(squares, k) for k in (1, 2, 3)]
    return finish(pick_rows(received, pick, usable, text_rows), squares, llm_gain)


def solution(mesh):
    torus = Mesh(mesh.devices.reshape(4, 4, 2, 2, 2), ("z", "x", "yh", "yl", "c"))
    return jax.shard_map(
        on_device,
        mesh=torus,
        in_specs=(
            P(SEC, None),
            P(SEC, None),
            P(None, None, TP),
            P(TP, None),
            P(),
            P(SEC, TP),
            P(SEC, TP),
            P(SEC),
            P(TP),
        ),
        out_specs=P(SEC, TP),
        check_vma=False,
    )
```

```python
import functools

import jax
import jax.numpy as jnp
from jax import lax
from jax.experimental import pallas as pl
from jax.experimental.pallas import tpu as pltpu
from jax.sharding import Mesh, PartitionSpec as P

HEAD_DIM = 80
MERGE = 4
EPSILON = 1e-06
LOG2E = 1.4426950408889634
SEC = ("z", "x", "yh")
TP = ("yl", "c")
BF = jnp.bfloat16
F32 = jnp.float32


def attention_kernel(row_ids, column_ids, patches, weight, context, queries, keys, values):
    heads = keys.shape[0]
    row_count = patches.shape[0]
    block = min(256, row_count)
    one = jnp.ones((block, 128 - HEAD_DIM), BF)

    def project(index, carry):
        rows = pl.ds(pl.multiple_of(index * block, block), block)
        query, key, value = (
            lax.dot_general(
                patches[rows, :], weight[c], (((1,), (1,)), ((), ())), preferred_element_type=F32
            ).astype(BF)
            for c in range(3)
        )
        for head in range(heads):
            columns = slice(head * HEAD_DIM, (head + 1) * HEAD_DIM)
            queries[head, rows, :] = query[:, columns]
            keys[head, rows, :] = key[:, columns]
            values[head, rows, :] = jnp.concatenate([value[:, columns], one], axis=1)
        return carry

    lax.fori_loop(0, row_count // block, project, 0)
    scale = HEAD_DIM ** (-0.5) * LOG2E

    def one_block(index, carry):
        rows = pl.ds(pl.multiple_of(index * block, block), block)
        same_image = row_ids[rows, :] == column_ids[...]
        outs = []
        for head in range(heads):
            scores = lax.dot_general(
                queries[head, rows, :],
                keys[head],
                (((1,), (1,)), ((), ())),
                preferred_element_type=F32,
            )
            scores = jnp.where(same_image, scores, -1e30)
            highest = jnp.max(scores, axis=1, keepdims=True)
            weights = jnp.exp2((scores - highest) * scale).astype(BF)
            summed = jnp.dot(weights, values[head], preferred_element_type=F32)
            outs.append(summed[:, :HEAD_DIM] / summed[:, HEAD_DIM : HEAD_DIM + 1])
        context[rows, :] = jnp.concatenate(outs, axis=1).astype(BF)
        return carry

    lax.fori_loop(0, row_count // block, one_block, 0)


def vision_context(patches, weight, patch_ids):
    row_count, depth = patches.shape
    width = weight.shape[1]
    heads = width // HEAD_DIM
    return pl.pallas_call(
        attention_kernel,
        out_shape=jax.ShapeDtypeStruct((row_count, width), BF),
        in_specs=[pl.BlockSpec(memory_space=pltpu.VMEM)] * 4,
        out_specs=pl.BlockSpec(memory_space=pltpu.VMEM),
        scratch_shapes=[
            pltpu.VMEM((heads, row_count, HEAD_DIM), BF),
            pltpu.VMEM((heads, row_count, HEAD_DIM), BF),
            pltpu.VMEM((heads, row_count, 128), BF),
        ],
        compiler_params=pltpu.CompilerParams(vmem_limit_bytes=20 * 2**20),
        cost_estimate=pl.CostEstimate(
            flops=4 * heads * row_count * row_count * 256 + 6 * row_count * depth * width,
            bytes_accessed=2 * (row_count + 3 * width) * depth,
            transcendentals=heads * row_count * row_count,
        ),
        name="vision_attention",
    )(patch_ids[:, None], patch_ids[None, :], patches, weight)


def norm_kernel(*refs):
    parts, outs, (patches, gain, merged, normed) = refs[1:5], refs[5:11], refs[11:]
    outs = [outs[0][...], outs[1][...]] + [
        jnp.concatenate([outs[k][...], outs[k + 1][...]], axis=0) for k in (2, 4)
    ]
    attended = patches[...].astype(F32)
    for part, weight in zip(parts, outs):
        attended += jnp.dot(part[...], weight, preferred_element_type=F32)
    moment = jnp.mean(attended * attended, axis=1, keepdims=True)
    scaled = attended * lax.rsqrt(moment + EPSILON) * gain[...]
    count, width = merged.shape[0], scaled.shape[1]
    for q in range(width // 128):
        normed[q] = scaled[:, q * 128 : (q + 1) * 128]
    for j in range(MERGE):
        for q in range(width // 128):
            piece = normed[q, pl.ds(j, count, stride=MERGE), :].astype(BF)
            columns = slice(j * width + q * 128, j * width + (q + 1) * 128)
            merged[:, columns] = piece


def project_and_norm(tp, parts, outs, patches, gain):
    rows, depth = parts[0].shape
    width = patches.shape[1]
    count = rows // MERGE
    whole = lambda shape: pl.BlockSpec(shape, lambda i, t: (0, 0))
    return pl.pallas_call(
        norm_kernel,
        grid_spec=pltpu.PrefetchScalarGridSpec(
            num_scalar_prefetch=1,
            grid=(1,),
            in_specs=[whole((rows, depth))] * 4
            + [whole(out.shape) for out in outs]
            + [pl.BlockSpec((rows, width), lambda i, t: (t[0], 0)), whole((1, width))],
            out_specs=whole((count, MERGE * width)),
            scratch_shapes=[pltpu.VMEM((width // 128, rows, 128), F32)],
        ),
        out_shape=jax.ShapeDtypeStruct((count, MERGE * width), BF),
        compiler_params=pltpu.CompilerParams(vmem_limit_bytes=18 * 2**20),
        cost_estimate=pl.CostEstimate(
            flops=8 * rows * depth * width,
            bytes_accessed=8 * depth * (rows + width) + 4 * rows * width,
            transcendentals=rows,
        ),
        name="project_and_norm",
    )(tp.reshape(1).astype(jnp.int32), *parts, *outs, patches, gain[None, :])


def stack_kernel(*refs):
    first = 0
    for block in refs[:-1]:
        refs[-1][first : first + block.shape[0], :] = block[...]
        first += block.shape[0]


def stack_rows(blocks):
    count = sum(block.shape[0] for block in blocks)
    depth = blocks[0].shape[1]
    tile = depth // 4
    return pl.pallas_call(
        stack_kernel,
        grid=(depth // tile,),
        out_shape=pltpu.HBM((count, depth), BF),
        in_specs=[pl.BlockSpec((b.shape[0], tile), lambda i: (0, i)) for b in blocks],
        out_specs=pl.BlockSpec((count, tile), lambda i: (0, i)),
        compiler_params=pltpu.CompilerParams(vmem_limit_bytes=10 * 2**20),
        cost_estimate=pl.CostEstimate(
            flops=0, bytes_accessed=4 * count * depth, transcendentals=0
        ),
        name="stack_rows",
    )(*blocks)


def merge_kernel(rows, weight, send, outgoing, rows_held, weight_held, send_held, sent, sems):
    depth, columns = weight_held.shape
    half = columns // 2
    left, right = pl.ds(0, half), pl.ds(half, half)
    edges = [depth * k // 40 for k in (0, 5, 15, 27, 40)]
    steps = len(edges) - 1
    copies = []
    for k in range(steps):
        part = pl.ds(edges[k], edges[k + 1] - edges[k])
        copies += [
            pltpu.make_async_copy(rows.at[:, part], rows_held.at[:, part], sems.at[2 * k]),
            pltpu.make_async_copy(
                weight.at[part, left], weight_held.at[part, left], sems.at[2 * k + 1]
            ),
        ]
    copies += [
        pltpu.make_async_copy(send, send_held, sems.at[2 * steps]),
        pltpu.make_async_copy(
            weight.at[:, right], weight_held.at[:, right], sems.at[2 * steps + 1]
        ),
    ]
    for copy in copies:
        copy.start()
    total = jnp.zeros((rows_held.shape[0], half), F32)
    for k in range(steps):
        copies[2 * k].wait()
        copies[2 * k + 1].wait()
        part = slice(edges[k], edges[k + 1])
        total += jnp.dot(
            rows_held[:, part], weight_held[part, :half], preferred_element_type=F32
        )
    copies[2 * steps].wait()
    sent[:, :half] = jnp.dot(
        send_held[...], total.astype(BF), preferred_element_type=F32
    ).astype(BF)
    first = pltpu.make_async_copy(sent.at[:, left], outgoing.at[:, left], sems.at[0])
    first.start()
    copies[2 * steps + 1].wait()
    image = jnp.dot(
        rows_held[...], weight_held[:, half:], preferred_element_type=F32
    ).astype(BF)
    pieces = 2
    count = sent.shape[0] // pieces
    writes = [first]
    for k in range(pieces):
        part = pl.ds(k * count, count)
        sent[part, half:] = jnp.dot(
            send_held[part, :], image, preferred_element_type=F32
        ).astype(BF)
        copy = pltpu.make_async_copy(
            sent.at[part, right], outgoing.at[part, right], sems.at[k + 1]
        )
        copy.start()
        writes.append(copy)
    for copy in writes:
        copy.wait()


def merge_and_select(rows, weight, send):
    slots, count = send.shape
    depth, columns = weight.shape
    hbm = pl.BlockSpec(memory_space=pltpu.HBM)
    return pl.pallas_call(
        merge_kernel,
        out_shape=pltpu.HBM((slots, columns), BF),
        in_specs=[hbm, hbm, hbm],
        out_specs=hbm,
        scratch_shapes=[
            pltpu.VMEM((count, depth), BF),
            pltpu.VMEM((depth, columns), BF),
            pltpu.VMEM((slots, count), BF),
            pltpu.VMEM((slots, columns), BF),
            pltpu.SemaphoreType.DMA((10,)),
        ],
        compiler_params=pltpu.CompilerParams(vmem_limit_bytes=60 * 2**20),
        cost_estimate=pl.CostEstimate(
            flops=2 * count * (depth + slots) * columns,
            bytes_accessed=2 * (count * depth + depth * columns + slots * columns),
            transcendentals=0,
        ),
        name="merge_rows",
    )(rows, weight, send)


def square_sums(block):
    value = block.astype(F32)
    return jnp.sum(value * value, axis=1, keepdims=True)


def diagonal():
    shape = (128, 128)
    return lax.broadcasted_iota(jnp.int32, shape, 0) == lax.broadcasted_iota(jnp.int32, shape, 1)


def to_lanes(column, out):
    eye = diagonal()
    for q in range(out.shape[0]):
        part = jnp.where(eye, column[q * 128 : (q + 1) * 128], 0.0)
        out[q : q + 1, :] = jnp.sum(part, axis=0, keepdims=True)


def to_column(lanes):
    eye = diagonal()
    return jnp.concatenate(
        [
            jnp.sum(jnp.where(eye, lanes[q : q + 1], 0.0), axis=1, keepdims=True)
            for q in range(lanes.shape[0])
        ],
        axis=0,
    )


def text_kernel(text, usable, squares):
    total = jnp.where(usable[...] > 0, 0.0, square_sums(text[...]))
    to_lanes(total, squares.at[pl.ds(pl.program_id(0), 1)])


def text_squares(text, usable):
    count, width = text.shape
    return pl.pallas_call(
        text_kernel,
        grid=(count // 128,),
        out_shape=jax.ShapeDtypeStruct((count // 128, 128), F32),
        in_specs=[
            pl.BlockSpec((128, width), lambda i: (i, 0)),
            pl.BlockSpec((128, 1), lambda i: (i, 0)),
        ],
        out_specs=pl.BlockSpec((count // 128, 128), lambda i: (0, 0)),
        compiler_params=pltpu.CompilerParams(vmem_limit_bytes=10 * 2**20),
        cost_estimate=pl.CostEstimate(
            flops=2 * count * width, bytes_accessed=2 * count * width, transcendentals=0
        ),
        name="text_squares",
    )(text, usable)


def squares_kernel(received, pick, base, squares, total):
    arrived = received[...].reshape(pick.shape[1], received.shape[-1])
    step = pl.program_id(0)

    @pl.when(step == 0)
    def _():
        total[...] = square_sums(arrived)

    @pl.when(step > 0)
    def _():
        total[...] += square_sums(arrived)

    @pl.when(step == pl.num_programs(0) - 1)
    def _():
        rest = jnp.broadcast_to(total[...], (total.shape[0], 128))
        chosen = jnp.zeros((pick.shape[0], 128), F32)
        for _ in range(3):
            part = rest.astype(BF)
            chosen += jnp.dot(pick[...], part, preferred_element_type=F32)
            rest = rest - part.astype(F32)
        to_lanes(chosen[:, :1], squares)
        squares[...] += base[...]


def slot_squares(received, pick, base):
    planes, halves, rows, part = received.shape
    count, slots = pick.shape
    return pl.pallas_call(
        squares_kernel,
        grid=(halves,),
        out_shape=jax.ShapeDtypeStruct((count // 128, 128), F32),
        in_specs=[
            pl.BlockSpec((planes, 1, rows, part), lambda h: (0, h, 0, 0)),
            pl.BlockSpec((count, slots), lambda h: (0, 0), pipeline_mode=pl.Buffered(1)),
            pl.BlockSpec((count // 128, 128), lambda h: (0, 0)),
        ],
        out_specs=pl.BlockSpec((count // 128, 128), lambda h: (0, 0)),
        scratch_shapes=[pltpu.VMEM((slots, 1), F32)],
        compiler_params=pltpu.CompilerParams(vmem_limit_bytes=12 * 2**20),
        cost_estimate=pl.CostEstimate(
            flops=2 * slots * halves * part,
            bytes_accessed=2 * slots * halves * part,
            transcendentals=0,
        ),
        name="slot_squares",
    )(received, pick, base)


def pick_kernel(received, pick, usable, text, prompt):
    arrived = received[...].reshape(pick.shape[1], received.shape[-1])
    picked = jnp.dot(pick[...], arrived, preferred_element_type=F32)
    prompt[...] = jnp.where(usable[...] > 0, picked, text[...].astype(F32)).astype(BF)


def pick_rows(received, pick, usable, text):
    planes, halves, rows, part = received.shape
    count, slots = pick.shape
    return pl.pallas_call(
        pick_kernel,
        grid=(halves,),
        out_shape=jax.ShapeDtypeStruct((count, halves * part), BF),
        in_specs=[
            pl.BlockSpec((planes, 1, rows, part), lambda h: (0, h, 0, 0)),
            pl.BlockSpec((count, slots), lambda h: (0, 0), pipeline_mode=pl.Buffered(1)),
            pl.BlockSpec((count, 1), lambda h: (0, 0), pipeline_mode=pl.Buffered(1)),
            pl.BlockSpec((count, part), lambda h: (0, h)),
        ],
        out_specs=pl.BlockSpec((count, part), lambda h: (0, h)),
        compiler_params=pltpu.CompilerParams(vmem_limit_bytes=14 * 2**20),
        cost_estimate=pl.CostEstimate(
            flops=2 * count * slots * halves * part,
            bytes_accessed=6 * count * halves * part,
            transcendentals=0,
        ),
        name="pick_rows",
    )(received, pick, usable, text)


def finish_kernel(prompt, own, core, far, both, gain, out, inverse, *, width):
    @pl.when(pl.program_id(0) == 0)
    def _():
        total = to_column(own[...] + core[...] + far[...] + both[...])
        inverse[...] = lax.rsqrt(total / width + EPSILON)

    out[...] = (prompt[...].astype(F32) * inverse[...] * gain[...]).astype(BF)


def finish(prompt, squares, gain):
    count, width = prompt.shape
    part = width // 4
    small = pl.BlockSpec((count // 128, 128), lambda h: (0, 0))
    return pl.pallas_call(
        functools.partial(finish_kernel, width=4 * width),
        grid=(4,),
        out_shape=jax.ShapeDtypeStruct((count, width), BF),
        in_specs=[pl.BlockSpec((count, part), lambda h: (0, h))]
        + [small] * 4
        + [pl.BlockSpec((1, part), lambda h: (0, h))],
        out_specs=pl.BlockSpec((count, part), lambda h: (0, h)),
        scratch_shapes=[pltpu.VMEM((count, 1), F32)],
        compiler_params=pltpu.CompilerParams(vmem_limit_bytes=10 * 2**20),
        cost_estimate=pl.CostEstimate(
            flops=3 * count * width, bytes_accessed=4 * count * width, transcendentals=count
        ),
        name="finish",
    )(prompt, *squares, gain[None, :])


def swap_tp(block, k):
    return lax.ppermute(block, TP, [(i, i ^ k) for i in range(4)])


def shift_y(block, d):
    return lax.ppermute(block, ("yh", "yl"), [(i, (i + d) % 4) for i in range(4)])


def swap_core(block):
    return lax.ppermute(block, "c", [(0, 1), (1, 0)])


def on_device(
    patches,
    image_ids,
    qkv_weight,
    out_weight,
    merge_gain,
    merge_weight,
    text_rows,
    image_refs,
    llm_gain,
):
    yh = lax.axis_index("yh")
    tp = lax.axis_index(TP)
    y = lax.axis_index(("yh", "yl"))
    core = lax.axis_index("c")

    half = merge_weight.shape[1] // 2
    other = lax.dynamic_slice_in_dim(merge_weight, (1 - yh) * half, half, 1)
    arrived = lax.ppermute(other, "yh", [(0, 1), (1, 0)])

    prompt_rows = image_refs.shape[0]
    usable = image_refs >= 0
    source = jnp.where(usable, image_refs // 256, -1)
    hits = (source[:, None] == jnp.arange(32)[None, :]).astype(BF)
    before = (jnp.arange(prompt_rows)[:, None] > jnp.arange(prompt_rows)[None, :]).astype(BF)
    earlier = jnp.dot(before, hits, preferred_element_type=F32)
    arrival = jnp.sum(earlier * hits.astype(F32), axis=1).astype(jnp.int32)
    slot = jnp.where(usable, source * 16 + arrival, -1)
    pick = (slot[:, None] == jnp.arange(512)[None, :]).astype(BF)
    names = jnp.where(usable, image_refs % 256 + 1, 0).astype(BF)
    table = jnp.dot(names[None, :], pick, preferred_element_type=F32).astype(jnp.int32)
    usable = usable.astype(jnp.int32)[:, None]

    arrived, table, pick, usable, out_weight, merge_weight = lax.optimization_barrier(
        (arrived, table, pick, usable, out_weight, merge_weight)
    )
    own = lax.dynamic_slice_in_dim(merge_weight, yh * half, half, 1)
    is_own = (jnp.arange(2) == yh)[:, None, None]
    both = jnp.where(is_own, own[None], arrived[None]).reshape(-1, half)
    weight = lax.all_gather(both, ("z", "x"), axis=0, tiled=True)

    middle = out_weight.shape[0] // 2
    out_far = [shift_y(out_weight[:middle], 1), shift_y(out_weight[middle:], -1)]

    patch_ids = jnp.repeat(image_ids.reshape(-1), MERGE)
    patch_ids, patches, both = lax.optimization_barrier((patch_ids, patches, both))
    context = vision_context(patches, jnp.swapaxes(qkv_weight, 1, 2), patch_ids)
    context, *out_far = lax.optimization_barrier((context, *out_far))
    rows = context.shape[0] // 4
    parts = [
        lax.dynamic_slice_in_dim(context, (tp ^ k) * rows, rows, 0) for k in range(4)
    ]
    parts = [parts[0]] + [swap_tp(parts[k], k) for k in (1, 2, 3)]
    out_blocks = [out_weight, swap_core(out_weight)] + out_far + [swap_core(b) for b in out_far]
    merged = project_and_norm(tp, parts, out_blocks, patches, merge_gain)

    table, merged = lax.optimization_barrier((table, merged))
    table = jnp.broadcast_to(table.reshape(16, 1, 32), (16, 2, 32)).reshape(32, 32)
    after, before = shift_y(merged, 1), shift_y(merged, -1)
    count = merged.shape[0] // 2
    far = [shift_y(after[:count], 1), shift_y(before[count:], -1)]
    table = lax.all_to_all(table, SEC, split_axis=0, concat_axis=0, tiled=True)
    after, before, table = lax.optimization_barrier((after, before, table))
    near_rows = [
        (0, 0, merged),
        (1, 0, after),
        (-1, 0, before),
        (2, 0, far[0]),
        (2, count, far[1]),
    ]
    blocks = []
    ids = []
    for d, offset, block in near_rows:
        blocks += [block, swap_core(block)]
        origin = (y - d + 4) % 4 * 128 + offset
        ids += [origin + c * 64 + jnp.arange(block.shape[0]) for c in (core, 1 - core)]
    row_ids = jnp.concatenate(ids)

    wanted = table.reshape(32, 2, 16) - 1
    wanted = jnp.where(wanted >= 0, wanted + jnp.arange(2)[None, :, None] * 256, -1).reshape(-1)
    send = (wanted[:, None] == row_ids[None, :]).astype(BF)

    from_text = text_squares(text_rows, usable)
    from_text, send = lax.optimization_barrier((from_text, send))
    outgoing = merge_and_select(stack_rows(blocks), weight, send)
    received = lax.all_to_all(outgoing, SEC, split_axis=0, concat_axis=0, tiled=True)
    received = received.reshape(16, 2, 32, half)
    squares = slot_squares(received, pick, from_text)
    squares = [squares] + [swap_tp(squares, k) for k in (1, 2, 3)]
    return finish(pick_rows(received, pick, usable, text_rows), squares, llm_gain)


def solution(mesh):
    torus = Mesh(mesh.devices.reshape(4, 4, 2, 2, 2), ("z", "x", "yh", "yl", "c"))
    return jax.shard_map(
        on_device,
        mesh=torus,
        in_specs=(
            P(SEC, None),
            P(SEC, None),
            P(None, None, TP),
            P(TP, None),
            P(),
            P(SEC, TP),
            P(SEC, TP),
            P(SEC),
            P(TP),
        ),
        out_specs=P(SEC, TP),
        check_vma=False,
    )
```

```python
import functools

import jax
import jax.numpy as jnp
from jax import lax
from jax.experimental import pallas as pl
from jax.experimental.pallas import tpu as pltpu
from jax.sharding import Mesh, PartitionSpec as P

HEAD_DIM = 80
MERGE = 4
EPSILON = 1e-06
LOG2E = 1.4426950408889634
SEC = ("z", "x", "yh")
TP = ("yl", "c")
BF = jnp.bfloat16
F32 = jnp.float32


def attention_kernel(row_ids, column_ids, patches, weight, context, queries, keys, values):
    heads = keys.shape[0]
    row_count = patches.shape[0]
    block = min(256, row_count)
    one = jnp.ones((block, 128 - HEAD_DIM), BF)

    def project(index, carry):
        rows = pl.ds(pl.multiple_of(index * block, block), block)
        query, key, value = (
            lax.dot_general(
                patches[rows, :], weight[c], (((1,), (1,)), ((), ())), preferred_element_type=F32
            ).astype(BF)
            for c in range(3)
        )
        for head in range(heads):
            columns = slice(head * HEAD_DIM, (head + 1) * HEAD_DIM)
            queries[head, rows, :] = query[:, columns]
            keys[head, rows, :] = key[:, columns]
            values[head, rows, :] = jnp.concatenate([value[:, columns], one], axis=1)
        return carry

    lax.fori_loop(0, row_count // block, project, 0)
    scale = HEAD_DIM ** (-0.5) * LOG2E

    def one_block(index, carry):
        rows = pl.ds(pl.multiple_of(index * block, block), block)
        same_image = row_ids[rows, :] == column_ids[...]
        outs = []
        for head in range(heads):
            scores = lax.dot_general(
                queries[head, rows, :],
                keys[head],
                (((1,), (1,)), ((), ())),
                preferred_element_type=F32,
            )
            scores = jnp.where(same_image, scores, -1e30)
            highest = jnp.max(scores, axis=1, keepdims=True)
            weights = jnp.exp2((scores - highest) * scale).astype(BF)
            summed = jnp.dot(weights, values[head], preferred_element_type=F32)
            outs.append(summed[:, :HEAD_DIM] / summed[:, HEAD_DIM : HEAD_DIM + 1])
        context[rows, :] = jnp.concatenate(outs, axis=1).astype(BF)
        return carry

    lax.fori_loop(0, row_count // block, one_block, 0)


def vision_context(patches, weight, patch_ids):
    row_count, depth = patches.shape
    width = weight.shape[1]
    heads = width // HEAD_DIM
    return pl.pallas_call(
        attention_kernel,
        out_shape=jax.ShapeDtypeStruct((row_count, width), BF),
        in_specs=[pl.BlockSpec(memory_space=pltpu.VMEM)] * 4,
        out_specs=pl.BlockSpec(memory_space=pltpu.VMEM),
        scratch_shapes=[
            pltpu.VMEM((heads, row_count, HEAD_DIM), BF),
            pltpu.VMEM((heads, row_count, HEAD_DIM), BF),
            pltpu.VMEM((heads, row_count, 128), BF),
        ],
        compiler_params=pltpu.CompilerParams(vmem_limit_bytes=20 * 2**20),
        cost_estimate=pl.CostEstimate(
            flops=4 * heads * row_count * row_count * 256 + 6 * row_count * depth * width,
            bytes_accessed=2 * (row_count + 3 * width) * depth,
            transcendentals=heads * row_count * row_count,
        ),
        name="vision_attention",
    )(patch_ids[:, None], patch_ids[None, :], patches, weight)


def norm_kernel(*refs):
    parts, outs, (patches, gain, merged, normed) = refs[1:5], refs[5:11], refs[11:]
    outs = [outs[0][...], outs[1][...]] + [
        jnp.concatenate([outs[k][...], outs[k + 1][...]], axis=0) for k in (2, 4)
    ]
    attended = patches[...].astype(F32)
    for part, weight in zip(parts, outs):
        attended += jnp.dot(part[...], weight, preferred_element_type=F32)
    moment = jnp.mean(attended * attended, axis=1, keepdims=True)
    scaled = attended * lax.rsqrt(moment + EPSILON) * gain[...]
    count, width = merged.shape[0], scaled.shape[1]
    for q in range(width // 128):
        normed[q] = scaled[:, q * 128 : (q + 1) * 128]
    for j in range(MERGE):
        for q in range(width // 128):
            piece = normed[q, pl.ds(j, count, stride=MERGE), :].astype(BF)
            columns = slice(j * width + q * 128, j * width + (q + 1) * 128)
            merged[:, columns] = piece


def project_and_norm(tp, parts, outs, patches, gain):
    rows, depth = parts[0].shape
    width = patches.shape[1]
    count = rows // MERGE
    whole = lambda shape: pl.BlockSpec(shape, lambda i, t: (0, 0))
    return pl.pallas_call(
        norm_kernel,
        grid_spec=pltpu.PrefetchScalarGridSpec(
            num_scalar_prefetch=1,
            grid=(1,),
            in_specs=[whole((rows, depth))] * 4
            + [whole(out.shape) for out in outs]
            + [pl.BlockSpec((rows, width), lambda i, t: (t[0], 0)), whole((1, width))],
            out_specs=whole((count, MERGE * width)),
            scratch_shapes=[pltpu.VMEM((width // 128, rows, 128), F32)],
        ),
        out_shape=jax.ShapeDtypeStruct((count, MERGE * width), BF),
        compiler_params=pltpu.CompilerParams(vmem_limit_bytes=18 * 2**20),
        cost_estimate=pl.CostEstimate(
            flops=8 * rows * depth * width,
            bytes_accessed=8 * depth * (rows + width) + 4 * rows * width,
            transcendentals=rows,
        ),
        name="project_and_norm",
    )(tp.reshape(1).astype(jnp.int32), *parts, *outs, patches, gain[None, :])


def stack_kernel(*refs):
    first = 0
    for block in refs[:-1]:
        refs[-1][first : first + block.shape[0], :] = block[...]
        first += block.shape[0]


def stack_rows(blocks):
    count = sum(block.shape[0] for block in blocks)
    depth = blocks[0].shape[1]
    tile = depth // 4
    return pl.pallas_call(
        stack_kernel,
        grid=(depth // tile,),
        out_shape=pltpu.HBM((count, depth), BF),
        in_specs=[pl.BlockSpec((b.shape[0], tile), lambda i: (0, i)) for b in blocks],
        out_specs=pl.BlockSpec((count, tile), lambda i: (0, i)),
        compiler_params=pltpu.CompilerParams(vmem_limit_bytes=10 * 2**20),
        cost_estimate=pl.CostEstimate(
            flops=0, bytes_accessed=4 * count * depth, transcendentals=0
        ),
        name="stack_rows",
    )(*blocks)


def merge_kernel(rows, weight, send, outgoing, rows_held, weight_held, send_held, sent, sems):
    depth, columns = weight_held.shape
    half = columns // 2
    left, right = pl.ds(0, half), pl.ds(half, half)
    edges = [depth * k // 40 for k in (0, 3, 10, 22, 40)]
    steps = len(edges) - 1
    copies = []
    for k in range(steps):
        part = pl.ds(edges[k], edges[k + 1] - edges[k])
        copies += [
            pltpu.make_async_copy(rows.at[:, part], rows_held.at[:, part], sems.at[2 * k]),
            pltpu.make_async_copy(
                weight.at[part, left], weight_held.at[part, left], sems.at[2 * k + 1]
            ),
        ]
    copies += [
        pltpu.make_async_copy(send, send_held, sems.at[2 * steps]),
        pltpu.make_async_copy(
            weight.at[:, right], weight_held.at[:, right], sems.at[2 * steps + 1]
        ),
    ]
    for copy in copies:
        copy.start()
    total = jnp.zeros((rows_held.shape[0], half), F32)
    for k in range(steps):
        copies[2 * k].wait()
        copies[2 * k + 1].wait()
        part = slice(edges[k], edges[k + 1])
        total += jnp.dot(
            rows_held[:, part], weight_held[part, :half], preferred_element_type=F32
        )
    copies[2 * steps].wait()
    sent[:, :half] = jnp.dot(
        send_held[...], total.astype(BF), preferred_element_type=F32
    ).astype(BF)
    first = pltpu.make_async_copy(sent.at[:, left], outgoing.at[:, left], sems.at[0])
    first.start()
    copies[2 * steps + 1].wait()
    image = jnp.dot(
        rows_held[...], weight_held[:, half:], preferred_element_type=F32
    ).astype(BF)
    pieces = 2
    count = sent.shape[0] // pieces
    writes = [first]
    for k in range(pieces):
        part = pl.ds(k * count, count)
        sent[part, half:] = jnp.dot(
            send_held[part, :], image, preferred_element_type=F32
        ).astype(BF)
        copy = pltpu.make_async_copy(
            sent.at[part, right], outgoing.at[part, right], sems.at[k + 1]
        )
        copy.start()
        writes.append(copy)
    for copy in writes:
        copy.wait()


def merge_and_select(rows, weight, send):
    slots, count = send.shape
    depth, columns = weight.shape
    hbm = pl.BlockSpec(memory_space=pltpu.HBM)
    return pl.pallas_call(
        merge_kernel,
        out_shape=pltpu.HBM((slots, columns), BF),
        in_specs=[hbm, hbm, hbm],
        out_specs=hbm,
        scratch_shapes=[
            pltpu.VMEM((count, depth), BF),
            pltpu.VMEM((depth, columns), BF),
            pltpu.VMEM((slots, count), BF),
            pltpu.VMEM((slots, columns), BF),
            pltpu.SemaphoreType.DMA((10,)),
        ],
        compiler_params=pltpu.CompilerParams(vmem_limit_bytes=60 * 2**20),
        cost_estimate=pl.CostEstimate(
            flops=2 * count * (depth + slots) * columns,
            bytes_accessed=2 * (count * depth + depth * columns + slots * columns),
            transcendentals=0,
        ),
        name="merge_rows",
    )(rows, weight, send)


def square_sums(block):
    value = block.astype(F32)
    return jnp.sum(value * value, axis=1, keepdims=True)


def diagonal():
    shape = (128, 128)
    return lax.broadcasted_iota(jnp.int32, shape, 0) == lax.broadcasted_iota(jnp.int32, shape, 1)


def to_lanes(column, out):
    eye = diagonal()
    for q in range(out.shape[0]):
        part = jnp.where(eye, column[q * 128 : (q + 1) * 128], 0.0)
        out[q : q + 1, :] = jnp.sum(part, axis=0, keepdims=True)


def to_column(lanes):
    eye = diagonal()
    return jnp.concatenate(
        [
            jnp.sum(jnp.where(eye, lanes[q : q + 1], 0.0), axis=1, keepdims=True)
            for q in range(lanes.shape[0])
        ],
        axis=0,
    )


def text_kernel(text, usable, squares):
    total = jnp.where(usable[...] > 0, 0.0, square_sums(text[...]))
    to_lanes(total, squares.at[pl.ds(pl.program_id(0), 1)])


def text_squares(text, usable):
    count, width = text.shape
    return pl.pallas_call(
        text_kernel,
        grid=(count // 128,),
        out_shape=jax.ShapeDtypeStruct((count // 128, 128), F32),
        in_specs=[
            pl.BlockSpec((128, width), lambda i: (i, 0)),
            pl.BlockSpec((128, 1), lambda i: (i, 0)),
        ],
        out_specs=pl.BlockSpec((count // 128, 128), lambda i: (0, 0)),
        compiler_params=pltpu.CompilerParams(vmem_limit_bytes=10 * 2**20),
        cost_estimate=pl.CostEstimate(
            flops=2 * count * width, bytes_accessed=2 * count * width, transcendentals=0
        ),
        name="text_squares",
    )(text, usable)


def squares_kernel(received, pick, base, squares, total):
    arrived = received[...].reshape(pick.shape[1], received.shape[-1])
    step = pl.program_id(0)

    @pl.when(step == 0)
    def _():
        total[...] = square_sums(arrived)

    @pl.when(step > 0)
    def _():
        total[...] += square_sums(arrived)

    @pl.when(step == pl.num_programs(0) - 1)
    def _():
        rest = jnp.broadcast_to(total[...], (total.shape[0], 128))
        chosen = jnp.zeros((pick.shape[0], 128), F32)
        for _ in range(3):
            part = rest.astype(BF)
            chosen += jnp.dot(pick[...], part, preferred_element_type=F32)
            rest = rest - part.astype(F32)
        to_lanes(chosen[:, :1], squares)
        squares[...] += base[...]


def slot_squares(received, pick, base):
    planes, halves, rows, part = received.shape
    count, slots = pick.shape
    return pl.pallas_call(
        squares_kernel,
        grid=(halves,),
        out_shape=jax.ShapeDtypeStruct((count // 128, 128), F32),
        in_specs=[
            pl.BlockSpec((planes, 1, rows, part), lambda h: (0, h, 0, 0)),
            pl.BlockSpec((count, slots), lambda h: (0, 0), pipeline_mode=pl.Buffered(1)),
            pl.BlockSpec((count // 128, 128), lambda h: (0, 0)),
        ],
        out_specs=pl.BlockSpec((count // 128, 128), lambda h: (0, 0)),
        scratch_shapes=[pltpu.VMEM((slots, 1), F32)],
        compiler_params=pltpu.CompilerParams(vmem_limit_bytes=12 * 2**20),
        cost_estimate=pl.CostEstimate(
            flops=2 * slots * halves * part,
            bytes_accessed=2 * slots * halves * part,
            transcendentals=0,
        ),
        name="slot_squares",
    )(received, pick, base)


def pick_kernel(received, pick, usable, text, prompt):
    arrived = received[...].reshape(pick.shape[1], received.shape[-1])
    picked = jnp.dot(pick[...], arrived, preferred_element_type=F32)
    prompt[...] = jnp.where(usable[...] > 0, picked, text[...].astype(F32)).astype(BF)


def pick_rows(received, pick, usable, text):
    planes, halves, rows, part = received.shape
    count, slots = pick.shape
    return pl.pallas_call(
        pick_kernel,
        grid=(halves,),
        out_shape=jax.ShapeDtypeStruct((count, halves * part), BF),
        in_specs=[
            pl.BlockSpec((planes, 1, rows, part), lambda h: (0, h, 0, 0)),
            pl.BlockSpec((count, slots), lambda h: (0, 0), pipeline_mode=pl.Buffered(1)),
            pl.BlockSpec((count, 1), lambda h: (0, 0), pipeline_mode=pl.Buffered(1)),
            pl.BlockSpec((count, part), lambda h: (0, h)),
        ],
        out_specs=pl.BlockSpec((count, part), lambda h: (0, h)),
        compiler_params=pltpu.CompilerParams(vmem_limit_bytes=14 * 2**20),
        cost_estimate=pl.CostEstimate(
            flops=2 * count * slots * halves * part,
            bytes_accessed=6 * count * halves * part,
            transcendentals=0,
        ),
        name="pick_rows",
    )(received, pick, usable, text)


def finish_kernel(prompt, own, core, far, both, gain, out, inverse, *, width):
    @pl.when(pl.program_id(0) == 0)
    def _():
        total = to_column(own[...] + core[...] + far[...] + both[...])
        inverse[...] = lax.rsqrt(total / width + EPSILON)

    out[...] = (prompt[...].astype(F32) * inverse[...] * gain[...]).astype(BF)


def finish(prompt, squares, gain):
    count, width = prompt.shape
    part = width // 4
    small = pl.BlockSpec((count // 128, 128), lambda h: (0, 0))
    return pl.pallas_call(
        functools.partial(finish_kernel, width=4 * width),
        grid=(4,),
        out_shape=jax.ShapeDtypeStruct((count, width), BF),
        in_specs=[pl.BlockSpec((count, part), lambda h: (0, h))]
        + [small] * 4
        + [pl.BlockSpec((1, part), lambda h: (0, h))],
        out_specs=pl.BlockSpec((count, part), lambda h: (0, h)),
        scratch_shapes=[pltpu.VMEM((count, 1), F32)],
        compiler_params=pltpu.CompilerParams(vmem_limit_bytes=10 * 2**20),
        cost_estimate=pl.CostEstimate(
            flops=3 * count * width, bytes_accessed=4 * count * width, transcendentals=count
        ),
        name="finish",
    )(prompt, *squares, gain[None, :])


def swap_tp(block, k):
    return lax.ppermute(block, TP, [(i, i ^ k) for i in range(4)])


def shift_y(block, d):
    return lax.ppermute(block, ("yh", "yl"), [(i, (i + d) % 4) for i in range(4)])


def swap_core(block):
    return lax.ppermute(block, "c", [(0, 1), (1, 0)])


def on_device(
    patches,
    image_ids,
    qkv_weight,
    out_weight,
    merge_gain,
    merge_weight,
    text_rows,
    image_refs,
    llm_gain,
):
    yh = lax.axis_index("yh")
    tp = lax.axis_index(TP)
    y = lax.axis_index(("yh", "yl"))
    core = lax.axis_index("c")

    half = merge_weight.shape[1] // 2
    other = lax.dynamic_slice_in_dim(merge_weight, (1 - yh) * half, half, 1)
    arrived = lax.ppermute(other, "yh", [(0, 1), (1, 0)])

    prompt_rows = image_refs.shape[0]
    usable = image_refs >= 0
    source = jnp.where(usable, image_refs // 256, -1)
    hits = (source[:, None] == jnp.arange(32)[None, :]).astype(BF)
    before = (jnp.arange(prompt_rows)[:, None] > jnp.arange(prompt_rows)[None, :]).astype(BF)
    earlier = jnp.dot(before, hits, preferred_element_type=F32)
    arrival = jnp.sum(earlier * hits.astype(F32), axis=1).astype(jnp.int32)
    slot = jnp.where(usable, source * 16 + arrival, -1)
    pick = (slot[:, None] == jnp.arange(512)[None, :]).astype(BF)
    names = jnp.where(usable, image_refs % 256 + 1, 0).astype(BF)
    table = jnp.dot(names[None, :], pick, preferred_element_type=F32).astype(jnp.int32)
    usable = usable.astype(jnp.int32)[:, None]

    arrived, table, pick, usable, out_weight, merge_weight = lax.optimization_barrier(
        (arrived, table, pick, usable, out_weight, merge_weight)
    )
    own = lax.dynamic_slice_in_dim(merge_weight, yh * half, half, 1)
    is_own = (jnp.arange(2) == yh)[:, None, None]
    both = jnp.where(is_own, own[None], arrived[None]).reshape(-1, half)
    weight = lax.all_gather(both, ("z", "x"), axis=0, tiled=True)

    middle = out_weight.shape[0] // 2
    out_far = [shift_y(out_weight[:middle], 1), shift_y(out_weight[middle:], -1)]

    patch_ids = jnp.repeat(image_ids.reshape(-1), MERGE)
    patch_ids, patches, both = lax.optimization_barrier((patch_ids, patches, both))
    context = vision_context(patches, jnp.swapaxes(qkv_weight, 1, 2), patch_ids)
    context, *out_far = lax.optimization_barrier((context, *out_far))
    rows = context.shape[0] // 4
    parts = [
        lax.dynamic_slice_in_dim(context, (tp ^ k) * rows, rows, 0) for k in range(4)
    ]
    parts = [parts[0]] + [swap_tp(parts[k], k) for k in (1, 2, 3)]
    out_blocks = [out_weight, swap_core(out_weight)] + out_far + [swap_core(b) for b in out_far]
    merged = project_and_norm(tp, parts, out_blocks, patches, merge_gain)

    table, merged = lax.optimization_barrier((table, merged))
    table = jnp.broadcast_to(table.reshape(16, 1, 32), (16, 2, 32)).reshape(32, 32)
    after, before = shift_y(merged, 1), shift_y(merged, -1)
    count = merged.shape[0] // 2
    far = [shift_y(after[:count], 1), shift_y(before[count:], -1)]
    table = lax.all_to_all(table, SEC, split_axis=0, concat_axis=0, tiled=True)
    after, before, table = lax.optimization_barrier((after, before, table))
    near_rows = [
        (0, 0, merged),
        (1, 0, after),
        (-1, 0, before),
        (2, 0, far[0]),
        (2, count, far[1]),
    ]
    blocks = []
    ids = []
    for d, offset, block in near_rows:
        blocks += [block, swap_core(block)]
        origin = (y - d + 4) % 4 * 128 + offset
        ids += [origin + c * 64 + jnp.arange(block.shape[0]) for c in (core, 1 - core)]
    row_ids = jnp.concatenate(ids)

    wanted = table.reshape(32, 2, 16) - 1
    wanted = jnp.where(wanted >= 0, wanted + jnp.arange(2)[None, :, None] * 256, -1).reshape(-1)
    send = (wanted[:, None] == row_ids[None, :]).astype(BF)

    from_text = text_squares(text_rows, usable)
    from_text, send = lax.optimization_barrier((from_text, send))
    outgoing = merge_and_select(stack_rows(blocks), weight, send)
    received = lax.all_to_all(outgoing, SEC, split_axis=0, concat_axis=0, tiled=True)
    received = received.reshape(16, 2, 32, half)
    squares = slot_squares(received, pick, from_text)
    squares = [squares] + [swap_tp(squares, k) for k in (1, 2, 3)]
    return finish(pick_rows(received, pick, usable, text_rows), squares, llm_gain)


def solution(mesh):
    torus = Mesh(mesh.devices.reshape(4, 4, 2, 2, 2), ("z", "x", "yh", "yl", "c"))
    return jax.shard_map(
        on_device,
        mesh=torus,
        in_specs=(
            P(SEC, None),
            P(SEC, None),
            P(None, None, TP),
            P(TP, None),
            P(),
            P(SEC, TP),
            P(SEC, TP),
            P(SEC),
            P(TP),
        ),
        out_specs=P(SEC, TP),
        check_vma=False,
    )
```
